32 devices in a mesh: regions: 16 (over z, y, x), shard: 2 (over core).
Axes of the slice: x: 2, y: 2, z: 4, core: 2. Of those that a mesh axis runs over, the one named last changes fastest.
Arguments:
- layer_in: bfloat16 [2, 9216, 768], P('shard', 'regions'), may hold values from -6 to 6
- out_grad: bfloat16 [2, 9216, 768], P('shard', 'regions'), may hold values from -6 to 6
- w_qkv: bfloat16 [768, 2304], P(('regions', 'shard')), may hold values from -0.21875 to 0.21875
- w_out: bfloat16 [768, 768], P(('regions', 'shard')), may hold values from -0.875 to 0.875
- w_up: bfloat16 [768, 3072], P(('regions', 'shard')), may hold values from -0.21875 to 0.21875
- w_down: bfloat16 [3072, 768], P(('regions', 'shard')), may hold values from -0.109375 to 0.109375
- vectors: bfloat16 [12, 768], P(None, ('regions', 'shard')), may hold values from 0.5 to 1.5
- relative: float32 [12, 253], replicated, may hold values from -3 to 3
- first_qkv: float32 [768, 2304], P(('regions', 'shard')), may hold values from -6 to 6
- second_qkv: float32 [768, 2304], P(('regions', 'shard')), may hold values from 0.5 to 50
- first_out: float32 [768, 768], P(('regions', 'shard')), may hold values from -6 to 6
- second_out: float32 [768, 768], P(('regions', 'shard')), may hold values from 0.05 to 5
- first_up: float32 [768, 3072], P(('regions', 'shard')), may hold values from -6 to 6
- second_up: float32 [768, 3072], P(('regions', 'shard')), may hold values from 0.5 to 50
- first_down: float32 [3072, 768], P(('regions', 'shard')), may hold values from -6 to 6
- second_down: float32 [3072, 768], P(('regions', 'shard')), may hold values from 0.5 to 50
- first_vectors: float32 [12, 768], P(None, ('regions', 'shard')), may hold values from -6 to 6
- second_vectors: float32 [12, 768], P(None, ('regions', 'shard')), may hold values from 0.5 to 50
- first_relative: float32 [12, 253], replicated, may hold values from -6 to 6
- second_relative: float32 [12, 253], replicated, may hold values from 0.05 to 5
- token_slot: int32 [2, 9216], P('shard', 'regions'), may hold values from 0 to 1151, as said below
- home_index: int32 [2, 9216], P('shard', 'regions'), may hold values from 0 to 1151, as said below
- box_x: int32 [2, 9216], P('shard', 'regions'), may hold values from 0 to 31
- box_y: int32 [2, 9216], P('shard', 'regions'), may hold values from 0 to 31
Outputs:
- layer_out: bfloat16 [2, 9216, 768], P('shard', 'regions')
- in_grad: float32 [2, 9216, 768], P('shard', 'regions')
- grad_qkv: float32 [768, 2304], P(('regions', 'shard'))
- firsts_qkv: float32 [768, 2304], P(('regions', 'shard'))
- seconds_qkv: float32 [768, 2304], P(('regions', 'shard'))
- update_qkv: float32 [768, 2304], P(('regions', 'shard'))
- grad_out: float32 [768, 768], P(('regions', 'shard'))
- firsts_out: float32 [768, 768], P(('regions', 'shard'))
- seconds_out: float32 [768, 768], P(('regions', 'shard'))
- update_out: float32 [768, 768], P(('regions', 'shard'))
- grad_up: float32 [768, 3072], P(('regions', 'shard'))
- firsts_up: float32 [768, 3072], P(('regions', 'shard'))
- seconds_up: float32 [768, 3072], P(('regions', 'shard'))
- update_up: float32 [768, 3072], P(('regions', 'shard'))
- grad_down: float32 [3072, 768], P(('regions', 'shard'))
- firsts_down: float32 [3072, 768], P(('regions', 'shard'))
- seconds_down: float32 [3072, 768], P(('regions', 'shard'))
- update_down: float32 [3072, 768], P(('regions', 'shard'))
- grad_vectors: float32 [12, 768], P(None, ('regions', 'shard'))
- firsts_vectors: float32 [12, 768], P(None, ('regions', 'shard'))
- seconds_vectors: float32 [12, 768], P(None, ('regions', 'shard'))
- update_vectors: float32 [12, 768], P(None, ('regions', 'shard'))
- grad_relative: float32 [12, 253], replicated
- firsts_relative: float32 [12, 253], replicated
- seconds_relative: float32 [12, 253], replicated
- update_relative: float32 [12, 253], replicated
The draws below stay inside these ranges and needn't reach their ends.
Inputs may be any that keep to these rules, and one draw needn't show every extreme that they name: `token_slot`: in each replica, one device's entries are distinct; entry h * 72 + c means the c-th row that the device sends to device h, and the rows sent to h use slots 0 upward without gaps. Each device sends exactly 576 rows in all, at most 72 to one device, and exactly 72 to some device. `home_index`: in each replica, one device's entries are distinct and name exactly the rows sent to it: s * 72 + c is the c-th row from device s. Each device receives exactly 576 rows, at most 72 from one device, and exactly 72 from some device.
All inputs are finite; a program needn't handle non-finite values.
Results may differ from the reference program's by a relative error of at most 0.014.
The reference program's roundings to bfloat16 on the way count: a program that leaves them out, or rounds other values in their place, can miss the bound.
Values may be sent and summed in bfloat16 or wider, within the bound.
A program may use at most 192 MiB of HBM per device.

```python
import math
import jax
import jax.numpy as jnp
import numpy as np
from jax import lax

D = 768
FF = 3072
HEADS = 12
HEAD = 64
PAGE = 576
RELS = 253
TOK_DEV = 576
CAP = 72
TOKENS = 9216
N_REGIONS = 16
N_SHARD = 2


def replica_tables(key):
    groups = N_REGIONS
    per_dev = TOK_DEV
    slot_cap = CAP
    streams = jax.random.split(key, 5)
    halves = jax.random.randint(streams[0], (groups // 2,), 0, slot_cap + 1).astype(jnp.int32)
    halves = halves.at[0].set(0)
    loads = jnp.stack([halves, slot_cap - halves], axis=1).reshape(groups)
    loads = loads[jax.random.permutation(streams[1], groups)]
    ranks = jax.random.permutation(streams[2], groups)
    counts = loads[(ranks[None, :] - ranks[:, None]) % groups].astype(jnp.int32)
    places = jnp.arange(per_dev, dtype=jnp.int32)
    send_end = jnp.cumsum(counts, axis=1).astype(jnp.int32)
    send_start = send_end - counts
    target = jnp.sum((send_end[:, None, :] <= places[None, :, None]).astype(jnp.int32), axis=2).astype(jnp.int32)
    first_at = jnp.take_along_axis(send_start, target, axis=1)
    slot_of = target * slot_cap + (places[None, :] - first_at)
    mixing = jax.vmap(lambda sub: jax.random.permutation(sub, per_dev))(jax.random.split(streams[3], groups))
    token_slot = jnp.take_along_axis(slot_of, mixing, axis=1)
    recv_end = jnp.cumsum(counts, axis=0).astype(jnp.int32).T
    recv_start = recv_end - counts.T
    sender = jnp.sum((recv_end[:, None, :] <= places[None, :, None]).astype(jnp.int32), axis=2).astype(jnp.int32)
    start_at = jnp.take_along_axis(recv_start, sender, axis=1)
    arrival = sender * slot_cap + (places[None, :] - start_at)
    shuffle = jax.vmap(lambda sub: jax.random.permutation(sub, per_dev))(jax.random.split(streams[4], groups))
    home_index = jnp.take_along_axis(arrival, shuffle, axis=1)
    return (token_slot.reshape(-1).astype(jnp.int32), home_index.reshape(-1).astype(jnp.int32))


def all_tables(key):
    slot_list = []
    home_list = []
    for replica in range(N_SHARD):
        slot_table, home_table = replica_tables(jax.random.fold_in(key, 7001 + replica))
        slot_list.append(slot_table)
        home_list.append(home_table)
    return (jnp.stack(slot_list), jnp.stack(home_list))


def draw_token_slot(key, part):
    return all_tables(key)[0]


def draw_home_index(key, part):
    return all_tables(key)[1]


def with_ends(drawn, rng, low, top_value):
    extent = drawn.shape
    place = [jax.random.randint(jax.random.fold_in(rng, axis), (), 0, extent[axis]) for axis in range(len(extent))]
    drawn = drawn.at[tuple(place)].set(low)
    longest = extent.index(max(extent))
    place[longest] = (place[longest] + 1) % extent[longest]
    return drawn.at[tuple(place)].set(top_value)


def steps_of(own_key, extent, pieces, least, largest):
    def one(axis_at, shards_of):
        steps = jax.random.uniform(jax.random.fold_in(jax.random.fold_in(own_key, 6), axis_at), (shards_of,), jnp.float32, least / len(pieces), largest / len(pieces))
        return jnp.repeat(jnp.exp(steps), extent[axis_at] // shards_of).reshape((-1,) + (1,) * (len(extent) - axis_at - 1))

    factor_of = one(*pieces[0])
    for cut in pieces[1:]:
        factor_of = factor_of * one(*cut)
    return factor_of


def bell_draw(stream_key, shape, deviation, limit, pieces=(), kind=jnp.bfloat16):
    loudness = steps_of(stream_key, shape, pieces, -0.22, 0.18) if pieces else 1.0
    values = jax.random.normal(stream_key, shape, jnp.float32) * deviation * loudness
    return jnp.minimum(jnp.maximum(values, -limit), limit).astype(kind)


def setup_inputs(seed: int = 0) -> dict:
    splits = jax.random.split(jax.random.key(seed), 25)
    layer_in = bell_draw(splits[0], (N_SHARD, TOKENS, D), 1.0, 6.0, ((0, 2), (1, 16)))
    out_grad = bell_draw(splits[1], (N_SHARD, TOKENS, D), 1.0, 6.0, ((0, 2), (1, 16)))
    w_qkv = bell_draw(splits[2], (D, 3 * D), D ** -0.5, 0.21875, ((0, 32),))
    w_out = bell_draw(splits[3], (D, D), (D // 16) ** -0.5, 0.875, ((0, 32),))
    w_up = bell_draw(splits[4], (D, FF), D ** -0.5, 0.21875, ((0, 32),))
    w_down = bell_draw(splits[5], (FF, D), FF ** -0.5, 0.109375, ((0, 32),))
    vectors = jnp.clip(0.5 + 1.0 * jax.random.uniform(splits[6], (12, D), jnp.float32) ** steps_of(splits[6], (12, D), ((1, 32),), -0.2, 0.2), 0.5, 1.5).astype(jnp.bfloat16)
    relative = bell_draw(splits[7], (HEADS, RELS), 0.5, 3.0, (), jnp.float32)
    first_qkv = bell_draw(splits[8], (D, 3 * D), 1.0, 6.0, ((0, 32),), jnp.float32)
    second_qkv = jnp.clip(jnp.exp(math.log(50.0) - 4.6051702 * jax.random.uniform(splits[9], (D, 3 * D), jnp.float32) ** steps_of(splits[9], (D, 3 * D), ((0, 32),), -0.2, 0.2)), 0.5, 50.0)
    first_out = bell_draw(splits[10], (D, D), 1.0, 6.0, ((0, 32),), jnp.float32)
    second_out = jnp.clip(jnp.exp(math.log(5.0) - 4.6051702 * jax.random.uniform(splits[11], (D, D), jnp.float32) ** steps_of(splits[11], (D, D), ((0, 32),), -0.2, 0.2)), 0.05, 5.0)
    first_up = bell_draw(splits[12], (D, FF), 1.0, 6.0, ((0, 32),), jnp.float32)
    second_up = jnp.clip(jnp.exp(math.log(50.0) - 4.6051702 * jax.random.uniform(splits[13], (D, FF), jnp.float32) ** steps_of(splits[13], (D, FF), ((0, 32),), -0.2, 0.2)), 0.5, 50.0)
    first_down = bell_draw(splits[14], (FF, D), 1.0, 6.0, ((0, 32),), jnp.float32)
    second_down = jnp.clip(jnp.exp(math.log(50.0) - 4.6051702 * jax.random.uniform(splits[15], (FF, D), jnp.float32) ** steps_of(splits[15], (FF, D), ((0, 32),), -0.2, 0.2)), 0.5, 50.0)
    first_vectors = bell_draw(splits[16], (12, D), 1.0, 6.0, ((1, 32),), jnp.float32)
    second_vectors = jnp.clip(jnp.exp(math.log(50.0) - 4.6051702 * jax.random.uniform(splits[17], (12, D), jnp.float32) ** steps_of(splits[17], (12, D), ((1, 32),), -0.2, 0.2)), 0.5, 50.0)
    first_relative = bell_draw(splits[18], (HEADS, RELS), 1.0, 6.0, (), jnp.float32)
    second_relative = jnp.clip(jnp.exp(jax.random.uniform(splits[19], (HEADS, RELS), jnp.float32, math.log(0.05), math.log(5.0))), 0.05, 5.0)
    token_slot = draw_token_slot(jax.random.fold_in(splits[24], 71), 0)
    home_index = draw_home_index(jax.random.fold_in(splits[24], 71), 0)
    box_x = with_ends(jax.random.randint(splits[22], (N_SHARD, TOKENS), 0, 32), jax.random.fold_in(splits[22], 1), 0, 31).astype(jnp.int32)
    box_y = with_ends(jax.random.randint(splits[23], (N_SHARD, TOKENS), 0, 32), jax.random.fold_in(splits[23], 1), 0, 31).astype(jnp.int32)
    return dict(layer_in=layer_in, out_grad=out_grad, w_qkv=w_qkv, w_out=w_out, w_up=w_up, w_down=w_down, vectors=vectors, relative=relative, first_qkv=first_qkv, second_qkv=second_qkv, first_out=first_out, second_out=second_out, first_up=first_up, second_up=second_up, first_down=first_down, second_down=second_down, first_vectors=first_vectors, second_vectors=second_vectors, first_relative=first_relative, second_relative=second_relative, token_slot=token_slot, home_index=home_index, box_x=box_x, box_y=box_y)


PRECISE = lax.Precision.HIGHEST
EPS_NORM = 1e-05
BETA_ONE = 0.9
BETA_TWO = 0.999
ADAM_EPS = 1e-08
LAYER_FACTOR = 0.5625
DECAY_RATE = 0.05
STEP_COUNT = 10.0

@jax.custom_vjp
def low(v):
    return lax.optimization_barrier(v.astype(jnp.bfloat16)).astype(jnp.float32)

@jax.custom_vjp
def low_back(v):
    return v

def low_keep(v):
    return (low(v), None)

def low_pass(kept, grad):
    return (grad,)

def back_keep(v):
    return (v, None)

def back_low(kept, grad):
    return (low(grad),)
low.defvjp(low_keep, low_pass)
low_back.defvjp(back_keep, back_low)

def table_index():
    first_ax = np.arange(128)[:, None]
    second_ax = np.arange(128)[None, :]
    offset = second_ax - first_ax
    result = np.full((128, 128), -1)
    result = np.where((first_ax < 64) & (second_ax < 64), offset + 63, result)
    inside_x = (first_ax >= 64) & (first_ax < 96) & (second_ax >= 64) & (second_ax < 96)
    result = np.where(inside_x, offset + 158, result)
    result = np.where((first_ax >= 96) & (second_ax >= 96), offset + 221, result)
    return result

def bias_table(relative):
    indices = table_index()
    picked = relative[:, np.maximum(indices, 0)]
    return jnp.where(jnp.asarray(indices >= 0)[None], picked, jnp.zeros_like(picked))

def position_codes(box_x, box_y):
    places = jnp.arange(PAGE, dtype=jnp.int32)
    seq_bucket = places * 64 // PAGE
    columns = jnp.arange(128, dtype=jnp.int32)
    matched = (columns[None, None, :] == seq_bucket[None, :, None]) | (columns == 64 + box_x[..., None]) | (columns == 96 + box_y[..., None])
    return matched.astype(jnp.float32)

def page_attend(page_qkv, code_rows, bias_mats):
    parted = page_qkv.reshape(PAGE, 3, HEADS, HEAD)
    queries = parted[:, 0]
    key_rows = parted[:, 1]
    values = parted[:, 2]
    lifted = jnp.einsum('pa,hab->hpb', code_rows, bias_mats, precision=PRECISE)
    layout_bias = jnp.einsum('hpb,qb->hpq', lifted, code_rows, precision=PRECISE)
    scores = jnp.einsum('phd,qhd->hpq', queries, key_rows, precision=PRECISE) * 0.125 + layout_bias
    scores = low_back(scores)
    row_max = lax.optimization_barrier(jnp.max(scores, axis=2, keepdims=True))
    raised = jnp.exp(scores - row_max)
    attn_w = raised / lax.optimization_barrier(jnp.sum(raised, axis=2, keepdims=True))
    context = jnp.einsum('hpq,qhd->phd', low(attn_w), values, precision=PRECISE)
    return context.reshape(PAGE, HEADS * HEAD)

def layer_norm(rows, gain, shift):
    centre = rows - lax.optimization_barrier(jnp.mean(rows, axis=-1, keepdims=True))
    spread = lax.rsqrt(lax.optimization_barrier(jnp.mean(centre * centre, axis=-1, keepdims=True)) + EPS_NORM)
    return centre * spread * gain + shift

def page_order(slot_table, home_table):
    groups = N_REGIONS
    senders = jnp.broadcast_to(jnp.arange(groups, dtype=jnp.int32)[:, None], (groups, TOK_DEV))
    token_ids = jnp.broadcast_to(jnp.arange(TOK_DEV, dtype=jnp.int32)[None, :], (groups, TOK_DEV))
    lookup = jnp.zeros((groups, groups * CAP), jnp.int32).at[senders, slot_table.reshape(groups, TOK_DEV)].set(token_ids)
    arrivals = home_table.reshape(groups, TOK_DEV)
    source = arrivals // CAP
    within = arrivals % CAP
    page_rows = (source * TOK_DEV + lookup[source, senders * CAP + within]).reshape(-1)
    token_rows = jnp.zeros((groups * TOK_DEV,), jnp.int32).at[page_rows].set(jnp.arange(groups * TOK_DEV, dtype=jnp.int32))
    return (page_rows, token_rows)

def forward(inputs, w_qkv, w_out, w_up, w_down, vectors, relative, page_rows, token_rows, code_rows):
    model_dim = inputs.shape[-1]
    qkv_bias = jnp.concatenate([vectors[0], jnp.zeros_like(vectors[0]), vectors[1]])
    projected = jnp.einsum('etd,df->etf', inputs, w_qkv, precision=PRECISE) + qkv_bias
    projected = low(low_back(projected))
    paged = jnp.stack([projected[replica][page_rows[replica]] for replica in range(N_SHARD)]).reshape(-1, PAGE, 3 * model_dim)
    bias_mats = bias_table(relative)
    attend = jax.checkpoint(lambda member: page_attend(member[0], member[1], bias_mats))
    context = lax.map(attend, (paged, code_rows)).reshape(N_SHARD, -1, model_dim)
    context = jnp.stack([context[replica][token_rows[replica]] for replica in range(N_SHARD)])
    context = low(low_back(context))
    attn_out = low_back(jnp.einsum('etd,df->etf', context, w_out, precision=PRECISE) + vectors[2])
    hidden = layer_norm(inputs + attn_out, vectors[3], vectors[4])
    pre_act = low_back(jnp.einsum('etd,df->etf', low(hidden), w_up, precision=PRECISE) + vectors[8:12].reshape(-1))
    act_low = low(jax.nn.gelu(pre_act, approximate=False))
    branch = low_back(jnp.einsum('etf,fd->etd', act_low, w_down, precision=PRECISE) + vectors[5])
    return layer_norm(hidden + branch, vectors[6], vectors[7])

def adam_step(param, grad, moment, square, decay):
    moment_new = BETA_ONE * moment + (1.0 - BETA_ONE) * grad
    square_new = BETA_TWO * square + (1.0 - BETA_TWO) * grad * grad
    moment_hat = moment_new / (1.0 - BETA_ONE ** STEP_COUNT)
    square_hat = square_new / (1.0 - BETA_TWO ** STEP_COUNT)
    update = LAYER_FACTOR * (moment_hat / (jnp.sqrt(square_hat) + ADAM_EPS) + decay * param)
    return (moment_new, square_new, update)

def reference(layer_in, out_grad, w_qkv, w_out, w_up, w_down, vectors, relative, first_qkv, second_qkv, first_out, second_out, first_up, second_up, first_down, second_down, first_vectors, second_vectors, first_relative, second_relative, token_slot, home_index, box_x, box_y):
    orders = [page_order(token_slot[replica], home_index[replica]) for replica in range(N_SHARD)]
    page_rows = jnp.stack([pair[0] for pair in orders])
    token_rows = jnp.stack([pair[1] for pair in orders])
    code_rows = position_codes(box_x.reshape(-1, PAGE), box_y.reshape(-1, PAGE))
    params = (layer_in.astype(jnp.float32), w_qkv.astype(jnp.float32), w_out.astype(jnp.float32), w_up.astype(jnp.float32), w_down.astype(jnp.float32), vectors.astype(jnp.float32), relative)

    def run(inputs, wa, wb, wc, wd, vecs, rel_tab):
        return forward(inputs, wa, wb, wc, wd, vecs, rel_tab, page_rows, token_rows, code_rows)
    result, pullback = jax.vjp(run, *params)
    grads = pullback(out_grad.astype(jnp.float32))
    layer_out = result.astype(jnp.bfloat16)
    in_grad = grads[0]
    grad_qkv, grad_out, grad_up, grad_down, grad_vectors, grad_relative = (grads[1], grads[2], grads[3], grads[4], grads[5], grads[6])
    firsts_qkv, seconds_qkv, update_qkv = adam_step(params[1], grad_qkv, first_qkv, second_qkv, DECAY_RATE)
    firsts_out, seconds_out, update_out = adam_step(params[2], grad_out, first_out, second_out, DECAY_RATE)
    firsts_up, seconds_up, update_up = adam_step(params[3], grad_up, first_up, second_up, DECAY_RATE)
    firsts_down, seconds_down, update_down = adam_step(params[4], grad_down, first_down, second_down, DECAY_RATE)
    firsts_vectors, seconds_vectors, update_vectors = adam_step(params[5], grad_vectors, first_vectors, second_vectors, 0.0)
    firsts_relative, seconds_relative, update_relative = adam_step(params[6], grad_relative, first_relative, second_relative, 0.0)
    return (layer_out, in_grad, grad_qkv, firsts_qkv, seconds_qkv, update_qkv, grad_out, firsts_out, seconds_out, update_out, grad_up, firsts_up, seconds_up, update_up, grad_down, firsts_down, seconds_down, update_down, grad_vectors, firsts_vectors, seconds_vectors, update_vectors, grad_relative, firsts_relative, seconds_relative, update_relative)
```

```python
import jax
import jax.numpy as jnp
import numpy as np
from jax import lax
from jax.sharding import PartitionSpec as P

HEADS = 12
HEAD = 64
PAGE = 576


PRECISE = lax.Precision.HIGHEST
EPS_NORM = 1e-05
BETA_ONE = 0.9
BETA_TWO = 0.999
ADAM_EPS = 1e-08
LAYER_FACTOR = 0.5625
DECAY_RATE = 0.05
STEP_COUNT = 10.0


def skewed(line, size):
    count = line.shape[0]
    wide = jnp.pad(line, ((0, 0), (0, 1)))
    flat = jnp.broadcast_to(wide[:, None, :], (count, size, 2 * size)).reshape(count, -1)
    rows = flat[:, : size * (2 * size - 1)].reshape(count, size, 2 * size - 1)
    return rows[:, :, size - 1 :]


def bias_table(relative):
    seq = skewed(relative[:, :127], 64)
    horizontal = skewed(relative[:, 127:190], 32)
    vertical = skewed(relative[:, 190:253], 32)
    return (
        jnp.pad(seq, ((0, 0), (0, 64), (0, 64)))
        + jnp.pad(horizontal, ((0, 0), (64, 32), (64, 32)))
        + jnp.pad(vertical, ((0, 0), (96, 0), (96, 0)))
    )


def position_codes(box_x, box_y):
    places = jnp.arange(PAGE, dtype=jnp.int32)
    seq_bucket = places * 64 // PAGE
    columns = jnp.arange(128, dtype=jnp.int32)
    matched = (
        (columns[None, None, :] == seq_bucket[None, :, None])
        | (columns == 64 + box_x[..., None])
        | (columns == 96 + box_y[..., None])
    )
    return matched.astype(jnp.float32)


def layout_bias(code_rows, bias_mats):
    lifted = jnp.einsum("pa,hab->hpb", code_rows, bias_mats, precision=PRECISE)
    return jnp.einsum("hpb,qb->hpq", lifted, code_rows, precision=PRECISE)


def page_scores(page_qkv, code_rows, bias_mats):
    parted = page_qkv.reshape(PAGE, 3, HEADS, HEAD)
    queries = parted[:, 0]
    key_rows = parted[:, 1]
    values = parted[:, 2]
    scores = jnp.einsum(
        "phd,qhd->hpq", queries, key_rows, preferred_element_type=jnp.float32
    ) * 0.125 + layout_bias(code_rows, bias_mats)
    return (queries, key_rows, values, scores)


def page_forward(page_qkv, code_rows, bias_mats):
    queries, key_rows, values, scores = page_scores(page_qkv, code_rows, bias_mats)
    row_max = jnp.max(scores, axis=2, keepdims=True)
    raised = jnp.exp(scores - row_max)
    totals = jnp.sum(raised, axis=2, keepdims=True)
    attn_w = (raised / totals).astype(jnp.bfloat16)
    context = jnp.einsum("hpq,qhd->phd", attn_w, values, preferred_element_type=jnp.float32)
    log_total = (row_max + jnp.log(totals))[..., 0]
    return (context.reshape(PAGE, HEADS * HEAD).astype(jnp.bfloat16), log_total)


def page_backward(page_qkv, code_rows, log_total, grad_ctx, bias_mats):
    queries, key_rows, values, scores = page_scores(page_qkv, code_rows, bias_mats)
    chances = jnp.exp(scores - log_total[..., None])
    attn_w = chances.astype(jnp.bfloat16)
    grad_heads = grad_ctx.reshape(PAGE, HEADS, HEAD)
    grad_values = jnp.einsum("hpq,phd->qhd", attn_w, grad_heads, preferred_element_type=jnp.float32)
    grad_chances = jnp.einsum(
        "phd,qhd->hpq", grad_heads, values, preferred_element_type=jnp.float32
    )
    inner = jnp.sum(chances * grad_chances, axis=2, keepdims=True)
    grad_scores = (chances * (grad_chances - inner)).astype(jnp.bfloat16)
    grad_queries = (
        jnp.einsum("hpq,qhd->phd", grad_scores, key_rows, preferred_element_type=jnp.float32)
        * 0.125
    )
    grad_keys = (
        jnp.einsum("hpq,phd->qhd", grad_scores, queries, preferred_element_type=jnp.float32) * 0.125
    )
    partial_codes = jnp.einsum(
        "hpq,qb->hpb",
        grad_scores,
        code_rows.astype(jnp.bfloat16),
        preferred_element_type=jnp.float32,
    )
    grad_mats = jnp.einsum("pa,hpb->hab", code_rows, partial_codes, precision=PRECISE)
    grad_page = jnp.stack([grad_queries, grad_keys, grad_values], axis=1).reshape(
        PAGE, 3 * HEADS * HEAD
    )
    return (grad_page.astype(jnp.bfloat16), grad_mats)


def exchange(rows, targets, picks, groups, slot_cap):
    slots = groups * slot_cap
    places = jnp.arange(slots, dtype=jnp.int32)
    packing = (places[:, None] == targets[None, :]).astype(jnp.bfloat16)
    packed = jnp.dot(packing, rows, preferred_element_type=jnp.float32).astype(jnp.bfloat16)
    arrived = lax.all_to_all(
        packed.reshape(groups, slot_cap, rows.shape[1]),
        "regions",
        split_axis=0,
        concat_axis=0,
        tiled=True,
    ).reshape(slots, rows.shape[1])
    picking = (picks[:, None] == places[None, :]).astype(jnp.bfloat16)
    return jnp.dot(picking, arrived, preferred_element_type=jnp.float32)


def norm_forward(rows, gain, shift):
    centre = rows - jnp.mean(rows, axis=-1, keepdims=True)
    spread = lax.rsqrt(jnp.mean(centre * centre, axis=-1, keepdims=True) + EPS_NORM)
    normed = centre * spread
    return (normed * gain + shift, normed, spread)


def norm_back(incoming, normed, spread, gain):
    scaled = incoming * gain
    grad_rows = spread * (
        scaled
        - jnp.mean(scaled, axis=-1, keepdims=True)
        - normed * jnp.mean(scaled * normed, axis=-1, keepdims=True)
    )
    return (grad_rows, jnp.sum(incoming * normed, axis=0), jnp.sum(incoming, axis=0))


def adam_step(param, grad, moment, square, decay):
    moment_new = BETA_ONE * moment + (1.0 - BETA_ONE) * grad
    square_new = BETA_TWO * square + (1.0 - BETA_TWO) * grad * grad
    moment_hat = moment_new / (1.0 - BETA_ONE**STEP_COUNT)
    square_hat = square_new / (1.0 - BETA_TWO**STEP_COUNT)
    update = LAYER_FACTOR * (moment_hat / (jnp.sqrt(square_hat) + ADAM_EPS) + decay * param)
    return (moment_new, square_new, update)


def per_device(
    layer_in,
    out_grad,
    w_qkv,
    w_out,
    w_up,
    w_down,
    vectors,
    relative,
    first_qkv,
    second_qkv,
    first_out,
    second_out,
    first_up,
    second_up,
    first_down,
    second_down,
    first_vectors,
    second_vectors,
    first_relative,
    second_relative,
    token_slot,
    home_index,
    box_x,
    box_y,
):
    tokens = layer_in[0]
    rows_dev = tokens.shape[0]
    model_dim = tokens.shape[1]
    groups = lax.axis_size("regions")
    slot_cap = 2 * rows_dev // groups
    page_num = rows_dev // PAGE
    slot_of = token_slot[0]
    home_rows = home_index[0]
    full_qkv, full_out, full_up, full_down, full_vec = (
        lax.all_gather(w_qkv, ("regions", "shard"), axis=0, tiled=True),
        lax.all_gather(w_out, ("regions", "shard"), axis=0, tiled=True),
        lax.all_gather(w_up, ("regions", "shard"), axis=0, tiled=True),
        lax.all_gather(w_down, ("regions", "shard"), axis=0, tiled=True),
        lax.all_gather(vectors, ("regions", "shard"), axis=1, tiled=True),
    )
    vec_rows = full_vec.astype(jnp.float32)
    qkv_bias = jnp.concatenate([vec_rows[0], jnp.zeros_like(vec_rows[0]), vec_rows[1]])
    code_rows = position_codes(box_x[0].reshape(page_num, PAGE), box_y[0].reshape(page_num, PAGE))
    bias_mats = bias_table(relative)
    homed = exchange(tokens, slot_of, home_rows, groups, slot_cap).astype(jnp.bfloat16)
    cotangent = exchange(out_grad[0], slot_of, home_rows, groups, slot_cap)
    projected = (jnp.dot(homed, full_qkv, preferred_element_type=jnp.float32) + qkv_bias).astype(
        jnp.bfloat16
    )
    paged = projected.reshape(page_num, PAGE, 3 * model_dim)
    context_pages, log_totals = lax.map(
        lambda member: page_forward(member[0], member[1], bias_mats), (paged, code_rows)
    )
    context = context_pages.reshape(rows_dev, model_dim)
    attn_out = jnp.dot(context, full_out, preferred_element_type=jnp.float32) + vec_rows[2]
    hidden, normed_one, spread_one = norm_forward(
        homed.astype(jnp.float32) + attn_out, vec_rows[3], vec_rows[4]
    )
    hidden_low = hidden.astype(jnp.bfloat16)
    pre_act = jnp.dot(hidden_low, full_up, preferred_element_type=jnp.float32) + vec_rows[
        8:12
    ].reshape(-1)
    activated, gelu_back = jax.vjp(lambda value: jax.nn.gelu(value, approximate=False), pre_act)
    act_low = activated.astype(jnp.bfloat16)
    branch = jnp.dot(act_low, full_down, preferred_element_type=jnp.float32) + vec_rows[5]
    result, normed_two, spread_two = norm_forward(hidden + branch, vec_rows[6], vec_rows[7])
    grad_two, grad_gain_two, grad_shift_two = norm_back(
        cotangent, normed_two, spread_two, vec_rows[6]
    )
    grad_branch = grad_two.astype(jnp.bfloat16)
    grad_down = jnp.einsum("tf,td->fd", act_low, grad_branch, preferred_element_type=jnp.float32)
    grad_act = jnp.einsum("td,fd->tf", grad_branch, full_down, preferred_element_type=jnp.float32)
    grad_pre = gelu_back(grad_act)[0].astype(jnp.bfloat16)
    grad_up = jnp.einsum("td,tf->df", hidden_low, grad_pre, preferred_element_type=jnp.float32)
    grad_hidden = grad_two + jnp.einsum(
        "tf,df->td", grad_pre, full_up, preferred_element_type=jnp.float32
    )
    grad_one, grad_gain_one, grad_shift_one = norm_back(
        grad_hidden, normed_one, spread_one, vec_rows[3]
    )
    grad_attn = grad_one.astype(jnp.bfloat16)
    grad_out = jnp.einsum("td,te->de", context, grad_attn, preferred_element_type=jnp.float32)
    grad_context = jnp.einsum(
        "te,de->td", grad_attn, full_out, preferred_element_type=jnp.float32
    ).astype(jnp.bfloat16)
    grad_home = grad_context.reshape(page_num, PAGE, model_dim)
    grad_pages, mats_pages = lax.map(
        lambda member: page_backward(member[0], member[1], member[2], member[3], bias_mats),
        (paged, code_rows, log_totals, grad_home),
    )
    grad_dense = grad_pages.reshape(rows_dev, 3 * model_dim)
    bias_sums = jnp.sum(grad_dense.astype(jnp.float32), axis=0)
    grad_qkv = jnp.einsum("td,tf->df", homed, grad_dense, preferred_element_type=jnp.float32)
    in_home = grad_one + jnp.einsum(
        "tf,df->td", grad_dense, full_qkv, preferred_element_type=jnp.float32
    )
    layer_out = exchange(result.astype(jnp.bfloat16), home_rows, slot_of, groups, slot_cap)
    in_grad = exchange(in_home.astype(jnp.bfloat16), home_rows, slot_of, groups, slot_cap)
    grad_vec = jnp.concatenate(
        [
            jnp.stack(
                [
                    bias_sums[:model_dim],
                    bias_sums[2 * model_dim :],
                    jnp.sum(grad_attn.astype(jnp.float32), axis=0),
                    grad_gain_one,
                    grad_shift_one,
                    jnp.sum(grad_branch.astype(jnp.float32), axis=0),
                    grad_gain_two,
                    grad_shift_two,
                ]
            ),
            jnp.sum(grad_pre.astype(jnp.float32), axis=0).reshape(4, model_dim),
        ],
        axis=0,
    )
    grad_qkv, grad_out, grad_up, grad_down, grad_vectors = (
        lax.psum_scatter(grad_qkv.astype(jnp.bfloat16), ("regions", "shard"), scatter_dimension=0, tiled=True).astype(jnp.float32),
        lax.psum_scatter(grad_out.astype(jnp.bfloat16), ("regions", "shard"), scatter_dimension=0, tiled=True).astype(jnp.float32),
        lax.psum_scatter(grad_up.astype(jnp.bfloat16), ("regions", "shard"), scatter_dimension=0, tiled=True).astype(jnp.float32),
        lax.psum_scatter(grad_down.astype(jnp.bfloat16), ("regions", "shard"), scatter_dimension=0, tiled=True).astype(jnp.float32),
        lax.psum_scatter(grad_vec, ("regions", "shard"), scatter_dimension=1, tiled=True),
    )
    mats_total = jnp.sum(mats_pages, axis=0)
    table_back = jax.vjp(bias_table, relative)[1]
    grad_relative = lax.psum(table_back(mats_total)[0], ("regions", "shard"))
    firsts_qkv, seconds_qkv, update_qkv = adam_step(
        w_qkv.astype(jnp.float32), grad_qkv, first_qkv, second_qkv, DECAY_RATE
    )
    firsts_out, seconds_out, update_out = adam_step(
        w_out.astype(jnp.float32), grad_out, first_out, second_out, DECAY_RATE
    )
    firsts_up, seconds_up, update_up = adam_step(
        w_up.astype(jnp.float32), grad_up, first_up, second_up, DECAY_RATE
    )
    firsts_down, seconds_down, update_down = adam_step(
        w_down.astype(jnp.float32), grad_down, first_down, second_down, DECAY_RATE
    )
    firsts_vectors, seconds_vectors, update_vectors = adam_step(
        vectors.astype(jnp.float32), grad_vectors, first_vectors, second_vectors, 0.0
    )
    firsts_relative, seconds_relative, update_relative = adam_step(
        relative, grad_relative, first_relative, second_relative, 0.0
    )
    return (
        layer_out.astype(jnp.bfloat16)[None],
        in_grad[None],
        grad_qkv,
        firsts_qkv,
        seconds_qkv,
        update_qkv,
        grad_out,
        firsts_out,
        seconds_out,
        update_out,
        grad_up,
        firsts_up,
        seconds_up,
        update_up,
        grad_down,
        firsts_down,
        seconds_down,
        update_down,
        grad_vectors,
        firsts_vectors,
        seconds_vectors,
        update_vectors,
        grad_relative,
        firsts_relative,
        seconds_relative,
        update_relative,
    )


def solution(mesh):
    return jax.shard_map(
        per_device,
        mesh=mesh,
        in_specs=(
            P("shard", "regions", None),
            P("shard", "regions", None),
            P(("regions", "shard"), None),
            P(("regions", "shard"), None),
            P(("regions", "shard"), None),
            P(("regions", "shard"), None),
            P(None, ("regions", "shard")),
            P(),
            P(("regions", "shard"), None),
            P(("regions", "shard"), None),
            P(("regions", "shard"), None),
            P(("regions", "shard"), None),
            P(("regions", "shard"), None),
            P(("regions", "shard"), None),
            P(("regions", "shard"), None),
            P(("regions", "shard"), None),
            P(None, ("regions", "shard")),
            P(None, ("regions", "shard")),
            P(),
            P(),
            P("shard", "regions"),
            P("shard", "regions"),
            P("shard", "regions"),
            P("shard", "regions"),
        ),
        out_specs=(
            P("shard", "regions", None),
            P("shard", "regions", None),
            P(("regions", "shard"), None),
            P(("regions", "shard"), None),
            P(("regions", "shard"), None),
            P(("regions", "shard"), None),
            P(("regions", "shard"), None),
            P(("regions", "shard"), None),
            P(("regions", "shard"), None),
            P(("regions", "shard"), None),
            P(("regions", "shard"), None),
            P(("regions", "shard"), None),
            P(("regions", "shard"), None),
            P(("regions", "shard"), None),
            P(("regions", "shard"), None),
            P(("regions", "shard"), None),
            P(("regions", "shard"), None),
            P(("regions", "shard"), None),
            P(None, ("regions", "shard")),
            P(None, ("regions", "shard")),
            P(None, ("regions", "shard")),
            P(None, ("regions", "shard")),
            P(),
            P(),
            P(),
            P(),
        ),
        check_vma=False,
    )
```

```python
import functools
import jax
import jax.numpy as jnp
import numpy as np
from jax import lax
from jax.experimental import pallas as pl
from jax.experimental.pallas import tpu as pltpu
from jax.sharding import PartitionSpec as P

HEADS = 12
HEAD = 64
PAGE = 576


PRECISE = lax.Precision.HIGHEST
EPS_NORM = 1e-05
BETA_ONE = 0.9
BETA_TWO = 0.999
ADAM_EPS = 1e-08
LAYER_FACTOR = 0.5625
DECAY_RATE = 0.05
STEP_COUNT = 10.0


def skewed(line, size):
    count = line.shape[0]
    wide = jnp.pad(line, ((0, 0), (0, 1)))
    flat = jnp.broadcast_to(wide[:, None, :], (count, size, 2 * size)).reshape(count, -1)
    rows = flat[:, : size * (2 * size - 1)].reshape(count, size, 2 * size - 1)
    return rows[:, :, size - 1 :]


def bias_table(relative):
    seq = skewed(relative[:, :127], 64)
    horizontal = skewed(relative[:, 127:190], 32)
    vertical = skewed(relative[:, 190:253], 32)
    return (
        jnp.pad(seq, ((0, 0), (0, 64), (0, 64)))
        + jnp.pad(horizontal, ((0, 0), (64, 32), (64, 32)))
        + jnp.pad(vertical, ((0, 0), (96, 0), (96, 0)))
    )


def position_codes(box_x, box_y):
    places = jnp.arange(PAGE, dtype=jnp.int32)
    seq_bucket = places * 64 // PAGE
    columns = jnp.arange(128, dtype=jnp.int32)
    matched = (
        (columns[None, None, :] == seq_bucket[None, :, None])
        | (columns == 64 + box_x[..., None])
        | (columns == 96 + box_y[..., None])
    )
    return matched.astype(jnp.float32)


def layout_bias(code_rows, bias_mats):
    lifted = jnp.einsum("pa,hab->hpb", code_rows, bias_mats, precision=PRECISE)
    return jnp.einsum("hpb,qb->hpq", lifted, code_rows, precision=PRECISE)


def page_scores(page_qkv, code_rows, bias_mats):
    parted = page_qkv.reshape(PAGE, 3, HEADS, HEAD)
    queries = parted[:, 0]
    key_rows = parted[:, 1]
    values = parted[:, 2]
    scores = jnp.einsum(
        "phd,qhd->hpq", queries, key_rows, preferred_element_type=jnp.float32
    ) * 0.125 + layout_bias(code_rows, bias_mats)
    return (queries, key_rows, values, scores)


def page_forward(page_qkv, code_rows, bias_mats):
    queries, key_rows, values, scores = page_scores(page_qkv, code_rows, bias_mats)
    row_max = jnp.max(scores, axis=2, keepdims=True)
    raised = jnp.exp(scores - row_max)
    totals = jnp.sum(raised, axis=2, keepdims=True)
    attn_w = (raised / totals).astype(jnp.bfloat16)
    context = jnp.einsum("hpq,qhd->phd", attn_w, values, preferred_element_type=jnp.float32)
    log_total = (row_max + jnp.log(totals))[..., 0]
    return (context.reshape(PAGE, HEADS * HEAD).astype(jnp.bfloat16), log_total)


def page_backward(page_qkv, code_rows, log_total, grad_ctx, bias_mats):
    queries, key_rows, values, scores = page_scores(page_qkv, code_rows, bias_mats)
    chances = jnp.exp(scores - log_total[..., None])
    attn_w = chances.astype(jnp.bfloat16)
    grad_heads = grad_ctx.reshape(PAGE, HEADS, HEAD)
    grad_values = jnp.einsum("hpq,phd->qhd", attn_w, grad_heads, preferred_element_type=jnp.float32)
    grad_chances = jnp.einsum(
        "phd,qhd->hpq", grad_heads, values, preferred_element_type=jnp.float32
    )
    inner = jnp.sum(chances * grad_chances, axis=2, keepdims=True)
    grad_scores = (chances * (grad_chances - inner)).astype(jnp.bfloat16)
    grad_queries = (
        jnp.einsum("hpq,qhd->phd", grad_scores, key_rows, preferred_element_type=jnp.float32)
        * 0.125
    )
    grad_keys = (
        jnp.einsum("hpq,phd->qhd", grad_scores, queries, preferred_element_type=jnp.float32) * 0.125
    )
    partial_codes = jnp.einsum(
        "hpq,qb->hpb",
        grad_scores,
        code_rows.astype(jnp.bfloat16),
        preferred_element_type=jnp.float32,
    )
    grad_mats = jnp.einsum("pa,hpb->hab", code_rows, partial_codes, precision=PRECISE)
    grad_page = jnp.stack([grad_queries, grad_keys, grad_values], axis=1).reshape(
        PAGE, 3 * HEADS * HEAD
    )
    return (grad_page.astype(jnp.bfloat16), grad_mats)


def exchange(rows, targets, picks, groups, slot_cap):
    slots = groups * slot_cap
    places = jnp.arange(slots, dtype=jnp.int32)
    packing = (places[:, None] == targets[None, :]).astype(jnp.bfloat16)
    packed = jnp.dot(packing, rows, preferred_element_type=jnp.float32).astype(jnp.bfloat16)
    arrived = lax.all_to_all(
        packed.reshape(groups, slot_cap, rows.shape[1]),
        "regions",
        split_axis=0,
        concat_axis=0,
        tiled=True,
    ).reshape(slots, rows.shape[1])
    picking = (picks[:, None] == places[None, :]).astype(jnp.bfloat16)
    return jnp.dot(picking, arrived, preferred_element_type=jnp.float32)


def norm_forward(rows, gain, shift):
    centre = rows - jnp.mean(rows, axis=-1, keepdims=True)
    spread = lax.rsqrt(jnp.mean(centre * centre, axis=-1, keepdims=True) + EPS_NORM)
    normed = centre * spread
    return (normed * gain + shift, normed, spread)


def norm_back(incoming, normed, spread, gain):
    scaled = incoming * gain
    grad_rows = spread * (
        scaled
        - jnp.mean(scaled, axis=-1, keepdims=True)
        - normed * jnp.mean(scaled * normed, axis=-1, keepdims=True)
    )
    return (grad_rows, jnp.sum(incoming * normed, axis=0), jnp.sum(incoming, axis=0))


def adam_step(param, grad, moment, square, decay):
    moment_new = BETA_ONE * moment + (1.0 - BETA_ONE) * grad
    square_new = BETA_TWO * square + (1.0 - BETA_TWO) * grad * grad
    moment_hat = moment_new / (1.0 - BETA_ONE**STEP_COUNT)
    square_hat = square_new / (1.0 - BETA_TWO**STEP_COUNT)
    update = LAYER_FACTOR * (moment_hat / (jnp.sqrt(square_hat) + ADAM_EPS) + decay * param)
    return (moment_new, square_new, update)


MESH = pl.DeviceIdType.MESH
PEERS = 16
VEC_COLS = 256


def place():
    me = lax.axis_index("regions")
    core = lax.axis_index("shard")
    z = lax.div(me, 4)
    y = lax.div(lax.rem(me, 4), 2)
    x = lax.rem(me, 2)
    return me, core, z, y, x


def enter(me, core):
    barrier = pltpu.get_barrier_semaphore()
    for k in range(1, PEERS):
        pl.semaphore_signal(barrier, inc=1, device_id=(me ^ k, core), device_id_type=MESH)
    pl.semaphore_signal(barrier, inc=1, device_id=(me, 1 - core), device_id_type=MESH)
    pl.semaphore_wait(barrier, PEERS)


def remote(src, dst, send, recv, device):
    return pltpu.make_async_remote_copy(
        src_ref=src, dst_ref=dst, send_sem=send, recv_sem=recv, device_id=device, device_id_type=MESH
    )


class Exchange:
    def __init__(self, where, packed, arrived, send, recv, local):
        self.me, self.core = where[0], where[1]
        self.packed, self.arrived = packed, arrived
        self.send, self.recv, self.local = send, recv, local
        self.slots, self.half = packed.shape[1], packed.shape[2]

    def pack(self, rows, row_of):
        left, right = rows[:, : self.half], rows[:, self.half :]

        def one(k, carry):
            d = self.me ^ k
            base = d * self.slots
            at = lax.broadcasted_iota(jnp.int32, (self.slots, rows.shape[0]), 0) + base
            target = row_of[...]
            lefts = jnp.where(at == target, 1.0, 0.0).astype(jnp.bfloat16)
            rights = jnp.where(at == target + self.slots // 2, 1.0, 0.0).astype(jnp.bfloat16)
            block = jnp.dot(lefts, left, preferred_element_type=jnp.float32) + jnp.dot(
                rights, right, preferred_element_type=jnp.float32
            )
            self.packed[d] = block.astype(jnp.bfloat16)

            @pl.when(k > 0)
            def _():
                self.copy(k).start()

            return carry

        lax.fori_loop(0, PEERS, one, 0)
        self.own().start()

    def copy(self, k):
        d = self.me ^ k
        return remote(
            self.packed.at[d], self.arrived.at[self.me], self.send.at[k], self.recv.at[k], (d, self.core)
        )

    def own(self):
        return pltpu.make_async_copy(self.packed.at[self.me], self.arrived.at[self.me], self.local)

    def wait(self):
        self.own().wait()

        def one(k, carry):
            self.copy(k).wait()
            return carry

        lax.fori_loop(1, PEERS, one, 0)

    def unpack(self, row_of, out, kind):
        total = PEERS * self.slots
        for part in range(2):
            wanted = row_of[...] + part * (self.slots // 2)
            at = lax.broadcasted_iota(jnp.int32, (out.shape[0], total), 1)
            picking = jnp.where(at == wanted, 1.0, 0.0).astype(jnp.bfloat16)
            got = jnp.dot(
                picking,
                self.arrived[...].reshape(total, self.half),
                preferred_element_type=jnp.float32,
            )
            out[:, part * self.half : (part + 1) * self.half] = got.astype(kind)


def pieces_of(rows, half):
    if rows % 32 == 0:
        return [(0, rows // 2, 0, half, True), (rows // 2, rows // 2, 0, half, False)]
    cut = (half // 128 + 1) // 2 * 128
    return [(0, rows, 0, cut, True), (0, rows, cut, half - cut, False)]


class Gather:
    STAGES = 7

    def __init__(self, where, whole, piece, sems):
        self.where, self.whole, self.piece, self.sems = where, whole, piece, sems

    def part(self, z, y, x):
        core = self.where[1]
        r0, rows, c0, cols, _ = self.piece
        half = self.whole.shape[4] // 2
        at = pl.multiple_of(core * half + c0, 128)
        return self.whole.at[z, y, x, pl.ds(r0, rows), pl.ds(at, cols)]

    def along_z(self, t, upward):
        me, core, z, y, x = self.where
        step = 1 if upward else -1
        origin = z - step * t
        ref = self.part(origin, y, x)
        i = 2 * t + (1 if upward else 0)
        return remote(ref, ref, self.sems.at[0, i], self.sems.at[1, i], (me + 4 * step, core))

    def z_sends(self, t, do):
        z = self.where[2]

        @pl.when((z >= t) & (z <= 2))
        def _():
            do(self.along_z(t, True))

        @pl.when((z + t <= 3) & (z >= 1))
        def _():
            do(self.along_z(t, False))

    def z_waits(self, t):
        z = self.where[2]

        @pl.when(z - 1 - t >= 0)
        def _():
            me, core, z, y, x = self.where
            ref = self.part(z - 1 - t, y, x)
            i = 2 * t + 1
            remote(ref, ref, self.sems.at[0, i], self.sems.at[1, i], (me, 1 - core)).wait_recv()

        @pl.when(z + 1 + t <= 3)
        def _():
            me, core, z, y, x = self.where
            ref = self.part(z + 1 + t, y, x)
            i = 2 * t
            remote(ref, ref, self.sems.at[0, i], self.sems.at[1, i], (me, 1 - core)).wait_recv()

    def plane(self, n):
        me, core, z, y, x = self.where
        x_first = self.piece[4]
        every = slice(None)
        if n == 2:
            ref, device = self.part(every, every, every), (me, 1 - core)
        elif n == 0:
            ref, device = self.part(every, y, x), (me ^ (1 if x_first else 2), core)
        elif x_first:
            ref, device = self.part(every, y, every), (me ^ 2, core)
        else:
            ref, device = self.part(every, every, x), (me ^ 1, core)
        return remote(ref, ref, self.sems.at[0, 6 + n], self.sems.at[1, 6 + n], device)

    def run(self, stage):
        if stage < 3:
            if stage:
                self.z_waits(stage - 1)
            self.z_sends(stage, lambda copy: copy.start())
        elif stage == 3:
            self.z_waits(2)
            self.plane(0).start()
        elif stage < 6:
            self.plane(stage - 4).wait_recv()
            self.plane(stage - 3).start()
        else:
            self.plane(2).wait_recv()

    def sent(self):
        for t in range(3):
            self.z_sends(t, lambda copy: copy.wait_send())
        for n in range(3):
            self.plane(n).wait_send()


class Scatter:
    STAGES = 9

    def __init__(self, where, local, sums, from_core, from_near, from_far, from_z, piece, sems):
        self.where, self.local, self.sums, self.piece, self.sems = where, local, sums, piece, sems
        self.from_core, self.from_near, self.from_far, self.from_z = from_core, from_near, from_far, from_z
        self.half = sums.shape[4]

    def cut(self, ref, *lead, core=None):
        r0, rows, c0, cols, _ = self.piece
        at = c0 if core is None else pl.multiple_of(core * self.half + c0, 128)
        return ref.at[(*lead, pl.ds(r0, rows), pl.ds(at, cols))]

    def between_cores(self):
        me, core = self.where[0], self.where[1]
        every = slice(None)
        src = self.cut(self.local, every, every, every, core=1 - core)
        dst = self.cut(self.from_core, every, every, every)
        return remote(src, dst, self.sems.at[0, 0], self.sems.at[1, 0], (me, 1 - core))

    def near(self):
        me, core, z, y, x = self.where
        every = slice(None)
        if self.piece[4]:
            src, device = self.cut(self.sums, every, 1 - y, every), (me ^ 2, core)
        else:
            src, device = self.cut(self.sums, every, every, 1 - x), (me ^ 1, core)
        dst = self.cut(self.from_near, every, every)
        return remote(src, dst, self.sems.at[0, 1], self.sems.at[1, 1], device)

    def far(self):
        me, core, z, y, x = self.where
        every = slice(None)
        if self.piece[4]:
            src, device = self.cut(self.sums, every, y, 1 - x), (me ^ 1, core)
        else:
            src, device = self.cut(self.sums, every, 1 - y, x), (me ^ 2, core)
        dst = self.cut(self.from_far, every)
        return remote(src, dst, self.sems.at[0, 2], self.sems.at[1, 2], device)

    def along_z(self, sender, upward):
        me, core, z, y, x = self.where
        lead = pl.ds(sender + 1, 3 - sender) if upward else pl.ds(0, sender)
        src = self.cut(self.sums, lead, y, x)
        dst = self.cut(self.from_z, 1 if upward else 0, lead)
        i = 3 + (1 if upward else 0)
        step = 4 if upward else -4
        return remote(src, dst, self.sems.at[0, i], self.sems.at[1, i], (me + step, core))

    def add(self, target, other):
        total = target[...].astype(jnp.float32) + other[...].astype(jnp.float32)
        target[...] = total.astype(jnp.bfloat16)

    def z_got(self, sender, upward):
        me, core, z, y, x = self.where
        self.along_z(sender, upward).wait_recv()
        for d in range(sender + 1, 4) if upward else range(sender):
            self.add(self.cut(self.sums, d, y, x), self.cut(self.from_z, 1 if upward else 0, d))

    def run(self, stage):
        me, core, z, y, x = self.where
        if stage == 0:
            self.between_cores().start()
        elif stage == 1:
            self.between_cores().wait_recv()

            def one(i, carry):
                a, b, c = lax.div(i, 4), lax.div(lax.rem(i, 4), 2), lax.rem(i, 2)
                mine = self.cut(self.local, a, b, c, core=core)[...].astype(jnp.float32)
                other = self.cut(self.from_core, a, b, c)[...].astype(jnp.float32)
                self.cut(self.sums, a, b, c)[...] = (mine + other).astype(jnp.bfloat16)
                return carry

            lax.fori_loop(0, 16, one, 0)
            self.near().start()
        elif stage == 2:
            self.near().wait_recv()

            def one(i, carry):
                a, b = lax.div(i, 2), lax.rem(i, 2)
                target = self.cut(self.sums, a, y, b) if self.piece[4] else self.cut(self.sums, a, b, x)
                self.add(target, self.cut(self.from_near, a, b))
                return carry

            lax.fori_loop(0, 8, one, 0)
            self.far().start()
        elif stage == 3:
            self.far().wait_recv()

            def one(i, carry):
                self.add(self.cut(self.sums, i, y, x), self.cut(self.from_far, i))
                return carry

            lax.fori_loop(0, 4, one, 0)

            @pl.when(z == 3)
            def _():
                self.along_z(3, False).start()

            @pl.when(z == 0)
            def _():
                self.along_z(0, True).start()

        elif stage == 4:

            @pl.when(z == 2)
            def _():
                self.z_got(3, False)
                self.along_z(2, False).start()

            @pl.when(z == 1)
            def _():
                self.z_got(0, True)
                self.along_z(1, True).start()

        elif stage == 5:

            @pl.when(z == 1)
            def _():
                self.z_got(2, False)
                self.along_z(1, False).start()

            @pl.when(z == 2)
            def _():
                self.z_got(1, True)
                self.along_z(2, True).start()

        elif stage == 6:

            @pl.when(z == 0)
            def _():
                self.z_got(1, False)

            @pl.when(z == 3)
            def _():
                self.z_got(2, True)

    def sent(self):
        z = self.where[2]
        self.between_cores().wait_send()
        self.near().wait_send()
        self.far().wait_send()
        for sender in range(4):

            @pl.when(z == sender)
            def _(sender=sender):
                if sender > 0:
                    self.along_z(sender, False).wait_send()
                if sender < 3:
                    self.along_z(sender, True).wait_send()


def staggered(tasks, stages, extra=None):
    for k in range(len(tasks) + stages - 1):
        for i, task in enumerate(tasks):
            if 0 <= k - i < stages:
                task.run(k - i)
        if extra is not None:
            extra(k)


def inbound_kernel(
    rows_ref, grad_ref, slot_line, home_column, s_qkv, s_out, s_up, s_down,
    homed, cotangent, w_qkv, w_out, w_up, w_down,
    packed_a, arrived_a, packed_b, arrived_b, p_qkv, p_out, p_up, p_down, b_qkv, b_out, b_up, b_down,
    send_a, recv_a, send_b, recv_b, local_sems, pair_sems, block_sems, piece_sems,
):
    where = place()
    me, core, z, y, x = where
    enter(me, core)
    shards = (s_qkv, s_out, s_up, s_down)
    others = (p_qkv, p_out, p_up, p_down)
    blocks = (b_qkv, b_out, b_up, b_down)
    wholes = (w_qkv, w_out, w_up, w_down)
    pairs = [
        remote(shards[i].at[1 - core], others[i], pair_sems.at[0, i], pair_sems.at[1, i], (me, 1 - core))
        for i in range(4)
    ]
    for pair in pairs:
        pair.start()
    moved = Exchange(where, packed_a, arrived_a, send_a, recv_a, local_sems.at[0])
    moved_grad = Exchange(where, packed_b, arrived_b, send_b, recv_b, local_sems.at[1])
    moved.pack(rows_ref, slot_line)
    placed = []
    tasks = []
    for i in range(4):
        pairs[i].wait_recv()
        half = blocks[i].shape[1]
        rows = blocks[i].shape[0] // 2
        mine = shards[i][core][:rows].astype(jnp.float32)
        other = others[i][:rows].astype(jnp.float32)
        first = jnp.where(core == 0, mine, other)
        second = jnp.where(core == 0, other, mine)
        blocks[i][...] = jnp.concatenate([first, second], axis=0).astype(jnp.bfloat16)
        at = pl.multiple_of(core * half, 128)
        copy = pltpu.make_async_copy(
            blocks[i], wholes[i].at[z, y, x, :, pl.ds(at, half)], block_sems.at[i]
        )
        copy.start()
        placed.append(copy)
    for i in range(4):
        placed[i].wait()
        for piece in pieces_of(blocks[i].shape[0], blocks[i].shape[1]):
            n = len(tasks)
            tasks.append(Gather(where, wholes[i], piece, piece_sems.at[n]))

    def extra(k):
        if k == 2:
            moved_grad.pack(grad_ref, slot_line)

    staggered(tasks, Gather.STAGES, extra)
    moved.wait()
    moved.unpack(home_column, homed, jnp.bfloat16)
    moved_grad.wait()
    moved_grad.unpack(home_column, cotangent, jnp.bfloat16)
    for pair in pairs:
        pair.wait_send()
    for task in tasks:
        task.sent()


def vmem(count):
    return [pl.BlockSpec(memory_space=pltpu.VMEM)] * count


def inbound(rows, grads, slot_line, home_column, shards):
    tokens, width = rows.shape
    slots = 2 * (2 * tokens // PEERS)
    buffer = pltpu.VMEM((PEERS, slots, width // 2), jnp.bfloat16)
    wholes, pair_shapes, block_shapes = [], [], []
    for shard, padded in shards:
        half = padded.shape[2]
        wholes.append(jax.ShapeDtypeStruct((4, 2, 2, 2 * shard, 2 * half), jnp.bfloat16))
        pair_shapes.append(pltpu.VMEM(padded.shape[1:], jnp.bfloat16))
        block_shapes.append(pltpu.VMEM((2 * shard, half), jnp.bfloat16))
    dma = pltpu.SemaphoreType.DMA
    return pl.pallas_call(
        inbound_kernel,
        out_shape=[jax.ShapeDtypeStruct(rows.shape, jnp.bfloat16)] * 2 + wholes,
        in_specs=vmem(8),
        out_specs=vmem(6),
        scratch_shapes=[buffer] * 4 + pair_shapes + block_shapes
        + [dma((PEERS,)), dma((PEERS,)), dma((PEERS,)), dma((PEERS,)), dma((2,)), dma((2, 4)), dma((4,)), dma((8, 2, 9))],
        compiler_params=pltpu.CompilerParams(
            collective_id=1, has_side_effects=True, vmem_limit_bytes=60 << 20
        ),
        name="inbound",
    )(rows, grads, slot_line, home_column, *[padded for _, padded in shards])


def outbound_kernel(
    result_ref, grad_ref, home_line, slot_column, table_ref, g_qkv, g_out, g_up, g_down,
    result_out, grad_out, table_out, o_qkv, o_out, o_up, o_down,
    packed_a, arrived_a, packed_b, arrived_b, table_got,
    t_qkv, t_out, t_up, t_down, c_qkv, c_out, c_up, c_down, n_qkv, n_out, n_up, n_down,
    f_qkv, f_out, f_up, f_down, z_qkv, z_out, z_up, z_down, e_qkv, e_out, e_up, e_down,
    send_a, recv_a, send_b, recv_b, local_sems, table_sems, piece_sems, last_sems,
):
    where = place()
    me, core, z, y, x = where
    enter(me, core)
    local = (g_qkv, g_out, g_up, g_down)
    sums = (t_qkv, t_out, t_up, t_down)
    from_core = (c_qkv, c_out, c_up, c_down)
    from_near = (n_qkv, n_out, n_up, n_down)
    from_far = (f_qkv, f_out, f_up, f_down)
    from_z = (z_qkv, z_out, z_up, z_down)
    ends = (e_qkv, e_out, e_up, e_down)
    outs = (o_qkv, o_out, o_up, o_down)
    tasks = []
    for i in (3, 2, 1, 0):
        for piece in pieces_of(sums[i].shape[3], sums[i].shape[4]):
            n = len(tasks)
            tasks.append(
                Scatter(where, local[i], sums[i], from_core[i], from_near[i], from_far[i], from_z[i], piece, piece_sems.at[n])
            )
    moved = Exchange(where, packed_a, arrived_a, send_a, recv_a, local_sems.at[0])
    moved_grad = Exchange(where, packed_b, arrived_b, send_b, recv_b, local_sems.at[1])
    table_out[...] = table_ref[...]
    steps = [(me, 1 - core), (me ^ 1, core), (me ^ 2, core), (me ^ 4, core), (me ^ 8, core)]
    shares = [
        remote(table_got.at[0, n], table_got.at[1, n], table_sems.at[0, n], table_sems.at[1, n], device)
        for n, device in enumerate(steps)
    ]

    def extra(k):
        if k == 0:
            moved.pack(result_ref, home_line)
        if k == 3:
            moved_grad.pack(grad_ref, home_line)
        if 4 <= k <= 9:
            n = k - 4
            if n > 0:
                shares[n - 1].wait_recv()
                table_out[...] += table_got[1, n - 1]
            if n < 5:
                table_got[0, n] = table_out[...]
                shares[n].start()

    staggered(tasks, 7, extra)
    finals = []
    for i in (3, 2, 1, 0):
        block = sums[i][z, y, x].astype(jnp.float32)
        rows = block.shape[0] // 2
        ends[i][0] = block[:rows]
        ends[i][1] = block[rows:]
        outs[i][core] = ends[i][core]
        copy = remote(ends[i].at[1 - core], outs[i].at[core], last_sems.at[0, i], last_sems.at[1, i], (me, 1 - core))
        copy.start()
        finals.append(copy)
    moved.wait()
    moved.unpack(slot_column, result_out, jnp.bfloat16)
    moved_grad.wait()
    moved_grad.unpack(slot_column, grad_out, jnp.float32)
    for copy in finals:
        copy.wait()
    for share in shares:
        share.wait_send()
    for task in tasks:
        task.sent()


def outbound(result, grads, home_line, slot_column, table, locals_):
    tokens, width = result.shape
    slots = 2 * (2 * tokens // PEERS)
    buffer = pltpu.VMEM((PEERS, slots, width // 2), jnp.bfloat16)
    halves = [(g.shape[3], g.shape[4] // 2) for g in locals_]
    low = jnp.bfloat16
    scratch = (
        [buffer] * 4
        + [pltpu.VMEM((2, 5, *table.shape), jnp.float32)]
        + [pltpu.VMEM((4, 2, 2, r, h), low) for r, h in halves]
        + [pltpu.VMEM((4, 2, 2, r, h), low) for r, h in halves]
        + [pltpu.VMEM((4, 2, r, h), low) for r, h in halves]
        + [pltpu.VMEM((4, r, h), low) for r, h in halves]
        + [pltpu.VMEM((2, 4, r, h), low) for r, h in halves]
        + [pltpu.VMEM((2, r // 2, h), jnp.float32) for r, h in halves]
    )
    dma = pltpu.SemaphoreType.DMA
    return pl.pallas_call(
        outbound_kernel,
        out_shape=[
            jax.ShapeDtypeStruct(result.shape, jnp.bfloat16),
            jax.ShapeDtypeStruct(result.shape, jnp.float32),
            jax.ShapeDtypeStruct(table.shape, jnp.float32),
        ]
        + [jax.ShapeDtypeStruct((2, r // 2, h), jnp.float32) for r, h in halves],
        in_specs=vmem(9),
        out_specs=vmem(7),
        scratch_shapes=scratch
        + [dma((PEERS,)), dma((PEERS,)), dma((PEERS,)), dma((PEERS,)), dma((2,)), dma((2, 5)), dma((8, 2, 5)), dma((2, 4))],
        compiler_params=pltpu.CompilerParams(
            collective_id=2, has_side_effects=True, vmem_limit_bytes=60 << 20
        ),
        name="outbound",
    )(result, grads, home_line, slot_column, table, *locals_)


def shard_halves(shard):
    rows, columns = shard.shape
    halves = shard.reshape(rows, 2, columns // 2).transpose(1, 0, 2)
    return (rows, jnp.pad(halves, ((0, 0), (0, -rows % 16), (0, 0))))


def chip_blocks(grad):
    rows, columns = grad.shape
    return grad.astype(jnp.bfloat16).reshape(4, 2, 2, rows // PEERS, columns)


def joined(halves):
    return jnp.concatenate([halves[0], halves[1]], axis=1)


def per_device(
    kernels,
    layer_in,
    out_grad,
    w_qkv,
    w_out,
    w_up,
    w_down,
    vectors,
    relative,
    first_qkv,
    second_qkv,
    first_out,
    second_out,
    first_up,
    second_up,
    first_down,
    second_down,
    first_vectors,
    second_vectors,
    first_relative,
    second_relative,
    token_slot,
    home_index,
    box_x,
    box_y,
):
    tokens = layer_in[0]
    rows_dev = tokens.shape[0]
    model_dim = tokens.shape[1]
    groups = lax.axis_size("regions")
    slot_cap = 2 * rows_dev // groups
    page_num = rows_dev // PAGE
    slot_of = token_slot[0]
    home_rows = home_index[0]
    if kernels:
        beside = jnp.pad(vectors.T, ((0, 0), (0, VEC_COLS - vectors.shape[0])))
        wide_qkv = jnp.concatenate([w_qkv, beside], axis=1)
        slot_at = slot_of + slot_cap * (slot_of // slot_cap)
        home_at = home_rows + slot_cap * (home_rows // slot_cap)
        homed, cotangent, *fulls = inbound(
            tokens,
            out_grad[0],
            slot_at[None],
            home_at[:, None],
            [shard_halves(shard) for shard in (wide_qkv, w_out, w_up, w_down)],
        )
        cotangent = cotangent.astype(jnp.float32)
        full_qkv, full_out, full_up, full_down = [
            full.reshape(-1, full.shape[4]) for full in fulls
        ]
        full_vec = full_qkv[:, 3 * model_dim : 3 * model_dim + vectors.shape[0]].T
        full_qkv = full_qkv[:, : 3 * model_dim]
    else:
        full_qkv, full_out, full_up, full_down, full_vec = (
            lax.all_gather(w_qkv, ("regions", "shard"), axis=0, tiled=True),
            lax.all_gather(w_out, ("regions", "shard"), axis=0, tiled=True),
            lax.all_gather(w_up, ("regions", "shard"), axis=0, tiled=True),
            lax.all_gather(w_down, ("regions", "shard"), axis=0, tiled=True),
            lax.all_gather(vectors, ("regions", "shard"), axis=1, tiled=True),
        )
        homed = exchange(tokens, slot_of, home_rows, groups, slot_cap).astype(jnp.bfloat16)
        cotangent = exchange(out_grad[0], slot_of, home_rows, groups, slot_cap)
    vec_rows = full_vec.astype(jnp.float32)
    qkv_bias = jnp.concatenate([vec_rows[0], jnp.zeros_like(vec_rows[0]), vec_rows[1]])
    code_rows = position_codes(box_x[0].reshape(page_num, PAGE), box_y[0].reshape(page_num, PAGE))
    bias_mats = bias_table(relative)
    projected = (jnp.dot(homed, full_qkv, preferred_element_type=jnp.float32) + qkv_bias).astype(
        jnp.bfloat16
    )
    paged = projected.reshape(page_num, PAGE, 3 * model_dim)
    context_pages, log_totals = lax.map(
        lambda member: page_forward(member[0], member[1], bias_mats), (paged, code_rows)
    )
    context = context_pages.reshape(rows_dev, model_dim)
    attn_out = jnp.dot(context, full_out, preferred_element_type=jnp.float32) + vec_rows[2]
    hidden, normed_one, spread_one = norm_forward(
        homed.astype(jnp.float32) + attn_out, vec_rows[3], vec_rows[4]
    )
    hidden_low = hidden.astype(jnp.bfloat16)
    pre_act = jnp.dot(hidden_low, full_up, preferred_element_type=jnp.float32) + vec_rows[
        8:12
    ].reshape(-1)
    activated, gelu_back = jax.vjp(lambda value: jax.nn.gelu(value, approximate=False), pre_act)
    act_low = activated.astype(jnp.bfloat16)
    branch = jnp.dot(act_low, full_down, preferred_element_type=jnp.float32) + vec_rows[5]
    result, normed_two, spread_two = norm_forward(hidden + branch, vec_rows[6], vec_rows[7])
    grad_two, grad_gain_two, grad_shift_two = norm_back(
        cotangent, normed_two, spread_two, vec_rows[6]
    )
    grad_branch = grad_two.astype(jnp.bfloat16)
    grad_down = jnp.einsum("tf,td->fd", act_low, grad_branch, preferred_element_type=jnp.float32)
    grad_act = jnp.einsum("td,fd->tf", grad_branch, full_down, preferred_element_type=jnp.float32)
    grad_pre = gelu_back(grad_act)[0].astype(jnp.bfloat16)
    grad_up = jnp.einsum("td,tf->df", hidden_low, grad_pre, preferred_element_type=jnp.float32)
    grad_hidden = grad_two + jnp.einsum(
        "tf,df->td", grad_pre, full_up, preferred_element_type=jnp.float32
    )
    grad_one, grad_gain_one, grad_shift_one = norm_back(
        grad_hidden, normed_one, spread_one, vec_rows[3]
    )
    grad_attn = grad_one.astype(jnp.bfloat16)
    grad_out = jnp.einsum("td,te->de", context, grad_attn, preferred_element_type=jnp.float32)
    grad_context = jnp.einsum(
        "te,de->td", grad_attn, full_out, preferred_element_type=jnp.float32
    ).astype(jnp.bfloat16)
    grad_home = grad_context.reshape(page_num, PAGE, model_dim)
    grad_pages, mats_pages = lax.map(
        lambda member: page_backward(member[0], member[1], member[2], member[3], bias_mats),
        (paged, code_rows, log_totals, grad_home),
    )
    grad_dense = grad_pages.reshape(rows_dev, 3 * model_dim)
    bias_sums = jnp.sum(grad_dense.astype(jnp.float32), axis=0)
    grad_qkv = jnp.einsum("td,tf->df", homed, grad_dense, preferred_element_type=jnp.float32)
    in_home = grad_one + jnp.einsum(
        "tf,df->td", grad_dense, full_qkv, preferred_element_type=jnp.float32
    )
    grad_vec = jnp.concatenate(
        [
            jnp.stack(
                [
                    bias_sums[:model_dim],
                    bias_sums[2 * model_dim :],
                    jnp.sum(grad_attn.astype(jnp.float32), axis=0),
                    grad_gain_one,
                    grad_shift_one,
                    jnp.sum(grad_branch.astype(jnp.float32), axis=0),
                    grad_gain_two,
                    grad_shift_two,
                ]
            ),
            jnp.sum(grad_pre.astype(jnp.float32), axis=0).reshape(4, model_dim),
        ],
        axis=0,
    )
    mats_total = jnp.sum(mats_pages, axis=0)
    table_back = jax.vjp(bias_table, relative)[1]
    table_local = table_back(mats_total)[0]
    if kernels:
        beside = jnp.pad(grad_vec.T, ((0, 0), (0, VEC_COLS - grad_vec.shape[0])))
        heads, entries = relative.shape
        layer_out, in_grad, table_sum, *ends = outbound(
            result.astype(jnp.bfloat16),
            in_home.astype(jnp.bfloat16),
            home_at[None],
            slot_at[:, None],
            jnp.pad(table_local, ((0, -heads % 8), (0, -entries % 128))),
            [
                chip_blocks(grad)
                for grad in (
                    jnp.concatenate([grad_qkv, beside], axis=1),
                    grad_out,
                    grad_up,
                    grad_down,
                )
            ],
        )
        grad_relative = table_sum[:heads, :entries]
        grad_qkv, grad_out, grad_up, grad_down = [joined(end) for end in ends]
        grad_vectors = grad_qkv[:, 3 * model_dim : 3 * model_dim + vectors.shape[0]].T
        grad_qkv = grad_qkv[:, : 3 * model_dim]
    else:
        layer_out = exchange(result.astype(jnp.bfloat16), home_rows, slot_of, groups, slot_cap)
        in_grad = exchange(in_home.astype(jnp.bfloat16), home_rows, slot_of, groups, slot_cap)
        over = ("regions", "shard")
        grad_qkv, grad_out, grad_up, grad_down = [
            lax.psum_scatter(grad, over, scatter_dimension=0, tiled=True)
            for grad in (grad_qkv, grad_out, grad_up, grad_down)
        ]
        grad_vectors = lax.psum_scatter(grad_vec, over, scatter_dimension=1, tiled=True)
        grad_relative = lax.psum(table_local, over)
    firsts_qkv, seconds_qkv, update_qkv = adam_step(
        w_qkv.astype(jnp.float32), grad_qkv, first_qkv, second_qkv, DECAY_RATE
    )
    firsts_out, seconds_out, update_out = adam_step(
        w_out.astype(jnp.float32), grad_out, first_out, second_out, DECAY_RATE
    )
    firsts_up, seconds_up, update_up = adam_step(
        w_up.astype(jnp.float32), grad_up, first_up, second_up, DECAY_RATE
    )
    firsts_down, seconds_down, update_down = adam_step(
        w_down.astype(jnp.float32), grad_down, first_down, second_down, DECAY_RATE
    )
    firsts_vectors, seconds_vectors, update_vectors = adam_step(
        vectors.astype(jnp.float32), grad_vectors, first_vectors, second_vectors, 0.0
    )
    firsts_relative, seconds_relative, update_relative = adam_step(
        relative, grad_relative, first_relative, second_relative, 0.0
    )
    return (
        layer_out.astype(jnp.bfloat16)[None],
        in_grad[None],
        grad_qkv,
        firsts_qkv,
        seconds_qkv,
        update_qkv,
        grad_out,
        firsts_out,
        seconds_out,
        update_out,
        grad_up,
        firsts_up,
        seconds_up,
        update_up,
        grad_down,
        firsts_down,
        seconds_down,
        update_down,
        grad_vectors,
        firsts_vectors,
        seconds_vectors,
        update_vectors,
        grad_relative,
        firsts_relative,
        seconds_relative,
        update_relative,
    )


def solution(mesh):
    kernels = mesh.shape["regions"] == PEERS and mesh.shape["shard"] == 2
    return jax.shard_map(
        functools.partial(per_device, kernels),
        mesh=mesh,
        in_specs=(
            P("shard", "regions", None),
            P("shard", "regions", None),
            P(("regions", "shard"), None),
            P(("regions", "shard"), None),
            P(("regions", "shard"), None),
            P(("regions", "shard"), None),
            P(None, ("regions", "shard")),
            P(),
            P(("regions", "shard"), None),
            P(("regions", "shard"), None),
            P(("regions", "shard"), None),
            P(("regions", "shard"), None),
            P(("regions", "shard"), None),
            P(("regions", "shard"), None),
            P(("regions", "shard"), None),
            P(("regions", "shard"), None),
            P(None, ("regions", "shard")),
            P(None, ("regions", "shard")),
            P(),
            P(),
            P("shard", "regions"),
            P("shard", "regions"),
            P("shard", "regions"),
            P("shard", "regions"),
        ),
        out_specs=(
            P("shard", "regions", None),
            P("shard", "regions", None),
            P(("regions", "shard"), None),
            P(("regions", "shard"), None),
            P(("regions", "shard"), None),
            P(("regions", "shard"), None),
            P(("regions", "shard"), None),
            P(("regions", "shard"), None),
            P(("regions", "shard"), None),
            P(("regions", "shard"), None),
            P(("regions", "shard"), None),
            P(("regions", "shard"), None),
            P(("regions", "shard"), None),
            P(("regions", "shard"), None),
            P(("regions", "shard"), None),
            P(("regions", "shard"), None),
            P(("regions", "shard"), None),
            P(("regions", "shard"), None),
            P(None, ("regions", "shard")),
            P(None, ("regions", "shard")),
            P(None, ("regions", "shard")),
            P(None, ("regions", "shard")),
            P(),
            P(),
            P(),
            P(),
        ),
        check_vma=False,
    )
```

```python
import jax
import jax.numpy as jnp
import numpy as np
from jax import lax
from jax.experimental import pallas as pl
from jax.experimental.pallas import tpu as pltpu
from jax.sharding import PartitionSpec as P

HEADS = 12
HEAD = 64
PAGE = 576


PRECISE = lax.Precision.HIGHEST
EPS_NORM = 1e-05
BETA_ONE = 0.9
BETA_TWO = 0.999
ADAM_EPS = 1e-08
LAYER_FACTOR = 0.5625
DECAY_RATE = 0.05
STEP_COUNT = 10.0


def skewed(line, size):
    count = line.shape[0]
    wide = jnp.pad(line, ((0, 0), (0, 1)))
    flat = jnp.broadcast_to(wide[:, None, :], (count, size, 2 * size)).reshape(count, -1)
    rows = flat[:, : size * (2 * size - 1)].reshape(count, size, 2 * size - 1)
    return rows[:, :, size - 1 :]


def bias_table(relative):
    seq = skewed(relative[:, :127], 64)
    horizontal = skewed(relative[:, 127:190], 32)
    vertical = skewed(relative[:, 190:253], 32)
    return (
        jnp.pad(seq, ((0, 0), (0, 64), (0, 64)))
        + jnp.pad(horizontal, ((0, 0), (64, 32), (64, 32)))
        + jnp.pad(vertical, ((0, 0), (96, 0), (96, 0)))
    )


def position_codes(box_x, box_y):
    places = jnp.arange(PAGE, dtype=jnp.int32)
    seq_bucket = places * 64 // PAGE
    columns = jnp.arange(128, dtype=jnp.int32)
    matched = (
        (columns[None, None, :] == seq_bucket[None, :, None])
        | (columns == 64 + box_x[..., None])
        | (columns == 96 + box_y[..., None])
    )
    return matched.astype(jnp.float32)


def layout_bias(code_rows, bias_mats):
    lifted = jnp.einsum("pa,hab->hpb", code_rows, bias_mats, precision=PRECISE)
    return jnp.einsum("hpb,qb->hpq", lifted, code_rows, precision=PRECISE)


def page_scores(page_qkv, code_rows, bias_mats):
    parted = page_qkv.reshape(PAGE, 3, HEADS, HEAD)
    queries = parted[:, 0]
    key_rows = parted[:, 1]
    values = parted[:, 2]
    scores = jnp.einsum(
        "phd,qhd->hpq", queries, key_rows, preferred_element_type=jnp.float32
    ) * 0.125 + layout_bias(code_rows, bias_mats)
    return (queries, key_rows, values, scores)


def page_forward(page_qkv, code_rows, bias_mats):
    queries, key_rows, values, scores = page_scores(page_qkv, code_rows, bias_mats)
    row_max = jnp.max(scores, axis=2, keepdims=True)
    raised = jnp.exp(scores - row_max)
    totals = jnp.sum(raised, axis=2, keepdims=True)
    attn_w = (raised / totals).astype(jnp.bfloat16)
    context = jnp.einsum("hpq,qhd->phd", attn_w, values, preferred_element_type=jnp.float32)
    log_total = (row_max + jnp.log(totals))[..., 0]
    return (context.reshape(PAGE, HEADS * HEAD).astype(jnp.bfloat16), log_total)


def page_backward(page_qkv, code_rows, log_total, grad_ctx, bias_mats):
    queries, key_rows, values, scores = page_scores(page_qkv, code_rows, bias_mats)
    chances = jnp.exp(scores - log_total[..., None])
    attn_w = chances.astype(jnp.bfloat16)
    grad_heads = grad_ctx.reshape(PAGE, HEADS, HEAD)
    grad_values = jnp.einsum("hpq,phd->qhd", attn_w, grad_heads, preferred_element_type=jnp.float32)
    grad_chances = jnp.einsum(
        "phd,qhd->hpq", grad_heads, values, preferred_element_type=jnp.float32
    )
    inner = jnp.sum(chances * grad_chances, axis=2, keepdims=True)
    grad_scores = (chances * (grad_chances - inner)).astype(jnp.bfloat16)
    grad_queries = (
        jnp.einsum("hpq,qhd->phd", grad_scores, key_rows, preferred_element_type=jnp.float32)
        * 0.125
    )
    grad_keys = (
        jnp.einsum("hpq,phd->qhd", grad_scores, queries, preferred_element_type=jnp.float32) * 0.125
    )
    partial_codes = jnp.einsum(
        "hpq,qb->hpb",
        grad_scores,
        code_rows.astype(jnp.bfloat16),
        preferred_element_type=jnp.float32,
    )
    grad_mats = jnp.einsum("pa,hpb->hab", code_rows, partial_codes, precision=PRECISE)
    grad_page = jnp.stack([grad_queries, grad_keys, grad_values], axis=1).reshape(
        PAGE, 3 * HEADS * HEAD
    )
    return (grad_page.astype(jnp.bfloat16), grad_mats)


def exchange(rows, targets, picks, groups, slot_cap):
    slots = groups * slot_cap
    places = jnp.arange(slots, dtype=jnp.int32)
    packing = (places[:, None] == targets[None, :]).astype(jnp.bfloat16)
    packed = jnp.dot(packing, rows, preferred_element_type=jnp.float32).astype(jnp.bfloat16)
    arrived = lax.all_to_all(
        packed.reshape(groups, slot_cap, rows.shape[1]),
        "regions",
        split_axis=0,
        concat_axis=0,
        tiled=True,
    ).reshape(slots, rows.shape[1])
    picking = (picks[:, None] == places[None, :]).astype(jnp.bfloat16)
    return jnp.dot(picking, arrived, preferred_element_type=jnp.float32)


def norm_forward(rows, gain, shift):
    centre = rows - jnp.mean(rows, axis=-1, keepdims=True)
    spread = lax.rsqrt(jnp.mean(centre * centre, axis=-1, keepdims=True) + EPS_NORM)
    normed = centre * spread
    return (normed * gain + shift, normed, spread)


def norm_back(incoming, normed, spread, gain):
    scaled = incoming * gain
    grad_rows = spread * (
        scaled
        - jnp.mean(scaled, axis=-1, keepdims=True)
        - normed * jnp.mean(scaled * normed, axis=-1, keepdims=True)
    )
    return (grad_rows, jnp.sum(incoming * normed, axis=0), jnp.sum(incoming, axis=0))


def adam_step(param, grad, moment, square, decay):
    moment_new = BETA_ONE * moment + (1.0 - BETA_ONE) * grad
    square_new = BETA_TWO * square + (1.0 - BETA_TWO) * grad * grad
    moment_hat = moment_new / (1.0 - BETA_ONE**STEP_COUNT)
    square_hat = square_new / (1.0 - BETA_TWO**STEP_COUNT)
    update = LAYER_FACTOR * (moment_hat / (jnp.sqrt(square_hat) + ADAM_EPS) + decay * param)
    return (moment_new, square_new, update)


ROWS = 576


def softly(scores, axis):
    peak = jnp.max(scores, axis=axis, keepdims=True)
    raised = jnp.exp(scores - peak)
    return raised * (1.0 / jnp.sum(raised, axis=axis, keepdims=True))


def head_lift(tables, codes, h):
    lines = tables[h]
    lane = lax.broadcasted_iota(jnp.int32, (64, 128), 1)

    def spread(n, size, low, high):
        line = jnp.broadcast_to(lines[n : n + 1], (size, 128))
        turned = pltpu.roll(line, 0, 1, stride=1, stride_axis=0)
        return jnp.where((lane[:size] >= low) & (lane[:size] < high), turned, 0.0)

    table = jnp.concatenate(
        [spread(0, 64, 0, 64), spread(1, 32, 64, 96), spread(2, 32, 96, 128)], axis=0
    )
    high = table.astype(jnp.bfloat16)
    low = (table - high.astype(jnp.float32)).astype(jnp.bfloat16)
    both = jnp.concatenate([high, low], axis=1)
    return jnp.dot(codes, both, preferred_element_type=jnp.float32).astype(jnp.bfloat16)


def lane_mask(rows, h):
    lane = lax.broadcasted_iota(jnp.int32, (rows, 128), 1)
    return (lane < 64) if h == 0 else (lane >= 64)


def pair_columns(qkv, pair):
    width = qkv.shape[1] // 3
    at = [pl.multiple_of(n * width + pair * 128, 128) for n in range(3)]
    return [qkv[:, pl.ds(a, 128)] for a in at]


NT = (((1,), (1,)), ((), ()))
TN = (((0,), (0,)), ((), ()))


def attend_pair(pair, qkv, tables, codes_ref, context):
    count = qkv.shape[0]
    codes = codes_ref[...]
    queries, keys, values = pair_columns(qkv, pair)
    right = jnp.concatenate([keys, codes, codes], axis=1)
    scaled = queries * jnp.bfloat16(0.125)
    results = []
    for h in range(2):
        mine = jnp.where(lane_mask(count, h), scaled, jnp.zeros_like(scaled))
        left = jnp.concatenate([mine, head_lift(tables, codes, 2 * pair + h)], axis=1)
        parts = []
        for r in range(0, count, ROWS):
            scores = lax.dot_general(left[r : r + ROWS], right, NT, preferred_element_type=jnp.float32)
            weights = softly(scores, 1).astype(jnp.bfloat16)
            parts.append(jnp.dot(weights, values, preferred_element_type=jnp.float32))
        results.append(parts)
    for n, r in enumerate(range(0, count, ROWS)):
        both = jnp.where(lane_mask(ROWS, 0), results[0][n], results[1][n])
        context[pl.ds(r, ROWS), pl.ds(pl.multiple_of(pair * 128, 128), 128)] = both.astype(jnp.bfloat16)


def attend_pair_back(pair, qkv, grad_ref, tables, codes_ref, flipped_ref, grad_qkv, grad_tables):
    count = qkv.shape[0]
    width = qkv.shape[1] // 3
    codes = codes_ref[...]
    queries, keys, values = pair_columns(qkv, pair)
    grads = grad_ref[:, pl.ds(pl.multiple_of(pair * 128, 128), 128)]
    left = jnp.concatenate([keys, codes, codes], axis=1)
    near = jnp.concatenate([keys, codes], axis=1)
    scaled = queries * jnp.bfloat16(0.125)
    out_q, out_k, out_v = [], [], []
    for h in range(2):
        mask = lane_mask(count, h)
        mine = jnp.where(mask, scaled, jnp.zeros_like(scaled))
        mine_grad = jnp.where(mask, grads, jnp.zeros_like(grads))
        right = jnp.concatenate([mine, head_lift(tables, codes, 2 * pair + h)], axis=1)
        total = None
        k_parts, v_parts = [], []
        if True:
            scores = lax.dot_general(left, right, NT, preferred_element_type=jnp.float32)
            chances = softly(scores, 0)
            grad_chances = lax.dot_general(values, mine_grad, NT, preferred_element_type=jnp.float32)
            inner = jnp.sum(chances * grad_chances, axis=0, keepdims=True)
            grad_scores = (chances * (grad_chances - inner)).astype(jnp.bfloat16)
            v_rows = jnp.dot(chances.astype(jnp.bfloat16), grads, preferred_element_type=jnp.float32)
            k_rows = jnp.dot(grad_scores, queries, preferred_element_type=jnp.float32)
            total = lax.dot_general(grad_scores, near, TN, preferred_element_type=jnp.float32)
        out_q.append(total[:, :128])
        out_k.append(k_rows)
        out_v.append(v_rows)
        partial = total[:, 128:]
        high = partial.astype(jnp.bfloat16)
        low = (partial - high.astype(jnp.float32)).astype(jnp.bfloat16)
        mats = lax.dot_general(
            flipped_ref[...], jnp.concatenate([high, low], axis=1), TN, preferred_element_type=jnp.float32
        )
        mats = mats[:, :128] + mats[:, 128:]
        lane = lax.broadcasted_iota(jnp.int32, (64, 128), 1)

        def gathered(row, size, low_lane, high_lane):
            part = jnp.where((lane[:size] >= low_lane) & (lane[:size] < high_lane), mats[row : row + size], 0.0)
            turned = pltpu.roll(part, 0, 1, stride=1, stride_axis=0)
            return jnp.sum(turned, axis=0, keepdims=True)

        grad_tables[2 * pair + h] = jnp.concatenate(
            [
                gathered(0, 64, 0, 64),
                gathered(64, 32, 64, 96),
                gathered(96, 32, 96, 128),
                jnp.zeros((5, 128), jnp.float32),
            ],
            axis=0,
        )
    mask = lane_mask(count, 0)
    for n, (parts, factor) in enumerate(((out_q, 0.125), (out_k, 0.125), (out_v, 1.0))):
        both = jnp.where(mask, parts[0], parts[1]) * factor
        grad_qkv[:, pl.ds(pl.multiple_of(n * width + pair * 128, 128), 128)] = both.astype(jnp.bfloat16)


def code_columns(seq, box_x, box_y):
    columns = jnp.arange(128, dtype=jnp.int32)[None]
    hit = (columns == seq[:, None]) | (columns == 64 + box_x[:, None]) | (columns == 96 + box_y[:, None])
    return hit.astype(jnp.bfloat16)


def table_lines(relative):
    seq = jnp.pad(relative[:, :127], ((0, 0), (0, 1)))
    horizontal = jnp.pad(relative[:, 127:190], ((0, 0), (0, 65)))
    vertical = jnp.pad(relative[:, 190:253], ((0, 0), (0, 65)))
    lines = [jnp.roll(seq, -63, 1), jnp.roll(horizontal, 33, 1), jnp.roll(vertical, 65, 1)]
    return jnp.pad(jnp.stack(lines, axis=1), ((0, 0), (0, 5), (0, 0)))


def lines_back(grad):
    return jnp.concatenate(
        [grad[:, 0, :127], grad[:, 1, 64:127], jnp.roll(grad[:, 2], -96, 1)[:, :63]], axis=1
    )


MESH = pl.DeviceIdType.MESH
PEERS = 16
VEC_COLS = 256


def place():
    me = lax.axis_index("regions")
    core = lax.axis_index("shard")
    z = lax.div(me, 4)
    y = lax.div(lax.rem(me, 4), 2)
    x = lax.rem(me, 2)
    return me, core, z, y, x


def enter(me, core):
    barrier = pltpu.get_barrier_semaphore()
    for k in range(1, PEERS):
        pl.semaphore_signal(barrier, inc=1, device_id=(me ^ k, core), device_id_type=MESH)
    pl.semaphore_signal(barrier, inc=1, device_id=(me, 1 - core), device_id_type=MESH)
    pl.semaphore_wait(barrier, PEERS)


def remote(src, dst, send, recv, device):
    return pltpu.make_async_remote_copy(
        src_ref=src, dst_ref=dst, send_sem=send, recv_sem=recv, device_id=device, device_id_type=MESH
    )


class Exchange:
    def __init__(self, where, packed, arrived, send, recv, local):
        self.me, self.core = where[0], where[1]
        self.packed, self.arrived = packed, arrived
        self.send, self.recv, self.local = send, recv, local
        self.slots, self.half = packed.shape[1], packed.shape[2]

    def pack(self, rows, row_of, groups=range(4)):
        self.pack_value(rows[...], row_of, groups)

    def pack_value(self, rows, row_of, groups=range(4)):
        span = 4 * self.slots
        left, right = rows[:, : self.half], rows[:, self.half :]
        shift = self.slots // 2
        for j in groups:
            group = lax.div(self.me, 4) ^ j
            at = lax.broadcasted_iota(jnp.int32, (span, rows.shape[0]), 0) + group * span
            target = row_of[...]
            lefts = jnp.where(at == target, 1.0, 0.0).astype(jnp.bfloat16)
            rights = jnp.where(at == target + shift, 1.0, 0.0).astype(jnp.bfloat16)
            block = jnp.dot(lefts, left, preferred_element_type=jnp.float32) + jnp.dot(
                rights, right, preferred_element_type=jnp.float32
            )
            self.packed[pl.ds(4 * group, 4)] = block.astype(jnp.bfloat16).reshape(4, self.slots, self.half)
            for k in range(4):
                if j + k:
                    self.copy(4 * j + k).start()
                else:
                    self.own().start()

    def copy(self, k):
        d = self.me ^ k
        return remote(
            self.packed.at[d], self.arrived.at[self.me], self.send.at[k], self.recv.at[k], (d, self.core)
        )

    def own(self):
        return pltpu.make_async_copy(self.packed.at[self.me], self.arrived.at[self.me], self.local)

    def wait(self):
        self.own().wait()

        def one(k, carry):
            self.copy(k).wait()
            return carry

        lax.fori_loop(1, PEERS, one, 0)

    def unpack(self, row_of, out, kind):
        total = PEERS * self.slots
        for part in range(2):
            wanted = row_of[...] + part * (self.slots // 2)
            at = lax.broadcasted_iota(jnp.int32, (out.shape[0], total), 1)
            picking = jnp.where(at == wanted, 1.0, 0.0).astype(jnp.bfloat16)
            got = jnp.dot(
                picking,
                self.arrived[...].reshape(total, self.half),
                preferred_element_type=jnp.float32,
            )
            out[:, part * self.half : (part + 1) * self.half] = got.astype(kind)


def pieces_of(rows, half):
    tiles = half // 128
    if rows % 64 == 0:
        cuts = [(n * rows // 4, rows // 4, 0, half) for n in range(4)]
    elif tiles < 4:
        wide = (tiles + 1) // 2 * 128
        cuts = [(0, rows, 0, wide), (0, rows, wide, half - wide)]
    else:
        ends = [0, (tiles + 3) // 4, tiles // 2, tiles - (tiles + 3) // 4, tiles]
        cuts = [(0, rows, 128 * ends[n], 128 * (ends[n + 1] - ends[n])) for n in range(4)]
    return [[(*cuts[n], True), (*cuts[n + 1], False)] for n in range(0, len(cuts), 2)]


class Gather:
    TIGHT = (0, 1, 2, 3, 4, 5, 6)
    OFFSETS = (0, 1, 2, 4, 6, 8, 10)

    def __init__(self, where, whole, piece, sems):
        self.where, self.whole, self.piece, self.sems = where, whole, piece, sems

    def part(self, z, y, x):
        core = self.where[1]
        r0, rows, c0, cols, _ = self.piece
        half = self.whole.shape[4] // 2
        at = pl.multiple_of(core * half + c0, 128)
        return self.whole.at[z, y, x, pl.ds(r0, rows), pl.ds(at, cols)]

    def along_z(self, t, upward):
        me, core, z, y, x = self.where
        step = 1 if upward else -1
        origin = z - step * t
        ref = self.part(origin, y, x)
        i = 2 * t + (1 if upward else 0)
        return remote(ref, ref, self.sems.at[0, i], self.sems.at[1, i], (me + 4 * step, core))

    def z_sends(self, t, do):
        z = self.where[2]

        @pl.when((z >= t) & (z <= 2))
        def _():
            do(self.along_z(t, True))

        @pl.when((z + t <= 3) & (z >= 1))
        def _():
            do(self.along_z(t, False))

    def z_waits(self, t):
        z = self.where[2]

        @pl.when(z - 1 - t >= 0)
        def _():
            me, core, z, y, x = self.where
            ref = self.part(z - 1 - t, y, x)
            i = 2 * t + 1
            remote(ref, ref, self.sems.at[0, i], self.sems.at[1, i], (me, 1 - core)).wait_recv()

        @pl.when(z + 1 + t <= 3)
        def _():
            me, core, z, y, x = self.where
            ref = self.part(z + 1 + t, y, x)
            i = 2 * t
            remote(ref, ref, self.sems.at[0, i], self.sems.at[1, i], (me, 1 - core)).wait_recv()

    def plane(self, n):
        me, core, z, y, x = self.where
        x_first = self.piece[4]
        every = slice(None)
        other = (me, 1 - core)
        if n == 0:
            ref, device = self.part(every, y, x), (me ^ (1 if x_first else 2), core)
        elif n == 1 and x_first:
            ref, device = self.part(every, y, every), (me ^ 2, core)
        elif n == 1:
            ref, device = self.part(every, every, x), (me ^ 1, core)
        elif n == 2:
            ref, device = self.part(every, y, x), other
        elif n == 3:
            ref, device = (self.part(every, y, 1 - x) if x_first else self.part(every, 1 - y, x)), other
        else:
            ref, device = (self.part(every, 1 - y, every) if x_first else self.part(every, every, 1 - x)), other
        return remote(ref, ref, self.sems.at[0, 6 + n], self.sems.at[1, 6 + n], device)

    def run(self, stage):
        if stage < 3:
            if stage:
                self.z_waits(stage - 1)
            self.z_sends(stage, lambda copy: copy.start())
        elif stage == 3:
            self.z_waits(2)
            self.plane(0).start()
            self.plane(2).start()
        elif stage == 4:
            self.plane(0).wait_recv()
            self.plane(1).start()
            self.plane(3).start()
        elif stage == 5:
            self.plane(1).wait_recv()
            self.plane(4).start()
        else:
            for n in (2, 3, 4):
                self.plane(n).wait_recv()

    def sent(self):
        for t in range(3):
            self.z_sends(t, lambda copy: copy.wait_send())
        for n in range(5):
            self.plane(n).wait_send()


class Scatter:
    OFFSETS = (0, 2, 4, 6, 8, 10, 12)

    def __init__(self, where, local, sums, from_core, from_near, from_far, from_z, fetch, piece, sems):
        self.where, self.local, self.sums, self.piece, self.sems = where, local, sums, piece, sems
        self.from_core, self.from_near, self.from_far, self.from_z = from_core, from_near, from_far, from_z
        self.half, self.fetch = sums.shape[4], fetch

    def cut(self, ref, *lead, core=None):
        r0, rows, c0, cols, _ = self.piece
        at = c0 if core is None else pl.multiple_of(core * self.half + c0, 128)
        return ref.at[(*lead, pl.ds(r0, rows), pl.ds(at, cols))]

    def between_cores(self):
        me, core = self.where[0], self.where[1]
        every = slice(None)
        src = self.cut(self.local, every, every, every, core=1 - core)
        dst = self.cut(self.from_core, every, every, every)
        return remote(src, dst, self.sems.at[0, 0], self.sems.at[1, 0], (me, 1 - core))

    def own_half(self):
        every = slice(None)
        src = self.cut(self.local, every, every, every, core=self.where[1])
        return pltpu.make_async_copy(src, self.cut(self.sums, every, every, every), self.fetch)

    def near(self):
        me, core, z, y, x = self.where
        every = slice(None)
        if self.piece[4]:
            src, device = self.cut(self.sums, every, 1 - y, every), (me ^ 2, core)
        else:
            src, device = self.cut(self.sums, every, every, 1 - x), (me ^ 1, core)
        dst = self.cut(self.from_near, every, every)
        return remote(src, dst, self.sems.at[0, 1], self.sems.at[1, 1], device)

    def far(self):
        me, core, z, y, x = self.where
        every = slice(None)
        if self.piece[4]:
            src, device = self.cut(self.sums, every, y, 1 - x), (me ^ 1, core)
        else:
            src, device = self.cut(self.sums, every, 1 - y, x), (me ^ 2, core)
        dst = self.cut(self.from_far, every)
        return remote(src, dst, self.sems.at[0, 2], self.sems.at[1, 2], device)

    def along_z(self, sender, upward):
        me, core, z, y, x = self.where
        lead = pl.ds(sender + 1, 3 - sender) if upward else pl.ds(0, sender)
        src = self.cut(self.sums, lead, y, x)
        dst = self.cut(self.from_z, 1 if upward else 0, lead)
        i = 3 + (1 if upward else 0)
        step = 4 if upward else -4
        return remote(src, dst, self.sems.at[0, i], self.sems.at[1, i], (me + step, core))

    def add(self, target, other):
        total = target[...].astype(jnp.float32) + other[...].astype(jnp.float32)
        target[...] = total.astype(jnp.bfloat16)

    def z_got(self, sender, upward):
        me, core, z, y, x = self.where
        self.along_z(sender, upward).wait_recv()
        for d in range(sender + 1, 4) if upward else range(sender):
            self.add(self.cut(self.sums, d, y, x), self.cut(self.from_z, 1 if upward else 0, d))

    def run(self, stage):
        me, core, z, y, x = self.where
        if stage == 0:
            self.between_cores().start()
            self.own_half().start()
        elif stage == 1:
            self.own_half().wait()
            self.between_cores().wait_recv()

            def one(i, carry):
                a, b, c = lax.div(i, 4), lax.div(lax.rem(i, 4), 2), lax.rem(i, 2)
                self.add(self.cut(self.sums, a, b, c), self.cut(self.from_core, a, b, c))
                return carry

            lax.fori_loop(0, 16, one, 0)
            self.near().start()
        elif stage == 2:
            self.near().wait_recv()

            def one(i, carry):
                a, b = lax.div(i, 2), lax.rem(i, 2)
                target = self.cut(self.sums, a, y, b) if self.piece[4] else self.cut(self.sums, a, b, x)
                self.add(target, self.cut(self.from_near, a, b))
                return carry

            lax.fori_loop(0, 8, one, 0)
            self.far().start()
        elif stage == 3:
            self.far().wait_recv()

            def one(i, carry):
                self.add(self.cut(self.sums, i, y, x), self.cut(self.from_far, i))
                return carry

            lax.fori_loop(0, 4, one, 0)

            @pl.when(z == 3)
            def _():
                self.along_z(3, False).start()

            @pl.when(z == 0)
            def _():
                self.along_z(0, True).start()

        elif stage == 4:

            @pl.when(z == 2)
            def _():
                self.z_got(3, False)
                self.along_z(2, False).start()

            @pl.when(z == 1)
            def _():
                self.z_got(0, True)
                self.along_z(1, True).start()

        elif stage == 5:

            @pl.when(z == 1)
            def _():
                self.z_got(2, False)
                self.along_z(1, False).start()

            @pl.when(z == 2)
            def _():
                self.z_got(1, True)
                self.along_z(2, True).start()

        elif stage == 6:

            @pl.when(z == 0)
            def _():
                self.z_got(1, False)

            @pl.when(z == 3)
            def _():
                self.z_got(2, True)

    def sent(self):
        z = self.where[2]
        self.between_cores().wait_send()
        self.near().wait_send()
        self.far().wait_send()
        for sender in range(4):

            @pl.when(z == sender)
            def _(sender=sender):
                if sender > 0:
                    self.along_z(sender, False).wait_send()
                if sender < 3:
                    self.along_z(sender, True).wait_send()


def stepper(tasks):
    def step(k):
        for pair, first, offsets in tasks:
            if k - first in offsets:
                for task in pair:
                    task.run(offsets.index(k - first))

    return step, max(first + offsets[-1] for _, first, offsets in tasks) + 1


PAIRS = 6
READY = 8


def inbound_kernel(
    rows_ref, grad_ref, slot_line, home_column, tables, codes, s_qkv, s_out, s_up, s_down,
    homed, cotangent, qkv, context, vec_rows, w_qkv, w_out, w_up, w_down,
    packed_a, arrived_a, packed_b, arrived_b, p_qkv, p_out, p_up, p_down, b_qkv, b_out, b_up, b_down,
    send_a, recv_a, send_b, recv_b, local_sems, pair_sems, block_sems, piece_sems,
):
    where = place()
    me, core, z, y, x = where
    enter(me, core)
    shards = (s_qkv, s_out, s_up, s_down)
    others = (p_qkv, p_out, p_up, p_down)
    blocks = (b_qkv, b_out, b_up, b_down)
    wholes = (w_qkv, w_out, w_up, w_down)
    pairs = [
        remote(shards[i].at[1 - core], others[i], pair_sems.at[0, i], pair_sems.at[1, i], (me, 1 - core))
        for i in range(4)
    ]
    for pair in pairs:
        pair.start()
    moved = Exchange(where, packed_a, arrived_a, send_a, recv_a, local_sems.at[0])
    moved_grad = Exchange(where, packed_b, arrived_b, send_b, recv_b, local_sems.at[1])
    placed = []
    tasks = []
    for i in range(4):
        pairs[i].wait_recv()
        half = blocks[i].shape[1]
        rows = blocks[i].shape[0] // 2
        mine = shards[i][core][:rows].astype(jnp.float32)
        other = others[i][:rows].astype(jnp.float32)
        first = jnp.where(core == 0, mine, other)
        second = jnp.where(core == 0, other, mine)
        blocks[i][...] = jnp.concatenate([first, second], axis=0).astype(jnp.bfloat16)
        at = pl.multiple_of(core * half, 128)
        copy = pltpu.make_async_copy(
            blocks[i], wholes[i].at[z, y, x, :, pl.ds(at, half)], block_sems.at[i]
        )
        copy.start()
        placed.append(copy)
    for i in range(4):
        placed[i].wait()
        for pair in pieces_of(blocks[i].shape[0], blocks[i].shape[1]):
            n = len(tasks)
            pair = [Gather(where, wholes[i], piece, piece_sems.at[2 * n + j]) for j, piece in enumerate(pair)]
            tasks.append((pair, n, Gather.TIGHT if i == 0 else Gather.OFFSETS))
    step, steps = stepper(tasks)

    step(0)
    moved.pack(rows_ref, slot_line)
    for k in range(1, READY):
        step(k)
    moved.wait()
    moved.unpack(home_column, homed, jnp.bfloat16)
    moved_grad.pack(grad_ref, slot_line)
    width = homed.shape[1]
    columns = w_qkv[:, :, :, :, 3 * width : 3 * width + 128].reshape(width, 128)
    vec_rows[...] = columns.astype(jnp.float32).T[: vec_rows.shape[0]]
    for n in range(3):
        part = w_qkv[:, :, :, :, n * width : (n + 1) * width].reshape(width, width)
        projected = jnp.dot(homed[...], part, preferred_element_type=jnp.float32)
        if n != 1:
            projected = projected + vec_rows[n // 2 : n // 2 + 1]
        qkv[:, n * width : (n + 1) * width] = projected.astype(jnp.bfloat16)

    def one(pair, carry):
        attend_pair(pair, qkv, tables, codes, context)
        for j in range(PAIRS):

            @pl.when(pair == j)
            def _(j=j):
                step(READY + j)

        return carry

    lax.fori_loop(0, PAIRS, one, 0)
    for k in range(READY + PAIRS, steps):
        step(k)
    moved_grad.wait()
    moved_grad.unpack(home_column, cotangent, jnp.bfloat16)
    for pair in pairs:
        pair.wait_send()
    for pair, _, _ in tasks:
        for task in pair:
            task.sent()


def vmem(count):
    return [pl.BlockSpec(memory_space=pltpu.VMEM)] * count


def inbound(rows, grads, slot_line, home_column, tables, codes, shards):
    tokens, width = rows.shape
    slots = 2 * (2 * tokens // PEERS)
    low = jnp.bfloat16
    buffer = pltpu.VMEM((PEERS, slots, width // 2), low)
    wholes, pair_shapes, block_shapes = [], [], []
    for shard, padded in shards:
        half = padded.shape[2]
        wholes.append(jax.ShapeDtypeStruct((4, 2, 2, 2 * shard, 2 * half), low))
        pair_shapes.append(pltpu.VMEM(padded.shape[1:], low))
        block_shapes.append(pltpu.VMEM((2 * shard, half), low))
    dma = pltpu.SemaphoreType.DMA
    return pl.pallas_call(
        inbound_kernel,
        out_shape=[
            jax.ShapeDtypeStruct((tokens, width), low),
            jax.ShapeDtypeStruct((tokens, width), low),
            jax.ShapeDtypeStruct((tokens, 3 * width), low),
            jax.ShapeDtypeStruct((tokens, width), low),
            jax.ShapeDtypeStruct((16, width), jnp.float32),
        ]
        + wholes,
        in_specs=vmem(10),
        out_specs=vmem(9),
        scratch_shapes=[buffer] * 4 + pair_shapes + block_shapes
        + [dma((PEERS,)), dma((PEERS,)), dma((PEERS,)), dma((PEERS,)), dma((2,)), dma((2, 4)), dma((4,)), dma((14, 2, 11))],
        compiler_params=pltpu.CompilerParams(
            collective_id=1, has_side_effects=True, vmem_limit_bytes=60 << 20
        ),
        name="inbound",
    )(rows, grads, slot_line, home_column, tables, codes, *[padded for _, padded in shards])


def normed_rows(rows):
    centre = rows - jnp.mean(rows, axis=-1, keepdims=True)
    spread = lax.rsqrt(jnp.mean(centre * centre, axis=-1, keepdims=True) + EPS_NORM)
    return centre * spread, spread


def dense_kernel(
    homed, cotangent, context, vec, w_out, w_up, w_down,
    result, grad_one_ref, grad_context, g_out, g_up, g_down, vec_grads,
    act, slope, hidden_low,
):
    width = homed.shape[1]
    chunks = w_up.shape[4] // width
    f32 = jnp.float32
    low = jnp.bfloat16

    def columns(ref, c):
        return ref[:, :, :, :, c * width : (c + 1) * width].reshape(width, width)

    def keep(n, line):
        vec_grads[n : n + 1] = jnp.sum(line, axis=0, keepdims=True)

    attn_out = jnp.dot(context[...], columns(w_out, 0), preferred_element_type=f32) + vec[2:3]
    normed_one, spread_one = normed_rows(homed[...].astype(f32) + attn_out)
    hidden = normed_one * vec[3:4] + vec[4:5]
    hidden_low[...] = hidden.astype(low)
    branch = None
    for c in range(chunks):
        pre = jnp.dot(hidden_low[...], columns(w_up, c), preferred_element_type=f32) + vec[8 + c : 9 + c]
        below = 0.5 * (1.0 + lax.erf(pre * 0.7071067811865476))
        act[c] = (pre * below).astype(low)
        slope[c] = below + pre * (jnp.exp(-0.5 * pre * pre) * 0.3989422804014327)
        part = jnp.dot(act[c], w_down[c].reshape(width, width), preferred_element_type=f32)
        branch = part if branch is None else branch + part
    normed_two, spread_two = normed_rows(hidden + branch + vec[5:6])
    result[...] = (normed_two * vec[6:7] + vec[7:8]).astype(low)

    def back(e, normed, spread, gain):
        scaled = e * gain
        return spread * (
            scaled
            - jnp.mean(scaled, axis=-1, keepdims=True)
            - normed * jnp.mean(scaled * normed, axis=-1, keepdims=True)
        )

    e = cotangent[...].astype(f32)
    keep(6, e * normed_two)
    keep(7, e)
    grad_two = back(e, normed_two, spread_two, vec[6:7])
    grad_branch = grad_two.astype(low)
    keep(5, grad_branch.astype(f32))
    grad_hidden = grad_two
    for c in range(chunks):
        g_down[c] = (
            lax.dot_general(act[c], grad_branch, TN, preferred_element_type=f32)
            .astype(low)
            .reshape(g_down.shape[1:])
        )
        grad_act = lax.dot_general(
            grad_branch, w_down[c].reshape(width, width), NT, preferred_element_type=f32
        )
        grad_pre = (grad_act * slope[c]).astype(low)
        keep(8 + c, grad_pre.astype(f32))
        g_up[:, :, :, :, c * width : (c + 1) * width] = (
            lax.dot_general(hidden_low[...], grad_pre, TN, preferred_element_type=f32)
            .astype(low)
            .reshape(*g_up.shape[:4], width)
        )
        grad_hidden = grad_hidden + lax.dot_general(
            grad_pre, columns(w_up, c), NT, preferred_element_type=f32
        )
    keep(3, grad_hidden * normed_one)
    keep(4, grad_hidden)
    grad_one = back(grad_hidden, normed_one, spread_one, vec[3:4])
    grad_one_ref[...] = grad_one
    grad_attn = grad_one.astype(low)
    keep(2, grad_attn.astype(f32))
    g_out[...] = (
        lax.dot_general(context[...], grad_attn, TN, preferred_element_type=f32)
        .astype(low)
        .reshape(g_out.shape)
    )
    grad_context[...] = lax.dot_general(
        grad_attn, columns(w_out, 0), NT, preferred_element_type=f32
    ).astype(low)
    vec_grads[0:2] = jnp.zeros((2, width), f32)
    vec_grads[12:] = jnp.zeros((vec_grads.shape[0] - 12, width), f32)


def dense(homed, cotangent, context, vec, w_out, w_up, w_down):
    tokens, width = homed.shape
    chunks = w_up.shape[4] // width
    low = jnp.bfloat16
    row_shape = jax.ShapeDtypeStruct((tokens, width), low)
    return pl.pallas_call(
        dense_kernel,
        out_shape=[row_shape, jax.ShapeDtypeStruct((tokens, width), jnp.float32), row_shape]
        + [jax.ShapeDtypeStruct(w.shape, low) for w in (w_out, w_up, w_down)]
        + [jax.ShapeDtypeStruct((128, width), jnp.float32)],
        in_specs=vmem(7),
        out_specs=vmem(7),
        scratch_shapes=[
            pltpu.VMEM((chunks, tokens, width), low),
            pltpu.VMEM((chunks, tokens, width), jnp.float32),
            pltpu.VMEM((tokens, width), low),
        ],
        compiler_params=pltpu.CompilerParams(vmem_limit_bytes=60 << 20),
        name="dense",
    )(homed, cotangent, context, vec, w_out, w_up, w_down)


LAST = 13


def outbound_kernel(
    result_ref, grad_one, qkv, grad_context, homed, vec_grads, home_line, slot_column, tables, codes, flipped,
    w_qkv, g_out, g_up, g_down,
    result_out, grad_out, table_out, o_qkv, o_out, o_up, o_down,
    packed, arrived_a, arrived_b, table_got, grad_qkv, g_qkv,
    t_qkv, t_out, t_up, t_down, c_qkv, c_out, c_up, c_down, n_qkv, n_out, n_up, n_down,
    f_qkv, f_out, f_up, f_down, z_qkv, z_out, z_up, z_down, e_qkv, e_out, e_up, e_down,
    send_a, recv_a, send_b, recv_b, local_sems, table_sems, piece_sems, fetch_sems, last_sems,
):
    where = place()
    me, core, z, y, x = where
    enter(me, core)
    local = (g_qkv, g_out, g_up, g_down)
    sums = (t_qkv, t_out, t_up, t_down)
    from_core = (c_qkv, c_out, c_up, c_down)
    from_near = (n_qkv, n_out, n_up, n_down)
    from_far = (f_qkv, f_out, f_up, f_down)
    from_z = (z_qkv, z_out, z_up, z_down)
    ends = (e_qkv, e_out, e_up, e_down)
    outs = (o_qkv, o_out, o_up, o_down)
    low = jnp.bfloat16
    tasks = []
    for i in (3, 2, 1, 0):
        refs = (local[i], sums[i], from_core[i], from_near[i], from_far[i], from_z[i])
        for pair in pieces_of(sums[i].shape[3], sums[i].shape[4]):
            n = len(tasks)
            pair = [
                Scatter(where, *refs, fetch_sems.at[2 * n + j], piece, piece_sems.at[2 * n + j])
                for j, piece in enumerate(pair)
            ]
            tasks.append((pair, n if i else LAST + n - 5, Scatter.OFFSETS))
    step, steps = stepper(tasks)
    moved = Exchange(where, packed, arrived_a, send_a, recv_a, local_sems.at[0])
    moved_grad = Exchange(where, packed, arrived_b, send_b, recv_b, local_sems.at[1])
    devices = [(me, 1 - core), (me ^ 1, core), (me ^ 2, core), (me ^ 4, core), (me ^ 8, core)]
    shares = [
        remote(table_got.at[0, n], table_got.at[1, n], table_sems.at[0, n], table_sems.at[1, n], device)
        for n, device in enumerate(devices)
    ]

    step(0)
    moved.pack(result_ref, home_line)

    def one(pair, carry):
        attend_pair_back(pair, qkv, grad_context, tables, codes, flipped, grad_qkv, table_out)
        for j in range(PAIRS):

            @pl.when(pair == j)
            def _(j=j):
                step(1 + 2 * j)
                step(2 + 2 * j)

        return carry

    lax.fori_loop(0, PAIRS, one, 0)
    width = homed.shape[1]
    sums_of = []
    in_home = grad_one[...]
    for n in range(3):
        part = grad_qkv[:, n * width : (n + 1) * width]
        g_qkv[:, :, :, :, n * width : (n + 1) * width] = (
            lax.dot_general(homed[...], part, TN, preferred_element_type=jnp.float32)
            .astype(low)
            .reshape(*g_qkv.shape[:4], width)
        )
        sums_of.append(jnp.sum(part.astype(jnp.float32), axis=0, keepdims=True))
        weights = w_qkv[:, :, :, :, n * width : (n + 1) * width].reshape(width, width)
        in_home = in_home + lax.dot_general(part, weights, NT, preferred_element_type=jnp.float32)
    row = lax.broadcasted_iota(jnp.int32, (128, width), 0)
    lines = jnp.where(row == 0, sums_of[0], jnp.where(row == 1, sums_of[2], vec_grads[...]))
    beside = lines.T.astype(low).reshape(*g_qkv.shape[:4], 128)
    g_qkv[:, :, :, :, 3 * width : 3 * width + 128] = beside
    g_qkv[:, :, :, :, 3 * width + 128 :] = jnp.zeros_like(beside)
    step(LAST)
    moved.wait()
    moved_grad.pack_value(in_home.astype(low), home_line)
    moved.unpack(slot_column, result_out, low)
    for k in range(LAST + 1, steps):
        step(k)
        n = k - LAST - 1
        if 0 < n <= 5:
            shares[n - 1].wait_recv()
            table_out[...] += table_got[1, n - 1]
        if n < 5:
            table_got[0, n] = table_out[...]
            shares[n].start()
    finals = []
    for i in (3, 2, 1, 0):
        block = sums[i][z, y, x].astype(jnp.float32)
        rows = block.shape[0] // 2
        ends[i][0] = block[:rows]
        ends[i][1] = block[rows:]
        outs[i][core] = ends[i][core]
        copy = remote(ends[i].at[1 - core], outs[i].at[core], last_sems.at[0, i], last_sems.at[1, i], (me, 1 - core))
        copy.start()
        finals.append(copy)
    moved_grad.wait()
    moved_grad.unpack(slot_column, grad_out, jnp.float32)
    for copy in finals:
        copy.wait()
    for share in shares:
        share.wait_send()
    for pair, _, _ in tasks:
        for task in pair:
            task.sent()


def outbound(result, grad_one, qkv, grad_context, homed, vec_grads, home_line, slot_column, tables, codes, flipped, w_qkv, locals_):
    tokens, width = result.shape
    slots = 2 * (2 * tokens // PEERS)
    low = jnp.bfloat16
    buffer = pltpu.VMEM((PEERS, slots, width // 2), low)
    halves = [(g.shape[3], g.shape[4] // 2) for g in (w_qkv, *locals_)]
    scratch = (
        [buffer] * 3
        + [pltpu.VMEM((2, 5, *tables.shape), jnp.float32)]
        + [pltpu.VMEM(qkv.shape, low), pltpu.VMEM(w_qkv.shape, low)]
        + [pltpu.VMEM((4, 2, 2, r, h), low) for r, h in halves]
        + [pltpu.VMEM((4, 2, 2, r, h), low) for r, h in halves]
        + [pltpu.VMEM((4, 2, r, h), low) for r, h in halves]
        + [pltpu.VMEM((4, r, h), low) for r, h in halves]
        + [pltpu.VMEM((2, 4, r, h), low) for r, h in halves]
        + [pltpu.VMEM((2, r // 2, h), jnp.float32) for r, h in halves]
    )
    dma = pltpu.SemaphoreType.DMA
    return pl.pallas_call(
        outbound_kernel,
        out_shape=[
            jax.ShapeDtypeStruct(result.shape, low),
            jax.ShapeDtypeStruct(result.shape, jnp.float32),
            jax.ShapeDtypeStruct(tables.shape, jnp.float32),
        ]
        + [jax.ShapeDtypeStruct((2, r // 2, h), jnp.float32) for r, h in halves],
        in_specs=vmem(12) + [pl.BlockSpec(memory_space=pl.ANY)] * 3,
        out_specs=vmem(7),
        scratch_shapes=scratch
        + [dma((PEERS,)), dma((PEERS,)), dma((PEERS,)), dma((PEERS,)), dma((2,)), dma((2, 5)), dma((14, 2, 5)), dma((14,)), dma((2, 4))],
        compiler_params=pltpu.CompilerParams(
            collective_id=2, has_side_effects=True, vmem_limit_bytes=62 << 20
        ),
        name="outbound",
    )(result, grad_one, qkv, grad_context, homed, vec_grads, home_line, slot_column, tables, codes, flipped, w_qkv, *locals_)


def shard_halves(shard):
    rows, columns = shard.shape
    halves = shard.reshape(rows, 2, columns // 2).transpose(1, 0, 2)
    return (rows, jnp.pad(halves, ((0, 0), (0, -rows % 16), (0, 0))))


def joined(halves):
    return jnp.concatenate([halves[0], halves[1]], axis=1)


def per_device(
    layer_in,
    out_grad,
    w_qkv,
    w_out,
    w_up,
    w_down,
    vectors,
    relative,
    first_qkv,
    second_qkv,
    first_out,
    second_out,
    first_up,
    second_up,
    first_down,
    second_down,
    first_vectors,
    second_vectors,
    first_relative,
    second_relative,
    token_slot,
    home_index,
    box_x,
    box_y,
):
    tokens = layer_in[0]
    rows_dev, model_dim = tokens.shape
    slot_cap = 2 * rows_dev // lax.axis_size("regions")
    kinds = vectors.shape[0]
    beside = jnp.pad(vectors.T, ((0, 0), (0, VEC_COLS - kinds)))
    wide_qkv = jnp.concatenate([w_qkv, beside], axis=1)
    slot_at = token_slot[0] + slot_cap * (token_slot[0] // slot_cap)
    home_at = home_index[0] + slot_cap * (home_index[0] // slot_cap)
    bucket = jnp.arange(PAGE, dtype=jnp.int32) * 64 // PAGE
    codes = code_columns(bucket, box_x[0], box_y[0])
    flipped = code_columns(63 - bucket, 31 - box_x[0], 31 - box_y[0])
    tables = table_lines(relative)
    homed, cotangent, qkv, context, vec, whole_qkv, whole_out, whole_up, whole_down = inbound(
        tokens,
        out_grad[0],
        slot_at[None],
        home_at[:, None],
        tables,
        codes,
        [shard_halves(shard) for shard in (wide_qkv, w_out, w_up, w_down)],
    )
    result, grad_one, grad_context, local_out, local_up, local_down, vec_grads = dense(
        homed, cotangent, context, vec, whole_out, whole_up, whole_down
    )
    layer_out, in_grad, table_sum, *ends = outbound(
        result,
        grad_one,
        qkv,
        grad_context,
        homed,
        vec_grads,
        home_at[None],
        slot_at[:, None],
        tables,
        codes,
        flipped,
        whole_qkv,
        [local_out, local_up, local_down],
    )
    grad_relative = lines_back(table_sum)
    grad_qkv, grad_out, grad_up, grad_down = [joined(end) for end in ends]
    grad_vectors = grad_qkv[:, 3 * model_dim : 3 * model_dim + kinds].T
    grad_qkv = grad_qkv[:, : 3 * model_dim]
    firsts_qkv, seconds_qkv, update_qkv = adam_step(
        w_qkv.astype(jnp.float32), grad_qkv, first_qkv, second_qkv, DECAY_RATE
    )
    firsts_out, seconds_out, update_out = adam_step(
        w_out.astype(jnp.float32), grad_out, first_out, second_out, DECAY_RATE
    )
    firsts_up, seconds_up, update_up = adam_step(
        w_up.astype(jnp.float32), grad_up, first_up, second_up, DECAY_RATE
    )
    firsts_down, seconds_down, update_down = adam_step(
        w_down.astype(jnp.float32), grad_down, first_down, second_down, DECAY_RATE
    )
    firsts_vectors, seconds_vectors, update_vectors = adam_step(
        vectors.astype(jnp.float32), grad_vectors, first_vectors, second_vectors, 0.0
    )
    firsts_relative, seconds_relative, update_relative = adam_step(
        relative, grad_relative, first_relative, second_relative, 0.0
    )
    return (
        layer_out[None],
        in_grad[None],
        grad_qkv,
        firsts_qkv,
        seconds_qkv,
        update_qkv,
        grad_out,
        firsts_out,
        seconds_out,
        update_out,
        grad_up,
        firsts_up,
        seconds_up,
        update_up,
        grad_down,
        firsts_down,
        seconds_down,
        update_down,
        grad_vectors,
        firsts_vectors,
        seconds_vectors,
        update_vectors,
        grad_relative,
        firsts_relative,
        seconds_relative,
        update_relative,
    )


def spread_device(
    layer_in,
    out_grad,
    w_qkv,
    w_out,
    w_up,
    w_down,
    vectors,
    relative,
    first_qkv,
    second_qkv,
    first_out,
    second_out,
    first_up,
    second_up,
    first_down,
    second_down,
    first_vectors,
    second_vectors,
    first_relative,
    second_relative,
    token_slot,
    home_index,
    box_x,
    box_y,
):
    tokens = layer_in[0]
    rows_dev = tokens.shape[0]
    model_dim = tokens.shape[1]
    groups = lax.axis_size("regions")
    slot_cap = 2 * rows_dev // groups
    page_num = rows_dev // PAGE
    slot_of = token_slot[0]
    home_rows = home_index[0]
    full_qkv, full_out, full_up, full_down, full_vec = (
        lax.all_gather(w_qkv, ("regions", "shard"), axis=0, tiled=True),
        lax.all_gather(w_out, ("regions", "shard"), axis=0, tiled=True),
        lax.all_gather(w_up, ("regions", "shard"), axis=0, tiled=True),
        lax.all_gather(w_down, ("regions", "shard"), axis=0, tiled=True),
        lax.all_gather(vectors, ("regions", "shard"), axis=1, tiled=True),
    )
    vec_rows = full_vec.astype(jnp.float32)
    qkv_bias = jnp.concatenate([vec_rows[0], jnp.zeros_like(vec_rows[0]), vec_rows[1]])
    code_rows = position_codes(box_x[0].reshape(page_num, PAGE), box_y[0].reshape(page_num, PAGE))
    bias_mats = bias_table(relative)
    homed = exchange(tokens, slot_of, home_rows, groups, slot_cap).astype(jnp.bfloat16)
    cotangent = exchange(out_grad[0], slot_of, home_rows, groups, slot_cap)
    projected = (jnp.dot(homed, full_qkv, preferred_element_type=jnp.float32) + qkv_bias).astype(
        jnp.bfloat16
    )
    paged = projected.reshape(page_num, PAGE, 3 * model_dim)
    context_pages, log_totals = lax.map(
        lambda member: page_forward(member[0], member[1], bias_mats), (paged, code_rows)
    )
    context = context_pages.reshape(rows_dev, model_dim)
    attn_out = jnp.dot(context, full_out, preferred_element_type=jnp.float32) + vec_rows[2]
    hidden, normed_one, spread_one = norm_forward(
        homed.astype(jnp.float32) + attn_out, vec_rows[3], vec_rows[4]
    )
    hidden_low = hidden.astype(jnp.bfloat16)
    pre_act = jnp.dot(hidden_low, full_up, preferred_element_type=jnp.float32) + vec_rows[
        8:12
    ].reshape(-1)
    activated, gelu_back = jax.vjp(lambda value: jax.nn.gelu(value, approximate=False), pre_act)
    act_low = activated.astype(jnp.bfloat16)
    branch = jnp.dot(act_low, full_down, preferred_element_type=jnp.float32) + vec_rows[5]
    result, normed_two, spread_two = norm_forward(hidden + branch, vec_rows[6], vec_rows[7])
    grad_two, grad_gain_two, grad_shift_two = norm_back(
        cotangent, normed_two, spread_two, vec_rows[6]
    )
    grad_branch = grad_two.astype(jnp.bfloat16)
    grad_down = jnp.einsum("tf,td->fd", act_low, grad_branch, preferred_element_type=jnp.float32)
    grad_act = jnp.einsum("td,fd->tf", grad_branch, full_down, preferred_element_type=jnp.float32)
    grad_pre = gelu_back(grad_act)[0].astype(jnp.bfloat16)
    grad_up = jnp.einsum("td,tf->df", hidden_low, grad_pre, preferred_element_type=jnp.float32)
    grad_hidden = grad_two + jnp.einsum(
        "tf,df->td", grad_pre, full_up, preferred_element_type=jnp.float32
    )
    grad_one, grad_gain_one, grad_shift_one = norm_back(
        grad_hidden, normed_one, spread_one, vec_rows[3]
    )
    grad_attn = grad_one.astype(jnp.bfloat16)
    grad_out = jnp.einsum("td,te->de", context, grad_attn, preferred_element_type=jnp.float32)
    grad_context = jnp.einsum(
        "te,de->td", grad_attn, full_out, preferred_element_type=jnp.float32
    ).astype(jnp.bfloat16)
    grad_home = grad_context.reshape(page_num, PAGE, model_dim)
    grad_pages, mats_pages = lax.map(
        lambda member: page_backward(member[0], member[1], member[2], member[3], bias_mats),
        (paged, code_rows, log_totals, grad_home),
    )
    grad_dense = grad_pages.reshape(rows_dev, 3 * model_dim)
    bias_sums = jnp.sum(grad_dense.astype(jnp.float32), axis=0)
    grad_qkv = jnp.einsum("td,tf->df", homed, grad_dense, preferred_element_type=jnp.float32)
    in_home = grad_one + jnp.einsum(
        "tf,df->td", grad_dense, full_qkv, preferred_element_type=jnp.float32
    )
    layer_out = exchange(result.astype(jnp.bfloat16), home_rows, slot_of, groups, slot_cap)
    in_grad = exchange(in_home.astype(jnp.bfloat16), home_rows, slot_of, groups, slot_cap)
    grad_vec = jnp.concatenate(
        [
            jnp.stack(
                [
                    bias_sums[:model_dim],
                    bias_sums[2 * model_dim :],
                    jnp.sum(grad_attn.astype(jnp.float32), axis=0),
                    grad_gain_one,
                    grad_shift_one,
                    jnp.sum(grad_branch.astype(jnp.float32), axis=0),
                    grad_gain_two,
                    grad_shift_two,
                ]
            ),
            jnp.sum(grad_pre.astype(jnp.float32), axis=0).reshape(4, model_dim),
        ],
        axis=0,
    )
    grad_qkv, grad_out, grad_up, grad_down, grad_vectors = (
        lax.psum_scatter(grad_qkv, ("regions", "shard"), scatter_dimension=0, tiled=True),
        lax.psum_scatter(grad_out, ("regions", "shard"), scatter_dimension=0, tiled=True),
        lax.psum_scatter(grad_up, ("regions", "shard"), scatter_dimension=0, tiled=True),
        lax.psum_scatter(grad_down, ("regions", "shard"), scatter_dimension=0, tiled=True),
        lax.psum_scatter(grad_vec, ("regions", "shard"), scatter_dimension=1, tiled=True),
    )
    mats_total = jnp.sum(mats_pages, axis=0)
    table_back = jax.vjp(bias_table, relative)[1]
    grad_relative = lax.psum(table_back(mats_total)[0], ("regions", "shard"))
    firsts_qkv, seconds_qkv, update_qkv = adam_step(
        w_qkv.astype(jnp.float32), grad_qkv, first_qkv, second_qkv, DECAY_RATE
    )
    firsts_out, seconds_out, update_out = adam_step(
        w_out.astype(jnp.float32), grad_out, first_out, second_out, DECAY_RATE
    )
    firsts_up, seconds_up, update_up = adam_step(
        w_up.astype(jnp.float32), grad_up, first_up, second_up, DECAY_RATE
    )
    firsts_down, seconds_down, update_down = adam_step(
        w_down.astype(jnp.float32), grad_down, first_down, second_down, DECAY_RATE
    )
    firsts_vectors, seconds_vectors, update_vectors = adam_step(
        vectors.astype(jnp.float32), grad_vectors, first_vectors, second_vectors, 0.0
    )
    firsts_relative, seconds_relative, update_relative = adam_step(
        relative, grad_relative, first_relative, second_relative, 0.0
    )
    return (
        layer_out.astype(jnp.bfloat16)[None],
        in_grad[None],
        grad_qkv,
        firsts_qkv,
        seconds_qkv,
        update_qkv,
        grad_out,
        firsts_out,
        seconds_out,
        update_out,
        grad_up,
        firsts_up,
        seconds_up,
        update_up,
        grad_down,
        firsts_down,
        seconds_down,
        update_down,
        grad_vectors,
        firsts_vectors,
        seconds_vectors,
        update_vectors,
        grad_relative,
        firsts_relative,
        seconds_relative,
        update_relative,
    )


def solution(mesh):
    kernels = mesh.shape["regions"] == PEERS and mesh.shape["shard"] == 2
    return jax.shard_map(
        per_device if kernels else spread_device,
        mesh=mesh,
        in_specs=(
            P("shard", "regions", None),
            P("shard", "regions", None),
            P(("regions", "shard"), None),
            P(("regions", "shard"), None),
            P(("regions", "shard"), None),
            P(("regions", "shard"), None),
            P(None, ("regions", "shard")),
            P(),
            P(("regions", "shard"), None),
            P(("regions", "shard"), None),
            P(("regions", "shard"), None),
            P(("regions", "shard"), None),
            P(("regions", "shard"), None),
            P(("regions", "shard"), None),
            P(("regions", "shard"), None),
            P(("regions", "shard"), None),
            P(None, ("regions", "shard")),
            P(None, ("regions", "shard")),
            P(),
            P(),
            P("shard", "regions"),
            P("shard", "regions"),
            P("shard", "regions"),
            P("shard", "regions"),
        ),
        out_specs=(
            P("shard", "regions", None),
            P("shard", "regions", None),
            P(("regions", "shard"), None),
            P(("regions", "shard"), None),
            P(("regions", "shard"), None),
            P(("regions", "shard"), None),
            P(("regions", "shard"), None),
            P(("regions", "shard"), None),
            P(("regions", "shard"), None),
            P(("regions", "shard"), None),
            P(("regions", "shard"), None),
            P(("regions", "shard"), None),
            P(("regions", "shard"), None),
            P(("regions", "shard"), None),
            P(("regions", "shard"), None),
            P(("regions", "shard"), None),
            P(("regions", "shard"), None),
            P(("regions", "shard"), None),
            P(None, ("regions", "shard")),
            P(None, ("regions", "shard")),
            P(None, ("regions", "shard")),
            P(None, ("regions", "shard")),
            P(),
            P(),
            P(),
            P(),
        ),
        check_vma=False,
    )
```

```python
import jax
import jax.numpy as jnp
import numpy as np
from jax import lax
from jax.experimental import pallas as pl
from jax.experimental.pallas import tpu as pltpu
from jax.sharding import PartitionSpec as P

HEADS = 12
HEAD = 64
PAGE = 576


PRECISE = lax.Precision.HIGHEST
EPS_NORM = 1e-05
BETA_ONE = 0.9
BETA_TWO = 0.999
ADAM_EPS = 1e-08
LAYER_FACTOR = 0.5625
DECAY_RATE = 0.05
STEP_COUNT = 10.0


def skewed(line, size):
    count = line.shape[0]
    wide = jnp.pad(line, ((0, 0), (0, 1)))
    flat = jnp.broadcast_to(wide[:, None, :], (count, size, 2 * size)).reshape(count, -1)
    rows = flat[:, : size * (2 * size - 1)].reshape(count, size, 2 * size - 1)
    return rows[:, :, size - 1 :]


def bias_table(relative):
    seq = skewed(relative[:, :127], 64)
    horizontal = skewed(relative[:, 127:190], 32)
    vertical = skewed(relative[:, 190:253], 32)
    return (
        jnp.pad(seq, ((0, 0), (0, 64), (0, 64)))
        + jnp.pad(horizontal, ((0, 0), (64, 32), (64, 32)))
        + jnp.pad(vertical, ((0, 0), (96, 0), (96, 0)))
    )


def position_codes(box_x, box_y):
    places = jnp.arange(PAGE, dtype=jnp.int32)
    seq_bucket = places * 64 // PAGE
    columns = jnp.arange(128, dtype=jnp.int32)
    matched = (
        (columns[None, None, :] == seq_bucket[None, :, None])
        | (columns == 64 + box_x[..., None])
        | (columns == 96 + box_y[..., None])
    )
    return matched.astype(jnp.float32)


def layout_bias(code_rows, bias_mats):
    lifted = jnp.einsum("pa,hab->hpb", code_rows, bias_mats, precision=PRECISE)
    return jnp.einsum("hpb,qb->hpq", lifted, code_rows, precision=PRECISE)


def page_scores(page_qkv, code_rows, bias_mats):
    parted = page_qkv.reshape(PAGE, 3, HEADS, HEAD)
    queries = parted[:, 0]
    key_rows = parted[:, 1]
    values = parted[:, 2]
    scores = jnp.einsum(
        "phd,qhd->hpq", queries, key_rows, preferred_element_type=jnp.float32
    ) * 0.125 + layout_bias(code_rows, bias_mats)
    return (queries, key_rows, values, scores)


def page_forward(page_qkv, code_rows, bias_mats):
    queries, key_rows, values, scores = page_scores(page_qkv, code_rows, bias_mats)
    row_max = jnp.max(scores, axis=2, keepdims=True)
    raised = jnp.exp(scores - row_max)
    totals = jnp.sum(raised, axis=2, keepdims=True)
    attn_w = (raised / totals).astype(jnp.bfloat16)
    context = jnp.einsum("hpq,qhd->phd", attn_w, values, preferred_element_type=jnp.float32)
    log_total = (row_max + jnp.log(totals))[..., 0]
    return (context.reshape(PAGE, HEADS * HEAD).astype(jnp.bfloat16), log_total)


def page_backward(page_qkv, code_rows, log_total, grad_ctx, bias_mats):
    queries, key_rows, values, scores = page_scores(page_qkv, code_rows, bias_mats)
    chances = jnp.exp(scores - log_total[..., None])
    attn_w = chances.astype(jnp.bfloat16)
    grad_heads = grad_ctx.reshape(PAGE, HEADS, HEAD)
    grad_values = jnp.einsum("hpq,phd->qhd", attn_w, grad_heads, preferred_element_type=jnp.float32)
    grad_chances = jnp.einsum(
        "phd,qhd->hpq", grad_heads, values, preferred_element_type=jnp.float32
    )
    inner = jnp.sum(chances * grad_chances, axis=2, keepdims=True)
    grad_scores = (chances * (grad_chances - inner)).astype(jnp.bfloat16)
    grad_queries = (
        jnp.einsum("hpq,qhd->phd", grad_scores, key_rows, preferred_element_type=jnp.float32)
        * 0.125
    )
    grad_keys = (
        jnp.einsum("hpq,phd->qhd", grad_scores, queries, preferred_element_type=jnp.float32) * 0.125
    )
    partial_codes = jnp.einsum(
        "hpq,qb->hpb",
        grad_scores,
        code_rows.astype(jnp.bfloat16),
        preferred_element_type=jnp.float32,
    )
    grad_mats = jnp.einsum("pa,hpb->hab", code_rows, partial_codes, precision=PRECISE)
    grad_page = jnp.stack([grad_queries, grad_keys, grad_values], axis=1).reshape(
        PAGE, 3 * HEADS * HEAD
    )
    return (grad_page.astype(jnp.bfloat16), grad_mats)


def exchange(rows, targets, picks, groups, slot_cap):
    slots = groups * slot_cap
    places = jnp.arange(slots, dtype=jnp.int32)
    packing = (places[:, None] == targets[None, :]).astype(jnp.bfloat16)
    packed = jnp.dot(packing, rows, preferred_element_type=jnp.float32).astype(jnp.bfloat16)
    arrived = lax.all_to_all(
        packed.reshape(groups, slot_cap, rows.shape[1]),
        "regions",
        split_axis=0,
        concat_axis=0,
        tiled=True,
    ).reshape(slots, rows.shape[1])
    picking = (picks[:, None] == places[None, :]).astype(jnp.bfloat16)
    return jnp.dot(picking, arrived, preferred_element_type=jnp.float32)


def norm_forward(rows, gain, shift):
    centre = rows - jnp.mean(rows, axis=-1, keepdims=True)
    spread = lax.rsqrt(jnp.mean(centre * centre, axis=-1, keepdims=True) + EPS_NORM)
    normed = centre * spread
    return (normed * gain + shift, normed, spread)


def norm_back(incoming, normed, spread, gain):
    scaled = incoming * gain
    grad_rows = spread * (
        scaled
        - jnp.mean(scaled, axis=-1, keepdims=True)
        - normed * jnp.mean(scaled * normed, axis=-1, keepdims=True)
    )
    return (grad_rows, jnp.sum(incoming * normed, axis=0), jnp.sum(incoming, axis=0))


def adam_step(param, grad, moment, square, decay):
    moment_new = BETA_ONE * moment + (1.0 - BETA_ONE) * grad
    square_new = BETA_TWO * square + (1.0 - BETA_TWO) * grad * grad
    moment_hat = moment_new / (1.0 - BETA_ONE**STEP_COUNT)
    square_hat = square_new / (1.0 - BETA_TWO**STEP_COUNT)
    update = LAYER_FACTOR * (moment_hat / (jnp.sqrt(square_hat) + ADAM_EPS) + decay * param)
    return (moment_new, square_new, update)


ROWS = 576


def softly(scores, axis):
    peak = jnp.max(scores, axis=axis, keepdims=True)
    raised = jnp.exp(scores - peak)
    return raised * (1.0 / jnp.sum(raised, axis=axis, keepdims=True))


def head_lift(tables, codes, h):
    lines = tables[h]
    lane = lax.broadcasted_iota(jnp.int32, (64, 128), 1)

    def spread(n, size, low, high):
        line = jnp.broadcast_to(lines[n : n + 1], (size, 128))
        turned = pltpu.roll(line, 0, 1, stride=1, stride_axis=0)
        return jnp.where((lane[:size] >= low) & (lane[:size] < high), turned, 0.0)

    table = jnp.concatenate(
        [spread(0, 64, 0, 64), spread(1, 32, 64, 96), spread(2, 32, 96, 128)], axis=0
    )
    high = table.astype(jnp.bfloat16)
    low = (table - high.astype(jnp.float32)).astype(jnp.bfloat16)
    both = jnp.concatenate([high, low], axis=1)
    return jnp.dot(codes, both, preferred_element_type=jnp.float32).astype(jnp.bfloat16)


def lane_mask(rows, h):
    lane = lax.broadcasted_iota(jnp.int32, (rows, 128), 1)
    return (lane < 64) if h == 0 else (lane >= 64)


def pair_columns(qkv, pair):
    width = qkv.shape[1] // 3
    at = [pl.multiple_of(n * width + pair * 128, 128) for n in range(3)]
    return [qkv[:, pl.ds(a, 128)] for a in at]


NT = (((1,), (1,)), ((), ()))
TN = (((0,), (0,)), ((), ()))


def attend_pair(pair, qkv, tables, codes_ref, context):
    count = qkv.shape[0]
    codes = codes_ref[...]
    queries, keys, values = pair_columns(qkv, pair)
    right = jnp.concatenate([keys, codes, codes], axis=1)
    scaled = queries * jnp.bfloat16(0.125)
    results = []
    for h in range(2):
        mine = jnp.where(lane_mask(count, h), scaled, jnp.zeros_like(scaled))
        left = jnp.concatenate([mine, head_lift(tables, codes, 2 * pair + h)], axis=1)
        parts = []
        for r in range(0, count, ROWS):
            scores = lax.dot_general(left[r : r + ROWS], right, NT, preferred_element_type=jnp.float32)
            weights = softly(scores, 1).astype(jnp.bfloat16)
            parts.append(jnp.dot(weights, values, preferred_element_type=jnp.float32))
        results.append(parts)
    for n, r in enumerate(range(0, count, ROWS)):
        both = jnp.where(lane_mask(ROWS, 0), results[0][n], results[1][n])
        context[pl.ds(r, ROWS), pl.ds(pl.multiple_of(pair * 128, 128), 128)] = both.astype(jnp.bfloat16)


def attend_pair_back(pair, qkv, grad_ref, tables, codes_ref, flipped_ref, grad_qkv, grad_tables):
    count = qkv.shape[0]
    width = qkv.shape[1] // 3
    codes = codes_ref[...]
    queries, keys, values = pair_columns(qkv, pair)
    grads = grad_ref[:, pl.ds(pl.multiple_of(pair * 128, 128), 128)]
    left = jnp.concatenate([keys, codes, codes], axis=1)
    near = jnp.concatenate([keys, codes], axis=1)
    scaled = queries * jnp.bfloat16(0.125)
    out_q, out_k, out_v = [], [], []
    for h in range(2):
        mask = lane_mask(count, h)
        mine = jnp.where(mask, scaled, jnp.zeros_like(scaled))
        mine_grad = jnp.where(mask, grads, jnp.zeros_like(grads))
        right = jnp.concatenate([mine, head_lift(tables, codes, 2 * pair + h)], axis=1)
        total = None
        k_parts, v_parts = [], []
        if True:
            scores = lax.dot_general(left, right, NT, preferred_element_type=jnp.float32)
            chances = softly(scores, 0)
            grad_chances = lax.dot_general(values, mine_grad, NT, preferred_element_type=jnp.float32)
            inner = jnp.sum(chances * grad_chances, axis=0, keepdims=True)
            grad_scores = (chances * (grad_chances - inner)).astype(jnp.bfloat16)
            v_rows = jnp.dot(chances.astype(jnp.bfloat16), grads, preferred_element_type=jnp.float32)
            k_rows = jnp.dot(grad_scores, queries, preferred_element_type=jnp.float32)
            total = lax.dot_general(grad_scores, near, TN, preferred_element_type=jnp.float32)
        out_q.append(total[:, :128])
        out_k.append(k_rows)
        out_v.append(v_rows)
        partial = total[:, 128:]
        high = partial.astype(jnp.bfloat16)
        low = (partial - high.astype(jnp.float32)).astype(jnp.bfloat16)
        mats = lax.dot_general(
            flipped_ref[...], jnp.concatenate([high, low], axis=1), TN, preferred_element_type=jnp.float32
        )
        mats = mats[:, :128] + mats[:, 128:]
        lane = lax.broadcasted_iota(jnp.int32, (64, 128), 1)

        def gathered(row, size, low_lane, high_lane):
            part = jnp.where((lane[:size] >= low_lane) & (lane[:size] < high_lane), mats[row : row + size], 0.0)
            turned = pltpu.roll(part, 0, 1, stride=1, stride_axis=0)
            return jnp.sum(turned, axis=0, keepdims=True)

        grad_tables[2 * pair + h] = jnp.concatenate(
            [
                gathered(0, 64, 0, 64),
                gathered(64, 32, 64, 96),
                gathered(96, 32, 96, 128),
                jnp.zeros((5, 128), jnp.float32),
            ],
            axis=0,
        )
    mask = lane_mask(count, 0)
    for n, (parts, factor) in enumerate(((out_q, 0.125), (out_k, 0.125), (out_v, 1.0))):
        both = jnp.where(mask, parts[0], parts[1]) * factor
        grad_qkv[:, pl.ds(pl.multiple_of(n * width + pair * 128, 128), 128)] = both.astype(jnp.bfloat16)


def code_columns(seq, box_x, box_y):
    columns = jnp.arange(128, dtype=jnp.int32)[None]
    hit = (columns == seq[:, None]) | (columns == 64 + box_x[:, None]) | (columns == 96 + box_y[:, None])
    return hit.astype(jnp.bfloat16)


def table_lines(relative):
    seq = jnp.pad(relative[:, :127], ((0, 0), (0, 1)))
    horizontal = jnp.pad(relative[:, 127:190], ((0, 0), (0, 65)))
    vertical = jnp.pad(relative[:, 190:253], ((0, 0), (0, 65)))
    lines = [jnp.roll(seq, -63, 1), jnp.roll(horizontal, 33, 1), jnp.roll(vertical, 65, 1)]
    return jnp.pad(jnp.stack(lines, axis=1), ((0, 0), (0, 5), (0, 0)))


def lines_back(grad):
    return jnp.concatenate(
        [grad[:, 0, :127], grad[:, 1, 64:127], jnp.roll(grad[:, 2], -96, 1)[:, :63]], axis=1
    )


MESH = pl.DeviceIdType.MESH
PEERS = 16
VEC_COLS = 256


def place():
    me = lax.axis_index("regions")
    core = lax.axis_index("shard")
    z = lax.div(me, 4)
    y = lax.div(lax.rem(me, 4), 2)
    x = lax.rem(me, 2)
    return me, core, z, y, x


def enter(me, core):
    barrier = pltpu.get_barrier_semaphore()
    for k in range(1, PEERS):
        pl.semaphore_signal(barrier, inc=1, device_id=(me ^ k, core), device_id_type=MESH)
    pl.semaphore_signal(barrier, inc=1, device_id=(me, 1 - core), device_id_type=MESH)
    pl.semaphore_wait(barrier, PEERS)


def remote(src, dst, send, recv, device):
    return pltpu.make_async_remote_copy(
        src_ref=src, dst_ref=dst, send_sem=send, recv_sem=recv, device_id=device, device_id_type=MESH
    )


class Exchange:
    def __init__(self, where, packed, arrived, loose, send, recv, local):
        self.me, self.core = where[0], where[1]
        self.packed, self.arrived, self.loose = packed, arrived, loose
        self.send, self.recv, self.local = send, recv, local
        self.slots, self.half = packed.shape[1], packed.shape[2]

    def pack(self, rows, slot_of):
        count = self.slots // 2
        for j in range(4):
            group = lax.div(self.me, 4) ^ j
            at = lax.broadcasted_iota(jnp.int32, (4 * count, rows.shape[0]), 0) + group * (4 * count)
            picking = jnp.where(at == slot_of[...], 1.0, 0.0).astype(jnp.bfloat16)
            block = jnp.dot(picking, rows[...], preferred_element_type=jnp.float32)
            for n in range(4):
                own = block[n * count : (n + 1) * count]
                both = jnp.concatenate([own[:, : self.half], own[:, self.half :]], axis=0)
                self.packed[4 * group + n] = both.astype(jnp.bfloat16)
            for k in range(4):
                if j + k:
                    self.copy(4 * j + k).start()
                else:
                    self.own().start()

    def copy(self, k):
        d = self.me ^ k
        return remote(
            self.packed.at[d], self.arrived.at[self.me], self.send.at[k], self.recv.at[k], (d, self.core)
        )

    def own(self):
        return pltpu.make_async_copy(self.packed.at[self.me], self.arrived.at[self.me], self.local)

    def wait(self):
        self.own().wait()

        def one(k, carry):
            self.copy(k).wait()
            return carry

        lax.fori_loop(1, PEERS, one, 0)

    def unpack(self, slot_of, out, kind):
        count = self.slots // 2
        rows = []
        for n in range(PEERS):
            block = self.arrived[n].astype(jnp.float32)
            rows.append(jnp.concatenate([block[:count], block[count:]], axis=1))
            if n % 2:
                pair = jnp.concatenate(rows, axis=0)
                self.loose[pl.ds((n - 1) * count, 2 * count)] = pair.astype(jnp.bfloat16)
                rows = []
        at = lax.broadcasted_iota(jnp.int32, (out.shape[0], PEERS * count), 1)
        picking = jnp.where(at == slot_of[...], 1.0, 0.0).astype(jnp.bfloat16)
        got = jnp.dot(picking, self.loose[...], preferred_element_type=jnp.float32)
        out[...] = got.astype(kind)


def pieces_of(rows, half):
    tiles = half // 128
    if rows % 64 == 0:
        cuts = [(n * rows // 4, rows // 4, 0, half) for n in range(4)]
    elif tiles < 4:
        wide = (tiles + 1) // 2 * 128
        cuts = [(0, rows, 0, wide), (0, rows, wide, half - wide)]
    else:
        ends = [0, (tiles + 3) // 4, tiles // 2, tiles - (tiles + 3) // 4, tiles]
        cuts = [(0, rows, 128 * ends[n], 128 * (ends[n + 1] - ends[n])) for n in range(4)]
    return [[(*cuts[n], True), (*cuts[n + 1], False)] for n in range(0, len(cuts), 2)]


class Gather:
    def __init__(self, where, whole, piece, sems):
        self.where, self.whole, self.piece, self.sems = where, whole, piece, sems

    def part(self, z, y, x):
        core = self.where[1]
        r0, rows, c0, cols, _ = self.piece
        half = self.whole.shape[4] // 2
        at = pl.multiple_of(core * half + c0, 128)
        return self.whole.at[z, y, x, pl.ds(r0, rows), pl.ds(at, cols)]

    def along_z(self, t, upward):
        me, core, z, y, x = self.where
        step = 1 if upward else -1
        origin = z - step * t
        ref = self.part(origin, y, x)
        i = 2 * t + (1 if upward else 0)
        return remote(ref, ref, self.sems.at[0, i], self.sems.at[1, i], (me + 4 * step, core))

    def z_sends(self, t, do):
        z = self.where[2]

        @pl.when((z >= t) & (z <= 2))
        def _():
            do(self.along_z(t, True))

        @pl.when((z + t <= 3) & (z >= 1))
        def _():
            do(self.along_z(t, False))

    def z_waits(self, t):
        z = self.where[2]

        @pl.when(z - 1 - t >= 0)
        def _():
            me, core, z, y, x = self.where
            ref = self.part(z - 1 - t, y, x)
            i = 2 * t + 1
            remote(ref, ref, self.sems.at[0, i], self.sems.at[1, i], (me, 1 - core)).wait_recv()

        @pl.when(z + 1 + t <= 3)
        def _():
            me, core, z, y, x = self.where
            ref = self.part(z + 1 + t, y, x)
            i = 2 * t
            remote(ref, ref, self.sems.at[0, i], self.sems.at[1, i], (me, 1 - core)).wait_recv()

    def plane(self, n):
        me, core, z, y, x = self.where
        x_first = self.piece[4]
        every = slice(None)
        other = (me, 1 - core)
        if n == 0:
            ref, device = self.part(every, y, x), (me ^ (1 if x_first else 2), core)
        elif n == 1 and x_first:
            ref, device = self.part(every, y, every), (me ^ 2, core)
        elif n == 1:
            ref, device = self.part(every, every, x), (me ^ 1, core)
        elif n == 2:
            ref, device = self.part(every, y, x), other
        elif n == 3:
            ref, device = (self.part(every, y, 1 - x) if x_first else self.part(every, 1 - y, x)), other
        else:
            ref, device = (self.part(every, 1 - y, every) if x_first else self.part(every, every, 1 - x)), other
        return remote(ref, ref, self.sems.at[0, 6 + n], self.sems.at[1, 6 + n], device)

    def run(self, stage):
        if stage < 3:
            if stage:
                self.z_waits(stage - 1)
            self.z_sends(stage, lambda copy: copy.start())
        elif stage == 3:
            self.z_waits(2)
            self.plane(0).start()
            self.plane(2).start()
        elif stage == 4:
            self.plane(0).wait_recv()
            self.plane(1).start()
            self.plane(3).start()
        elif stage == 5:
            self.plane(1).wait_recv()
            self.plane(4).start()
        else:
            for n in (2, 3, 4):
                self.plane(n).wait_recv()

    def sent(self):
        for t in range(3):
            self.z_sends(t, lambda copy: copy.wait_send())
        for n in range(5):
            self.plane(n).wait_send()


class Scatter:
    def __init__(self, where, local, sums, from_core, from_near, from_far, from_z, fetch, piece, sems):
        self.where, self.local, self.sums, self.piece, self.sems = where, local, sums, piece, sems
        self.from_core, self.from_near, self.from_far, self.from_z = from_core, from_near, from_far, from_z
        self.half, self.fetch = sums.shape[4], fetch

    def cut(self, ref, *lead, core=None):
        r0, rows, c0, cols, _ = self.piece
        at = c0 if core is None else pl.multiple_of(core * self.half + c0, 128)
        return ref.at[(*lead, pl.ds(r0, rows), pl.ds(at, cols))]

    def between_cores(self):
        me, core = self.where[0], self.where[1]
        every = slice(None)
        src = self.cut(self.local, every, every, every, core=1 - core)
        dst = self.cut(self.from_core, every, every, every)
        return remote(src, dst, self.sems.at[0, 0], self.sems.at[1, 0], (me, 1 - core))

    def own_half(self):
        every = slice(None)
        src = self.cut(self.local, every, every, every, core=self.where[1])
        return pltpu.make_async_copy(src, self.cut(self.sums, every, every, every), self.fetch)

    def near(self):
        me, core, z, y, x = self.where
        every = slice(None)
        if self.piece[4]:
            src, device = self.cut(self.sums, every, 1 - y, every), (me ^ 2, core)
        else:
            src, device = self.cut(self.sums, every, every, 1 - x), (me ^ 1, core)
        dst = self.cut(self.from_near, every, every)
        return remote(src, dst, self.sems.at[0, 1], self.sems.at[1, 1], device)

    def far(self):
        me, core, z, y, x = self.where
        every = slice(None)
        if self.piece[4]:
            src, device = self.cut(self.sums, every, y, 1 - x), (me ^ 1, core)
        else:
            src, device = self.cut(self.sums, every, 1 - y, x), (me ^ 2, core)
        dst = self.cut(self.from_far, every)
        return remote(src, dst, self.sems.at[0, 2], self.sems.at[1, 2], device)

    def along_z(self, sender, upward):
        me, core, z, y, x = self.where
        lead = pl.ds(sender + 1, 3 - sender) if upward else pl.ds(0, sender)
        src = self.cut(self.sums, lead, y, x)
        dst = self.cut(self.from_z, 1 if upward else 0, lead)
        i = 3 + (1 if upward else 0)
        step = 4 if upward else -4
        return remote(src, dst, self.sems.at[0, i], self.sems.at[1, i], (me + step, core))

    def add(self, target, other):
        total = target[...].astype(jnp.float32) + other[...].astype(jnp.float32)
        target[...] = total.astype(jnp.bfloat16)

    def z_got(self, sender, upward):
        me, core, z, y, x = self.where
        self.along_z(sender, upward).wait_recv()
        for d in range(sender + 1, 4) if upward else range(sender):
            self.add(self.cut(self.sums, d, y, x), self.cut(self.from_z, 1 if upward else 0, d))

    def run(self, stage):
        me, core, z, y, x = self.where
        if stage == 0:
            self.between_cores().start()
            self.own_half().start()
        elif stage == 1:
            self.own_half().wait()
            self.between_cores().wait_recv()

            def one(i, carry):
                a, b, c = lax.div(i, 4), lax.div(lax.rem(i, 4), 2), lax.rem(i, 2)
                self.add(self.cut(self.sums, a, b, c), self.cut(self.from_core, a, b, c))
                return carry

            lax.fori_loop(0, 16, one, 0)
            self.near().start()
        elif stage == 2:
            self.near().wait_recv()

            def one(i, carry):
                a, b = lax.div(i, 2), lax.rem(i, 2)
                target = self.cut(self.sums, a, y, b) if self.piece[4] else self.cut(self.sums, a, b, x)
                self.add(target, self.cut(self.from_near, a, b))
                return carry

            lax.fori_loop(0, 8, one, 0)
            self.far().start()
        elif stage == 3:
            self.far().wait_recv()

            def one(i, carry):
                self.add(self.cut(self.sums, i, y, x), self.cut(self.from_far, i))
                return carry

            lax.fori_loop(0, 4, one, 0)

            @pl.when(z == 3)
            def _():
                self.along_z(3, False).start()

            @pl.when(z == 0)
            def _():
                self.along_z(0, True).start()

        elif stage == 4:

            @pl.when(z == 2)
            def _():
                self.z_got(3, False)
                self.along_z(2, False).start()

            @pl.when(z == 1)
            def _():
                self.z_got(0, True)
                self.along_z(1, True).start()

        elif stage == 5:

            @pl.when(z == 1)
            def _():
                self.z_got(2, False)
                self.along_z(1, False).start()

            @pl.when(z == 2)
            def _():
                self.z_got(1, True)
                self.along_z(2, True).start()

        elif stage == 6:

            @pl.when(z == 0)
            def _():
                self.z_got(1, False)

            @pl.when(z == 3)
            def _():
                self.z_got(2, True)

    def sent(self):
        z = self.where[2]
        self.between_cores().wait_send()
        self.near().wait_send()
        self.far().wait_send()
        for sender in range(4):

            @pl.when(z == sender)
            def _(sender=sender):
                if sender > 0:
                    self.along_z(sender, False).wait_send()
                if sender < 3:
                    self.along_z(sender, True).wait_send()


def stepper(tasks):
    def step(k):
        for pair, plan in tasks:
            if k in plan:
                for task in pair:
                    task.run(plan.index(k))

    return step, max(plan[-1] for _, plan in tasks) + 1


PAIRS = 6
READY = 8
SEND_ROWS = 4


def gather_plan(n, early):
    z, wide = n // 2, 3 + n
    if early:
        return (z, z + 1, z + 2, wide, wide + 1, wide + 2, wide + 3)
    return (z, z + 1, z + 2, wide, wide + 2, wide + 4, wide + 6)


def inbound_kernel(
    rows_ref, grad_ref, slot_line, home_column, tables, codes, s_qkv, s_out, s_up, s_down,
    homed, cotangent, qkv, context, vec_rows, w_qkv, w_out, w_up, w_down,
    packed_a, arrived_a, packed_b, arrived_b, loose, p_qkv, p_out, p_up, p_down, b_qkv, b_out, b_up, b_down,
    send_a, recv_a, send_b, recv_b, local_sems, pair_sems, block_sems, piece_sems,
):
    where = place()
    me, core, z, y, x = where
    enter(me, core)
    shards = (s_qkv, s_out, s_up, s_down)
    others = (p_qkv, p_out, p_up, p_down)
    blocks = (b_qkv, b_out, b_up, b_down)
    wholes = (w_qkv, w_out, w_up, w_down)
    pairs = [
        remote(shards[i].at[1 - core], others[i], pair_sems.at[0, i], pair_sems.at[1, i], (me, 1 - core))
        for i in range(4)
    ]
    for pair in pairs:
        pair.start()
    moved = Exchange(where, packed_a, arrived_a, loose, send_a, recv_a, local_sems.at[0])
    moved_grad = Exchange(where, packed_b, arrived_b, loose, send_b, recv_b, local_sems.at[1])
    placed = []
    tasks = []
    for i in range(4):
        pairs[i].wait_recv()
        half = blocks[i].shape[1]
        rows = blocks[i].shape[0] // 2
        mine = shards[i][core][:rows].astype(jnp.float32)
        other = others[i][:rows].astype(jnp.float32)
        first = jnp.where(core == 0, mine, other)
        second = jnp.where(core == 0, other, mine)
        blocks[i][...] = jnp.concatenate([first, second], axis=0).astype(jnp.bfloat16)
        at = pl.multiple_of(core * half, 128)
        copy = pltpu.make_async_copy(
            blocks[i], wholes[i].at[z, y, x, :, pl.ds(at, half)], block_sems.at[i]
        )
        copy.start()
        placed.append(copy)
    for i in range(4):
        placed[i].wait()
        for pair in pieces_of(blocks[i].shape[0], blocks[i].shape[1]):
            n = len(tasks)
            pair = [Gather(where, wholes[i], piece, piece_sems.at[2 * n + j]) for j, piece in enumerate(pair)]
            tasks.append((pair, gather_plan(n, i == 0)))
    step, steps = stepper(tasks)

    for k in range(READY):
        step(k)
        if k == SEND_ROWS:
            moved.pack(rows_ref, slot_line)
    moved.wait()
    moved.unpack(home_column, homed, jnp.bfloat16)
    moved_grad.pack(grad_ref, slot_line)
    width = homed.shape[1]
    columns = w_qkv[:, :, :, :, 3 * width : 3 * width + 128].reshape(width, 128)
    vec_rows[...] = columns.astype(jnp.float32).T[: vec_rows.shape[0]]
    for n in range(3):
        part = w_qkv[:, :, :, :, n * width : (n + 1) * width].reshape(width, width)
        projected = jnp.dot(homed[...], part, preferred_element_type=jnp.float32)
        if n != 1:
            projected = projected + vec_rows[n // 2 : n // 2 + 1]
        qkv[:, n * width : (n + 1) * width] = projected.astype(jnp.bfloat16)

    def one(pair, carry):
        attend_pair(pair, qkv, tables, codes, context)
        for j in range(PAIRS):

            @pl.when(pair == j)
            def _(j=j):
                step(READY + j)

        return carry

    lax.fori_loop(0, PAIRS, one, 0)
    for k in range(READY + PAIRS, steps):
        step(k)
    moved_grad.wait()
    moved_grad.unpack(home_column, cotangent, jnp.bfloat16)
    for pair in pairs:
        pair.wait_send()
    for pair, _ in tasks:
        for task in pair:
            task.sent()


def vmem(count):
    return [pl.BlockSpec(memory_space=pltpu.VMEM)] * count


def inbound(rows, grads, slot_line, home_column, tables, codes, shards):
    tokens, width = rows.shape
    slots = 2 * (2 * tokens // PEERS)
    low = jnp.bfloat16
    buffer = pltpu.VMEM((PEERS, slots, width // 2), low)
    wholes, pair_shapes, block_shapes = [], [], []
    for shard, padded in shards:
        half = padded.shape[2]
        wholes.append(jax.ShapeDtypeStruct((4, 2, 2, 2 * shard, 2 * half), low))
        pair_shapes.append(pltpu.VMEM(padded.shape[1:], low))
        block_shapes.append(pltpu.VMEM((2 * shard, half), low))
    dma = pltpu.SemaphoreType.DMA
    return pl.pallas_call(
        inbound_kernel,
        out_shape=[
            jax.ShapeDtypeStruct((tokens, width), low),
            jax.ShapeDtypeStruct((tokens, width), low),
            jax.ShapeDtypeStruct((tokens, 3 * width), low),
            jax.ShapeDtypeStruct((tokens, width), low),
            jax.ShapeDtypeStruct((16, width), jnp.float32),
        ]
        + wholes,
        in_specs=vmem(10),
        out_specs=vmem(9),
        scratch_shapes=[buffer] * 4 + [pltpu.VMEM((PEERS * (slots // 2), width), low)] + pair_shapes + block_shapes
        + [dma((PEERS,)), dma((PEERS,)), dma((PEERS,)), dma((PEERS,)), dma((2,)), dma((2, 4)), dma((4,)), dma((14, 2, 11))],
        compiler_params=pltpu.CompilerParams(
            collective_id=1, has_side_effects=True, vmem_limit_bytes=60 << 20
        ),
        name="inbound",
    )(rows, grads, slot_line, home_column, tables, codes, *[padded for _, padded in shards])


def normed_rows(rows):
    centre = rows - jnp.mean(rows, axis=-1, keepdims=True)
    spread = lax.rsqrt(jnp.mean(centre * centre, axis=-1, keepdims=True) + EPS_NORM)
    return centre * spread, spread


def dense_kernel(
    homed, cotangent, context, vec, w_out, w_up, w_down,
    result, grad_one_ref, grad_context, g_out, g_up, g_down, vec_grads,
    act, slope, hidden_low,
):
    width = homed.shape[1]
    chunks = w_up.shape[4] // width
    f32 = jnp.float32
    low = jnp.bfloat16

    def columns(ref, c):
        return ref[:, :, :, :, c * width : (c + 1) * width].reshape(width, width)

    def keep(n, line):
        vec_grads[n : n + 1] = jnp.sum(line, axis=0, keepdims=True)

    attn_out = jnp.dot(context[...], columns(w_out, 0), preferred_element_type=f32) + vec[2:3]
    normed_one, spread_one = normed_rows(homed[...].astype(f32) + attn_out)
    hidden = normed_one * vec[3:4] + vec[4:5]
    hidden_low[...] = hidden.astype(low)
    branch = None
    for c in range(chunks):
        pre = jnp.dot(hidden_low[...], columns(w_up, c), preferred_element_type=f32) + vec[8 + c : 9 + c]
        below = 0.5 * (1.0 + lax.erf(pre * 0.7071067811865476))
        act[c] = (pre * below).astype(low)
        slope[c] = below + pre * (jnp.exp(-0.5 * pre * pre) * 0.3989422804014327)
        part = jnp.dot(act[c], w_down[c].reshape(width, width), preferred_element_type=f32)
        branch = part if branch is None else branch + part
    normed_two, spread_two = normed_rows(hidden + branch + vec[5:6])
    result[...] = (normed_two * vec[6:7] + vec[7:8]).astype(low)

    def back(e, normed, spread, gain):
        scaled = e * gain
        return spread * (
            scaled
            - jnp.mean(scaled, axis=-1, keepdims=True)
            - normed * jnp.mean(scaled * normed, axis=-1, keepdims=True)
        )

    e = cotangent[...].astype(f32)
    keep(6, e * normed_two)
    keep(7, e)
    grad_two = back(e, normed_two, spread_two, vec[6:7])
    grad_branch = grad_two.astype(low)
    keep(5, grad_branch.astype(f32))
    grad_hidden = grad_two
    for c in range(chunks):
        g_down[c] = (
            lax.dot_general(act[c], grad_branch, TN, preferred_element_type=f32)
            .astype(low)
            .reshape(g_down.shape[1:])
        )
        grad_act = lax.dot_general(
            grad_branch, w_down[c].reshape(width, width), NT, preferred_element_type=f32
        )
        grad_pre = (grad_act * slope[c]).astype(low)
        keep(8 + c, grad_pre.astype(f32))
        g_up[:, :, :, :, c * width : (c + 1) * width] = (
            lax.dot_general(hidden_low[...], grad_pre, TN, preferred_element_type=f32)
            .astype(low)
            .reshape(*g_up.shape[:4], width)
        )
        grad_hidden = grad_hidden + lax.dot_general(
            grad_pre, columns(w_up, c), NT, preferred_element_type=f32
        )
    keep(3, grad_hidden * normed_one)
    keep(4, grad_hidden)
    grad_one = back(grad_hidden, normed_one, spread_one, vec[3:4])
    grad_one_ref[...] = grad_one
    grad_attn = grad_one.astype(low)
    keep(2, grad_attn.astype(f32))
    g_out[...] = (
        lax.dot_general(context[...], grad_attn, TN, preferred_element_type=f32)
        .astype(low)
        .reshape(g_out.shape)
    )
    grad_context[...] = lax.dot_general(
        grad_attn, columns(w_out, 0), NT, preferred_element_type=f32
    ).astype(low)
    vec_grads[0:2] = jnp.zeros((2, width), f32)
    vec_grads[12:] = jnp.zeros((vec_grads.shape[0] - 12, width), f32)


def dense(homed, cotangent, context, vec, w_out, w_up, w_down):
    tokens, width = homed.shape
    chunks = w_up.shape[4] // width
    low = jnp.bfloat16
    row_shape = jax.ShapeDtypeStruct((tokens, width), low)
    return pl.pallas_call(
        dense_kernel,
        out_shape=[row_shape, jax.ShapeDtypeStruct((tokens, width), jnp.float32), row_shape]
        + [jax.ShapeDtypeStruct(w.shape, low) for w in (w_out, w_up, w_down)]
        + [jax.ShapeDtypeStruct((128, width), jnp.float32)],
        in_specs=vmem(7),
        out_specs=vmem(7),
        scratch_shapes=[
            pltpu.VMEM((chunks, tokens, width), low),
            pltpu.VMEM((chunks, tokens, width), jnp.float32),
            pltpu.VMEM((tokens, width), low),
        ],
        compiler_params=pltpu.CompilerParams(vmem_limit_bytes=60 << 20),
        name="dense",
    )(homed, cotangent, context, vec, w_out, w_up, w_down)


LAST = 7


def scatter_plan(n, late):
    if late:
        return tuple(range(LAST, LAST + 7))
    return (n // 2, 3 + n, 5 + n, 7 + n, 8 + n, 9 + n, 10 + n)


def outbound_kernel(
    result_ref, grad_one, qkv, grad_context, homed, vec_grads, home_line, slot_column, tables, codes, flipped,
    w_qkv, g_out, g_up, g_down,
    result_out, grad_out, table_out, o_qkv, o_out, o_up, o_down,
    packed, arrived_a, arrived_b, loose, table_got, grad_qkv, g_qkv,
    t_qkv, t_out, t_up, t_down, c_qkv, c_out, c_up, c_down, n_qkv, n_out, n_up, n_down,
    f_qkv, f_out, f_up, f_down, z_qkv, z_out, z_up, z_down, e_qkv, e_out, e_up, e_down,
    send_a, recv_a, send_b, recv_b, local_sems, table_sems, piece_sems, fetch_sems, last_sems,
):
    where = place()
    me, core, z, y, x = where
    enter(me, core)
    local = (g_qkv, g_out, g_up, g_down)
    sums = (t_qkv, t_out, t_up, t_down)
    from_core = (c_qkv, c_out, c_up, c_down)
    from_near = (n_qkv, n_out, n_up, n_down)
    from_far = (f_qkv, f_out, f_up, f_down)
    from_z = (z_qkv, z_out, z_up, z_down)
    ends = (e_qkv, e_out, e_up, e_down)
    outs = (o_qkv, o_out, o_up, o_down)
    low = jnp.bfloat16
    tasks = []
    for i in (3, 2, 1, 0):
        refs = (local[i], sums[i], from_core[i], from_near[i], from_far[i], from_z[i])
        for pair in pieces_of(sums[i].shape[3], sums[i].shape[4]):
            n = len(tasks)
            pair = [
                Scatter(where, *refs, fetch_sems.at[2 * n + j], piece, piece_sems.at[2 * n + j])
                for j, piece in enumerate(pair)
            ]
            tasks.append((pair, scatter_plan(n, i == 0)))
    step, steps = stepper(tasks)
    moved = Exchange(where, packed, arrived_a, loose, send_a, recv_a, local_sems.at[0])
    moved_grad = Exchange(where, packed, arrived_b, loose, send_b, recv_b, local_sems.at[1])
    devices = [(me, 1 - core), (me ^ 1, core), (me ^ 2, core), (me ^ 4, core), (me ^ 8, core)]
    shares = [
        remote(table_got.at[0, n], table_got.at[1, n], table_sems.at[0, n], table_sems.at[1, n], device)
        for n, device in enumerate(devices)
    ]

    step(0)
    moved.pack(result_ref, home_line)

    def one(pair, carry):
        attend_pair_back(pair, qkv, grad_context, tables, codes, flipped, grad_qkv, table_out)
        for j in range(PAIRS):

            @pl.when(pair == j)
            def _(j=j):
                step(1 + j)

        return carry

    lax.fori_loop(0, PAIRS, one, 0)
    width = homed.shape[1]
    sums_of = []
    in_home = grad_one[...]
    for n in range(3):
        part = grad_qkv[:, n * width : (n + 1) * width]
        g_qkv[:, :, :, :, n * width : (n + 1) * width] = (
            lax.dot_general(homed[...], part, TN, preferred_element_type=jnp.float32)
            .astype(low)
            .reshape(*g_qkv.shape[:4], width)
        )
        sums_of.append(jnp.sum(part.astype(jnp.float32), axis=0, keepdims=True))
        weights = w_qkv[:, :, :, :, n * width : (n + 1) * width].reshape(width, width)
        in_home = in_home + lax.dot_general(part, weights, NT, preferred_element_type=jnp.float32)
    row = lax.broadcasted_iota(jnp.int32, (128, width), 0)
    lines = jnp.where(row == 0, sums_of[0], jnp.where(row == 1, sums_of[2], vec_grads[...]))
    beside = lines.T.astype(low).reshape(*g_qkv.shape[:4], 128)
    g_qkv[:, :, :, :, 3 * width : 3 * width + 128] = beside
    g_qkv[:, :, :, :, 3 * width + 128 :] = jnp.zeros_like(beside)
    step(LAST)
    moved.wait()
    moved_grad.pack(in_home.astype(low), home_line)
    moved.unpack(slot_column, result_out, low)
    for k in range(LAST + 1, steps):
        step(k)
        n = k - LAST - 1
        if 0 < n <= 5:
            shares[n - 1].wait_recv()
            table_out[...] += table_got[1, n - 1]
        if n < 5:
            table_got[0, n] = table_out[...]
            shares[n].start()
    finals = []
    for i in (3, 2, 1, 0):
        block = sums[i][z, y, x].astype(jnp.float32)
        rows = block.shape[0] // 2
        ends[i][0] = block[:rows]
        ends[i][1] = block[rows:]
        outs[i][core] = ends[i][core]
        copy = remote(ends[i].at[1 - core], outs[i].at[core], last_sems.at[0, i], last_sems.at[1, i], (me, 1 - core))
        copy.start()
        finals.append(copy)
    moved_grad.wait()
    moved_grad.unpack(slot_column, grad_out, jnp.float32)
    for copy in finals:
        copy.wait()
    for share in shares:
        share.wait_send()
    for pair, _ in tasks:
        for task in pair:
            task.sent()


def outbound(result, grad_one, qkv, grad_context, homed, vec_grads, home_line, slot_column, tables, codes, flipped, w_qkv, locals_):
    tokens, width = result.shape
    slots = 2 * (2 * tokens // PEERS)
    low = jnp.bfloat16
    buffer = pltpu.VMEM((PEERS, slots, width // 2), low)
    halves = [(g.shape[3], g.shape[4] // 2) for g in (w_qkv, *locals_)]
    scratch = (
        [buffer] * 3
        + [pltpu.VMEM((PEERS * (slots // 2), width), low)]
        + [pltpu.VMEM((2, 5, *tables.shape), jnp.float32)]
        + [pltpu.VMEM(qkv.shape, low), pltpu.VMEM(w_qkv.shape, low)]
        + [pltpu.VMEM((4, 2, 2, r, h), low) for r, h in halves]
        + [pltpu.VMEM((4, 2, 2, r, h), low) for r, h in halves]
        + [pltpu.VMEM((4, 2, r, h), low) for r, h in halves]
        + [pltpu.VMEM((4, r, h), low) for r, h in halves]
        + [pltpu.VMEM((2, 4, r, h), low) for r, h in halves]
        + [pltpu.VMEM((2, r // 2, h), jnp.float32) for r, h in halves]
    )
    dma = pltpu.SemaphoreType.DMA
    return pl.pallas_call(
        outbound_kernel,
        out_shape=[
            jax.ShapeDtypeStruct(result.shape, low),
            jax.ShapeDtypeStruct(result.shape, jnp.float32),
            jax.ShapeDtypeStruct(tables.shape, jnp.float32),
        ]
        + [jax.ShapeDtypeStruct((2, r // 2, h), jnp.float32) for r, h in halves],
        in_specs=vmem(12) + [pl.BlockSpec(memory_space=pl.ANY)] * 3,
        out_specs=vmem(7),
        scratch_shapes=scratch
        + [dma((PEERS,)), dma((PEERS,)), dma((PEERS,)), dma((PEERS,)), dma((2,)), dma((2, 5)), dma((14, 2, 5)), dma((14,)), dma((2, 4))],
        compiler_params=pltpu.CompilerParams(
            collective_id=2, has_side_effects=True, vmem_limit_bytes=62 << 20
        ),
        name="outbound",
    )(result, grad_one, qkv, grad_context, homed, vec_grads, home_line, slot_column, tables, codes, flipped, w_qkv, *locals_)


def shard_halves(shard):
    rows, columns = shard.shape
    halves = shard.reshape(rows, 2, columns // 2).transpose(1, 0, 2)
    return (rows, jnp.pad(halves, ((0, 0), (0, -rows % 16), (0, 0))))


def joined(halves):
    return jnp.concatenate([halves[0], halves[1]], axis=1)


def per_device(
    layer_in,
    out_grad,
    w_qkv,
    w_out,
    w_up,
    w_down,
    vectors,
    relative,
    first_qkv,
    second_qkv,
    first_out,
    second_out,
    first_up,
    second_up,
    first_down,
    second_down,
    first_vectors,
    second_vectors,
    first_relative,
    second_relative,
    token_slot,
    home_index,
    box_x,
    box_y,
):
    tokens = layer_in[0]
    rows_dev, model_dim = tokens.shape
    kinds = vectors.shape[0]
    beside = jnp.pad(vectors.T, ((0, 0), (0, VEC_COLS - kinds)))
    wide_qkv = jnp.concatenate([w_qkv, beside], axis=1)
    slot_at, home_at = token_slot[0], home_index[0]
    bucket = jnp.arange(PAGE, dtype=jnp.int32) * 64 // PAGE
    codes = code_columns(bucket, box_x[0], box_y[0])
    flipped = code_columns(63 - bucket, 31 - box_x[0], 31 - box_y[0])
    tables = table_lines(relative)
    homed, cotangent, qkv, context, vec, whole_qkv, whole_out, whole_up, whole_down = inbound(
        tokens,
        out_grad[0],
        slot_at[None],
        home_at[:, None],
        tables,
        codes,
        [shard_halves(shard) for shard in (wide_qkv, w_out, w_up, w_down)],
    )
    result, grad_one, grad_context, local_out, local_up, local_down, vec_grads = dense(
        homed, cotangent, context, vec, whole_out, whole_up, whole_down
    )
    layer_out, in_grad, table_sum, *ends = outbound(
        result,
        grad_one,
        qkv,
        grad_context,
        homed,
        vec_grads,
        home_at[None],
        slot_at[:, None],
        tables,
        codes,
        flipped,
        whole_qkv,
        [local_out, local_up, local_down],
    )
    grad_relative = lines_back(table_sum)
    grad_qkv, grad_out, grad_up, grad_down = [joined(end) for end in ends]
    grad_vectors = grad_qkv[:, 3 * model_dim : 3 * model_dim + kinds].T
    grad_qkv = grad_qkv[:, : 3 * model_dim]
    firsts_qkv, seconds_qkv, update_qkv = adam_step(
        w_qkv.astype(jnp.float32), grad_qkv, first_qkv, second_qkv, DECAY_RATE
    )
    firsts_out, seconds_out, update_out = adam_step(
        w_out.astype(jnp.float32), grad_out, first_out, second_out, DECAY_RATE
    )
    firsts_up, seconds_up, update_up = adam_step(
        w_up.astype(jnp.float32), grad_up, first_up, second_up, DECAY_RATE
    )
    firsts_down, seconds_down, update_down = adam_step(
        w_down.astype(jnp.float32), grad_down, first_down, second_down, DECAY_RATE
    )
    firsts_vectors, seconds_vectors, update_vectors = adam_step(
        vectors.astype(jnp.float32), grad_vectors, first_vectors, second_vectors, 0.0
    )
    firsts_relative, seconds_relative, update_relative = adam_step(
        relative, grad_relative, first_relative, second_relative, 0.0
    )
    return (
        layer_out[None],
        in_grad[None],
        grad_qkv,
        firsts_qkv,
        seconds_qkv,
        update_qkv,
        grad_out,
        firsts_out,
        seconds_out,
        update_out,
        grad_up,
        firsts_up,
        seconds_up,
        update_up,
        grad_down,
        firsts_down,
        seconds_down,
        update_down,
        grad_vectors,
        firsts_vectors,
        seconds_vectors,
        update_vectors,
        grad_relative,
        firsts_relative,
        seconds_relative,
        update_relative,
    )


def spread_device(
    layer_in,
    out_grad,
    w_qkv,
    w_out,
    w_up,
    w_down,
    vectors,
    relative,
    first_qkv,
    second_qkv,
    first_out,
    second_out,
    first_up,
    second_up,
    first_down,
    second_down,
    first_vectors,
    second_vectors,
    first_relative,
    second_relative,
    token_slot,
    home_index,
    box_x,
    box_y,
):
    tokens = layer_in[0]
    rows_dev = tokens.shape[0]
    model_dim = tokens.shape[1]
    groups = lax.axis_size("regions")
    slot_cap = 2 * rows_dev // groups
    page_num = rows_dev // PAGE
    slot_of = token_slot[0]
    home_rows = home_index[0]
    full_qkv, full_out, full_up, full_down, full_vec = (
        lax.all_gather(w_qkv, ("regions", "shard"), axis=0, tiled=True),
        lax.all_gather(w_out, ("regions", "shard"), axis=0, tiled=True),
        lax.all_gather(w_up, ("regions", "shard"), axis=0, tiled=True),
        lax.all_gather(w_down, ("regions", "shard"), axis=0, tiled=True),
        lax.all_gather(vectors, ("regions", "shard"), axis=1, tiled=True),
    )
    vec_rows = full_vec.astype(jnp.float32)
    qkv_bias = jnp.concatenate([vec_rows[0], jnp.zeros_like(vec_rows[0]), vec_rows[1]])
    code_rows = position_codes(box_x[0].reshape(page_num, PAGE), box_y[0].reshape(page_num, PAGE))
    bias_mats = bias_table(relative)
    homed = exchange(tokens, slot_of, home_rows, groups, slot_cap).astype(jnp.bfloat16)
    cotangent = exchange(out_grad[0], slot_of, home_rows, groups, slot_cap)
    projected = (jnp.dot(homed, full_qkv, preferred_element_type=jnp.float32) + qkv_bias).astype(
        jnp.bfloat16
    )
    paged = projected.reshape(page_num, PAGE, 3 * model_dim)
    context_pages, log_totals = lax.map(
        lambda member: page_forward(member[0], member[1], bias_mats), (paged, code_rows)
    )
    context = context_pages.reshape(rows_dev, model_dim)
    attn_out = jnp.dot(context, full_out, preferred_element_type=jnp.float32) + vec_rows[2]
    hidden, normed_one, spread_one = norm_forward(
        homed.astype(jnp.float32) + attn_out, vec_rows[3], vec_rows[4]
    )
    hidden_low = hidden.astype(jnp.bfloat16)
    pre_act = jnp.dot(hidden_low, full_up, preferred_element_type=jnp.float32) + vec_rows[
        8:12
    ].reshape(-1)
    activated, gelu_back = jax.vjp(lambda value: jax.nn.gelu(value, approximate=False), pre_act)
    act_low = activated.astype(jnp.bfloat16)
    branch = jnp.dot(act_low, full_down, preferred_element_type=jnp.float32) + vec_rows[5]
    result, normed_two, spread_two = norm_forward(hidden + branch, vec_rows[6], vec_rows[7])
    grad_two, grad_gain_two, grad_shift_two = norm_back(
        cotangent, normed_two, spread_two, vec_rows[6]
    )
    grad_branch = grad_two.astype(jnp.bfloat16)
    grad_down = jnp.einsum("tf,td->fd", act_low, grad_branch, preferred_element_type=jnp.float32)
    grad_act = jnp.einsum("td,fd->tf", grad_branch, full_down, preferred_element_type=jnp.float32)
    grad_pre = gelu_back(grad_act)[0].astype(jnp.bfloat16)
    grad_up = jnp.einsum("td,tf->df", hidden_low, grad_pre, preferred_element_type=jnp.float32)
    grad_hidden = grad_two + jnp.einsum(
        "tf,df->td", grad_pre, full_up, preferred_element_type=jnp.float32
    )
    grad_one, grad_gain_one, grad_shift_one = norm_back(
        grad_hidden, normed_one, spread_one, vec_rows[3]
    )
    grad_attn = grad_one.astype(jnp.bfloat16)
    grad_out = jnp.einsum("td,te->de", context, grad_attn, preferred_element_type=jnp.float32)
    grad_context = jnp.einsum(
        "te,de->td", grad_attn, full_out, preferred_element_type=jnp.float32
    ).astype(jnp.bfloat16)
    grad_home = grad_context.reshape(page_num, PAGE, model_dim)
    grad_pages, mats_pages = lax.map(
        lambda member: page_backward(member[0], member[1], member[2], member[3], bias_mats),
        (paged, code_rows, log_totals, grad_home),
    )
    grad_dense = grad_pages.reshape(rows_dev, 3 * model_dim)
    bias_sums = jnp.sum(grad_dense.astype(jnp.float32), axis=0)
    grad_qkv = jnp.einsum("td,tf->df", homed, grad_dense, preferred_element_type=jnp.float32)
    in_home = grad_one + jnp.einsum(
        "tf,df->td", grad_dense, full_qkv, preferred_element_type=jnp.float32
    )
    layer_out = exchange(result.astype(jnp.bfloat16), home_rows, slot_of, groups, slot_cap)
    in_grad = exchange(in_home.astype(jnp.bfloat16), home_rows, slot_of, groups, slot_cap)
    grad_vec = jnp.concatenate(
        [
            jnp.stack(
                [
                    bias_sums[:model_dim],
                    bias_sums[2 * model_dim :],
                    jnp.sum(grad_attn.astype(jnp.float32), axis=0),
                    grad_gain_one,
                    grad_shift_one,
                    jnp.sum(grad_branch.astype(jnp.float32), axis=0),
                    grad_gain_two,
                    grad_shift_two,
                ]
            ),
            jnp.sum(grad_pre.astype(jnp.float32), axis=0).reshape(4, model_dim),
        ],
        axis=0,
    )
    grad_qkv, grad_out, grad_up, grad_down, grad_vectors = (
        lax.psum_scatter(grad_qkv, ("regions", "shard"), scatter_dimension=0, tiled=True),
        lax.psum_scatter(grad_out, ("regions", "shard"), scatter_dimension=0, tiled=True),
        lax.psum_scatter(grad_up, ("regions", "shard"), scatter_dimension=0, tiled=True),
        lax.psum_scatter(grad_down, ("regions", "shard"), scatter_dimension=0, tiled=True),
        lax.psum_scatter(grad_vec, ("regions", "shard"), scatter_dimension=1, tiled=True),
    )
    mats_total = jnp.sum(mats_pages, axis=0)
    table_back = jax.vjp(bias_table, relative)[1]
    grad_relative = lax.psum(table_back(mats_total)[0], ("regions", "shard"))
    firsts_qkv, seconds_qkv, update_qkv = adam_step(
        w_qkv.astype(jnp.float32), grad_qkv, first_qkv, second_qkv, DECAY_RATE
    )
    firsts_out, seconds_out, update_out = adam_step(
        w_out.astype(jnp.float32), grad_out, first_out, second_out, DECAY_RATE
    )
    firsts_up, seconds_up, update_up = adam_step(
        w_up.astype(jnp.float32), grad_up, first_up, second_up, DECAY_RATE
    )
    firsts_down, seconds_down, update_down = adam_step(
        w_down.astype(jnp.float32), grad_down, first_down, second_down, DECAY_RATE
    )
    firsts_vectors, seconds_vectors, update_vectors = adam_step(
        vectors.astype(jnp.float32), grad_vectors, first_vectors, second_vectors, 0.0
    )
    firsts_relative, seconds_relative, update_relative = adam_step(
        relative, grad_relative, first_relative, second_relative, 0.0
    )
    return (
        layer_out.astype(jnp.bfloat16)[None],
        in_grad[None],
        grad_qkv,
        firsts_qkv,
        seconds_qkv,
        update_qkv,
        grad_out,
        firsts_out,
        seconds_out,
        update_out,
        grad_up,
        firsts_up,
        seconds_up,
        update_up,
        grad_down,
        firsts_down,
        seconds_down,
        update_down,
        grad_vectors,
        firsts_vectors,
        seconds_vectors,
        update_vectors,
        grad_relative,
        firsts_relative,
        seconds_relative,
        update_relative,
    )


def solution(mesh):
    kernels = mesh.shape["regions"] == PEERS and mesh.shape["shard"] == 2
    return jax.shard_map(
        per_device if kernels else spread_device,
        mesh=mesh,
        in_specs=(
            P("shard", "regions", None),
            P("shard", "regions", None),
            P(("regions", "shard"), None),
            P(("regions", "shard"), None),
            P(("regions", "shard"), None),
            P(("regions", "shard"), None),
            P(None, ("regions", "shard")),
            P(),
            P(("regions", "shard"), None),
            P(("regions", "shard"), None),
            P(("regions", "shard"), None),
            P(("regions", "shard"), None),
            P(("regions", "shard"), None),
            P(("regions", "shard"), None),
            P(("regions", "shard"), None),
            P(("regions", "shard"), None),
            P(None, ("regions", "shard")),
            P(None, ("regions", "shard")),
            P(),
            P(),
            P("shard", "regions"),
            P("shard", "regions"),
            P("shard", "regions"),
            P("shard", "regions"),
        ),
        out_specs=(
            P("shard", "regions", None),
            P("shard", "regions", None),
            P(("regions", "shard"), None),
            P(("regions", "shard"), None),
            P(("regions", "shard"), None),
            P(("regions", "shard"), None),
            P(("regions", "shard"), None),
            P(("regions", "shard"), None),
            P(("regions", "shard"), None),
            P(("regions", "shard"), None),
            P(("regions", "shard"), None),
            P(("regions", "shard"), None),
            P(("regions", "shard"), None),
            P(("regions", "shard"), None),
            P(("regions", "shard"), None),
            P(("regions", "shard"), None),
            P(("regions", "shard"), None),
            P(("regions", "shard"), None),
            P(None, ("regions", "shard")),
            P(None, ("regions", "shard")),
            P(None, ("regions", "shard")),
            P(None, ("regions", "shard")),
            P(),
            P(),
            P(),
            P(),
        ),
        check_vma=False,
    )
```

```python
import jax
import jax.numpy as jnp
import numpy as np
from jax import lax
from jax.experimental import pallas as pl
from jax.experimental.pallas import tpu as pltpu
from jax.sharding import PartitionSpec as P

HEADS = 12
HEAD = 64
PAGE = 576


PRECISE = lax.Precision.HIGHEST
EPS_NORM = 1e-05
BETA_ONE = 0.9
BETA_TWO = 0.999
ADAM_EPS = 1e-08
LAYER_FACTOR = 0.5625
DECAY_RATE = 0.05
STEP_COUNT = 10.0


def skewed(line, size):
    count = line.shape[0]
    wide = jnp.pad(line, ((0, 0), (0, 1)))
    flat = jnp.broadcast_to(wide[:, None, :], (count, size, 2 * size)).reshape(count, -1)
    rows = flat[:, : size * (2 * size - 1)].reshape(count, size, 2 * size - 1)
    return rows[:, :, size - 1 :]


def bias_table(relative):
    seq = skewed(relative[:, :127], 64)
    horizontal = skewed(relative[:, 127:190], 32)
    vertical = skewed(relative[:, 190:253], 32)
    return (
        jnp.pad(seq, ((0, 0), (0, 64), (0, 64)))
        + jnp.pad(horizontal, ((0, 0), (64, 32), (64, 32)))
        + jnp.pad(vertical, ((0, 0), (96, 0), (96, 0)))
    )


def position_codes(box_x, box_y):
    places = jnp.arange(PAGE, dtype=jnp.int32)
    seq_bucket = places * 64 // PAGE
    columns = jnp.arange(128, dtype=jnp.int32)
    matched = (
        (columns[None, None, :] == seq_bucket[None, :, None])
        | (columns == 64 + box_x[..., None])
        | (columns == 96 + box_y[..., None])
    )
    return matched.astype(jnp.float32)


def layout_bias(code_rows, bias_mats):
    lifted = jnp.einsum("pa,hab->hpb", code_rows, bias_mats, precision=PRECISE)
    return jnp.einsum("hpb,qb->hpq", lifted, code_rows, precision=PRECISE)


def page_scores(page_qkv, code_rows, bias_mats):
    parted = page_qkv.reshape(PAGE, 3, HEADS, HEAD)
    queries = parted[:, 0]
    key_rows = parted[:, 1]
    values = parted[:, 2]
    scores = jnp.einsum(
        "phd,qhd->hpq", queries, key_rows, preferred_element_type=jnp.float32
    ) * 0.125 + layout_bias(code_rows, bias_mats)
    return (queries, key_rows, values, scores)


def page_forward(page_qkv, code_rows, bias_mats):
    queries, key_rows, values, scores = page_scores(page_qkv, code_rows, bias_mats)
    row_max = jnp.max(scores, axis=2, keepdims=True)
    raised = jnp.exp(scores - row_max)
    totals = jnp.sum(raised, axis=2, keepdims=True)
    attn_w = (raised / totals).astype(jnp.bfloat16)
    context = jnp.einsum("hpq,qhd->phd", attn_w, values, preferred_element_type=jnp.float32)
    log_total = (row_max + jnp.log(totals))[..., 0]
    return (context.reshape(PAGE, HEADS * HEAD).astype(jnp.bfloat16), log_total)


def page_backward(page_qkv, code_rows, log_total, grad_ctx, bias_mats):
    queries, key_rows, values, scores = page_scores(page_qkv, code_rows, bias_mats)
    chances = jnp.exp(scores - log_total[..., None])
    attn_w = chances.astype(jnp.bfloat16)
    grad_heads = grad_ctx.reshape(PAGE, HEADS, HEAD)
    grad_values = jnp.einsum("hpq,phd->qhd", attn_w, grad_heads, preferred_element_type=jnp.float32)
    grad_chances = jnp.einsum(
        "phd,qhd->hpq", grad_heads, values, preferred_element_type=jnp.float32
    )
    inner = jnp.sum(chances * grad_chances, axis=2, keepdims=True)
    grad_scores = (chances * (grad_chances - inner)).astype(jnp.bfloat16)
    grad_queries = (
        jnp.einsum("hpq,qhd->phd", grad_scores, key_rows, preferred_element_type=jnp.float32)
        * 0.125
    )
    grad_keys = (
        jnp.einsum("hpq,phd->qhd", grad_scores, queries, preferred_element_type=jnp.float32) * 0.125
    )
    partial_codes = jnp.einsum(
        "hpq,qb->hpb",
        grad_scores,
        code_rows.astype(jnp.bfloat16),
        preferred_element_type=jnp.float32,
    )
    grad_mats = jnp.einsum("pa,hpb->hab", code_rows, partial_codes, precision=PRECISE)
    grad_page = jnp.stack([grad_queries, grad_keys, grad_values], axis=1).reshape(
        PAGE, 3 * HEADS * HEAD
    )
    return (grad_page.astype(jnp.bfloat16), grad_mats)


def exchange(rows, targets, picks, groups, slot_cap):
    slots = groups * slot_cap
    places = jnp.arange(slots, dtype=jnp.int32)
    packing = (places[:, None] == targets[None, :]).astype(jnp.bfloat16)
    packed = jnp.dot(packing, rows, preferred_element_type=jnp.float32).astype(jnp.bfloat16)
    arrived = lax.all_to_all(
        packed.reshape(groups, slot_cap, rows.shape[1]),
        "regions",
        split_axis=0,
        concat_axis=0,
        tiled=True,
    ).reshape(slots, rows.shape[1])
    picking = (picks[:, None] == places[None, :]).astype(jnp.bfloat16)
    return jnp.dot(picking, arrived, preferred_element_type=jnp.float32)


def norm_forward(rows, gain, shift):
    centre = rows - jnp.mean(rows, axis=-1, keepdims=True)
    spread = lax.rsqrt(jnp.mean(centre * centre, axis=-1, keepdims=True) + EPS_NORM)
    normed = centre * spread
    return (normed * gain + shift, normed, spread)


def norm_back(incoming, normed, spread, gain):
    scaled = incoming * gain
    grad_rows = spread * (
        scaled
        - jnp.mean(scaled, axis=-1, keepdims=True)
        - normed * jnp.mean(scaled * normed, axis=-1, keepdims=True)
    )
    return (grad_rows, jnp.sum(incoming * normed, axis=0), jnp.sum(incoming, axis=0))


def adam_step(param, grad, moment, square, decay):
    moment_new = BETA_ONE * moment + (1.0 - BETA_ONE) * grad
    square_new = BETA_TWO * square + (1.0 - BETA_TWO) * grad * grad
    moment_hat = moment_new / (1.0 - BETA_ONE**STEP_COUNT)
    square_hat = square_new / (1.0 - BETA_TWO**STEP_COUNT)
    update = LAYER_FACTOR * (moment_hat / (jnp.sqrt(square_hat) + ADAM_EPS) + decay * param)
    return (moment_new, square_new, update)


ROWS = 576


def softly(scores, axis):
    peak = jnp.max(scores, axis=axis, keepdims=True)
    raised = jnp.exp(scores - peak)
    return raised * (1.0 / jnp.sum(raised, axis=axis, keepdims=True))


def head_lift(tables, codes, h):
    line = tables[pl.ds(h, 1), :]
    lane = lax.broadcasted_iota(jnp.int32, (64, 128), 1)

    def spread(entry, size, low, high):
        if low == 0:
            start = pltpu.roll(line[:, :128], 128 - entry, 1)
        else:
            start = pltpu.roll(line, 256 - entry, 1)[:, :128]
        turned = pltpu.roll(jnp.broadcast_to(start, (size, 128)), 0, 1, stride=1, stride_axis=0)
        return jnp.where((lane[:size] >= low) & (lane[:size] < high), turned, 0.0)

    table = jnp.concatenate(
        [spread(63, 64, 0, 64), spread(94, 32, 64, 96), spread(125, 32, 96, 128)], axis=0
    )
    high = table.astype(jnp.bfloat16)
    low = (table - high.astype(jnp.float32)).astype(jnp.bfloat16)
    both = jnp.concatenate([high, low], axis=1)
    return jnp.dot(codes, both, preferred_element_type=jnp.float32).astype(jnp.bfloat16)


def lane_mask(rows, h):
    lane = lax.broadcasted_iota(jnp.int32, (rows, 128), 1)
    return (lane < 64) if h == 0 else (lane >= 64)


def pair_columns(qkv, pair):
    width = qkv.shape[1] // 3
    at = [pl.multiple_of(n * width + pair * 128, 128) for n in range(3)]
    return [qkv[:, pl.ds(a, 128)] for a in at]


NT = (((1,), (1,)), ((), ()))
TN = (((0,), (0,)), ((), ()))


def attend_pair(pair, qkv, tables, codes_ref, context):
    count = qkv.shape[0]
    codes = codes_ref[...]
    queries, keys, values = pair_columns(qkv, pair)
    right = jnp.concatenate([keys, codes, codes], axis=1)
    scaled = queries * jnp.bfloat16(0.125)
    results = []
    for h in range(2):
        mine = jnp.where(lane_mask(count, h), scaled, jnp.zeros_like(scaled))
        left = jnp.concatenate([mine, head_lift(tables, codes, 2 * pair + h)], axis=1)
        parts = []
        for r in range(0, count, ROWS):
            scores = lax.dot_general(left[r : r + ROWS], right, NT, preferred_element_type=jnp.float32)
            weights = softly(scores, 1).astype(jnp.bfloat16)
            parts.append(jnp.dot(weights, values, preferred_element_type=jnp.float32))
        results.append(parts)
    for n, r in enumerate(range(0, count, ROWS)):
        both = jnp.where(lane_mask(ROWS, 0), results[0][n], results[1][n])
        context[pl.ds(r, ROWS), pl.ds(pl.multiple_of(pair * 128, 128), 128)] = both.astype(jnp.bfloat16)


def attend_pair_back(pair, qkv, grad_ref, tables, codes_ref, flipped_ref, grad_qkv, grad_tables):
    count = qkv.shape[0]
    width = qkv.shape[1] // 3
    codes = codes_ref[...]
    queries, keys, values = pair_columns(qkv, pair)
    grads = grad_ref[:, pl.ds(pl.multiple_of(pair * 128, 128), 128)]
    left = jnp.concatenate([keys, codes, codes], axis=1)
    near = jnp.concatenate([keys, codes], axis=1)
    scaled = queries * jnp.bfloat16(0.125)
    out_q, out_k, out_v = [], [], []
    for h in range(2):
        mask = lane_mask(count, h)
        mine = jnp.where(mask, scaled, jnp.zeros_like(scaled))
        mine_grad = jnp.where(mask, grads, jnp.zeros_like(grads))
        right = jnp.concatenate([mine, head_lift(tables, codes, 2 * pair + h)], axis=1)
        total = None
        k_parts, v_parts = [], []
        if True:
            scores = lax.dot_general(left, right, NT, preferred_element_type=jnp.float32)
            chances = softly(scores, 0)
            grad_chances = lax.dot_general(values, mine_grad, NT, preferred_element_type=jnp.float32)
            inner = jnp.sum(chances * grad_chances, axis=0, keepdims=True)
            grad_scores = (chances * (grad_chances - inner)).astype(jnp.bfloat16)
            v_rows = jnp.dot(chances.astype(jnp.bfloat16), grads, preferred_element_type=jnp.float32)
            k_rows = jnp.dot(grad_scores, queries, preferred_element_type=jnp.float32)
            total = lax.dot_general(grad_scores, near, TN, preferred_element_type=jnp.float32)
        out_q.append(total[:, :128])
        out_k.append(k_rows)
        out_v.append(v_rows)
        partial = total[:, 128:]
        high = partial.astype(jnp.bfloat16)
        low = (partial - high.astype(jnp.float32)).astype(jnp.bfloat16)
        mats = lax.dot_general(
            flipped_ref[...], jnp.concatenate([high, low], axis=1), TN, preferred_element_type=jnp.float32
        )
        mats = mats[:, :128] + mats[:, 128:]
        lane = lax.broadcasted_iota(jnp.int32, (64, 128), 1)

        def gathered(row, size, low_lane, high_lane):
            part = jnp.where((lane[:size] >= low_lane) & (lane[:size] < high_lane), mats[row : row + size], 0.0)
            turned = pltpu.roll(part, 0, 1, stride=1, stride_axis=0)
            return jnp.sum(turned, axis=0, keepdims=True)

        blank = jnp.zeros((1, 128), jnp.float32)
        seq, across, down = [
            jnp.concatenate([part, blank], axis=1)
            for part in (gathered(0, 64, 0, 64), gathered(64, 32, 64, 96), pltpu.roll(gathered(96, 32, 96, 128), 32, 1))
        ]
        grad_tables[pl.ds(2 * pair + h, 1), :] = seq + pltpu.roll(across, 63, 1) + pltpu.roll(down, 190, 1)
    mask = lane_mask(count, 0)
    for n, (parts, factor) in enumerate(((out_q, 0.125), (out_k, 0.125), (out_v, 1.0))):
        both = jnp.where(mask, parts[0], parts[1]) * factor
        grad_qkv[:, pl.ds(pl.multiple_of(n * width + pair * 128, 128), 128)] = both.astype(jnp.bfloat16)


def code_rows_of(box_x, box_y, flip):
    count = box_x.shape[1]
    column = lax.broadcasted_iota(jnp.int32, (128, count), 0)
    row = lax.broadcasted_iota(jnp.int32, (128, count), 1)
    start = (63 - column if flip else column) * (count // 64)
    hit_seq = (column < 64) & (row >= start) & (row < start + count // 64)
    across, down = box_x[...], box_y[...]
    if flip:
        across, down = 31 - across, 31 - down
    hit = hit_seq | (column == 64 + across) | (column == 96 + down)
    return jnp.where(hit, 1.0, 0.0).T.astype(jnp.bfloat16)


def as_columns(line):
    wide = jnp.broadcast_to(line[...].astype(jnp.float32), (128, line.shape[1]))
    return wide.T.astype(jnp.int32)


MESH = pl.DeviceIdType.MESH
PEERS = 16
VEC_COLS = 256


def place():
    me = lax.axis_index("regions")
    core = lax.axis_index("shard")
    z = lax.div(me, 4)
    y = lax.div(lax.rem(me, 4), 2)
    x = lax.rem(me, 2)
    return me, core, z, y, x


def enter(me, core):
    barrier = pltpu.get_barrier_semaphore()
    for k in range(1, PEERS):
        pl.semaphore_signal(barrier, inc=1, device_id=(me ^ k, core), device_id_type=MESH)
    pl.semaphore_signal(barrier, inc=1, device_id=(me, 1 - core), device_id_type=MESH)
    pl.semaphore_wait(barrier, PEERS)


def remote(src, dst, send, recv, device):
    return pltpu.make_async_remote_copy(
        src_ref=src, dst_ref=dst, send_sem=send, recv_sem=recv, device_id=device, device_id_type=MESH
    )


class Exchange:
    def __init__(self, where, packed, arrived, loose, send, recv, local):
        self.me, self.core = where[0], where[1]
        self.packed, self.arrived, self.loose = packed, arrived, loose
        self.send, self.recv, self.local = send, recv, local
        self.slots, self.half = packed.shape[1], packed.shape[2]

    def pack(self, rows, slot_of):
        count = self.slots // 2
        for j in range(4):
            group = lax.div(self.me, 4) ^ j
            at = lax.broadcasted_iota(jnp.int32, (4 * count, rows.shape[0]), 0) + group * (4 * count)
            picking = jnp.where(at == slot_of[...], 1.0, 0.0).astype(jnp.bfloat16)
            block = jnp.dot(picking, rows[...], preferred_element_type=jnp.float32)
            for n in range(4):
                own = block[n * count : (n + 1) * count]
                both = jnp.concatenate([own[:, : self.half], own[:, self.half :]], axis=0)
                self.packed[4 * group + n] = both.astype(jnp.bfloat16)
            for k in range(4):
                if j + k:
                    self.copy(4 * j + k).start()
                else:
                    self.own().start()

    def copy(self, k):
        d = self.me ^ k
        return remote(
            self.packed.at[d], self.arrived.at[self.me], self.send.at[k], self.recv.at[k], (d, self.core)
        )

    def own(self):
        return pltpu.make_async_copy(self.packed.at[self.me], self.arrived.at[self.me], self.local)

    def wait(self):
        self.own().wait()

        def one(k, carry):
            self.copy(k).wait()
            return carry

        lax.fori_loop(1, PEERS, one, 0)

    def unpack(self, slot_of, out, kind):
        out[...] = unpacked(self.arrived, self.loose, slot_of).astype(kind)


def unpacked(arrived, loose, slot_of):
    count = arrived.shape[1] // 2
    rows = []
    for n in range(PEERS):
        block = arrived[n].astype(jnp.float32)
        rows.append(jnp.concatenate([block[:count], block[count:]], axis=1))
        if n % 2:
            pair = jnp.concatenate(rows, axis=0)
            loose[pl.ds((n - 1) * count, 2 * count)] = pair.astype(jnp.bfloat16)
            rows = []
    wanted = as_columns(slot_of)
    lane = lax.broadcasted_iota(jnp.int32, wanted.shape, 1)
    picking = jnp.concatenate(
        [
            jnp.where(lane + first == wanted, 1.0, 0.0).astype(jnp.bfloat16)
            for first in range(0, PEERS * count, 128)
        ],
        axis=1,
    )
    return jnp.dot(picking, loose[...], preferred_element_type=jnp.float32)


def pieces_of(rows, half):
    tiles = half // 128
    if rows % 64 == 0:
        cuts = [(n * rows // 4, rows // 4, 0, half) for n in range(4)]
    elif tiles < 4:
        wide = (tiles + 1) // 2 * 128
        cuts = [(0, rows, 0, wide), (0, rows, wide, half - wide)]
    else:
        ends = [0, (tiles + 3) // 4, tiles // 2, tiles - (tiles + 3) // 4, tiles]
        cuts = [(0, rows, 128 * ends[n], 128 * (ends[n + 1] - ends[n])) for n in range(4)]
    return [[(*cuts[n], True), (*cuts[n + 1], False)] for n in range(0, len(cuts), 2)]


class Gather:
    def __init__(self, where, whole, piece, sems):
        self.where, self.whole, self.piece, self.sems = where, whole, piece, sems

    def part(self, z, y, x):
        core = self.where[1]
        r0, rows, c0, cols, _ = self.piece
        half = self.whole.shape[4] // 2
        at = pl.multiple_of(core * half + c0, 128)
        return self.whole.at[z, y, x, pl.ds(r0, rows), pl.ds(at, cols)]

    def along_z(self, t, upward):
        me, core, z, y, x = self.where
        step = 1 if upward else -1
        origin = z - step * t
        ref = self.part(origin, y, x)
        i = 2 * t + (1 if upward else 0)
        return remote(ref, ref, self.sems.at[0, i], self.sems.at[1, i], (me + 4 * step, core))

    def z_sends(self, t, do):
        z = self.where[2]

        @pl.when((z >= t) & (z <= 2))
        def _():
            do(self.along_z(t, True))

        @pl.when((z + t <= 3) & (z >= 1))
        def _():
            do(self.along_z(t, False))

    def z_waits(self, t):
        z = self.where[2]

        @pl.when(z - 1 - t >= 0)
        def _():
            me, core, z, y, x = self.where
            ref = self.part(z - 1 - t, y, x)
            i = 2 * t + 1
            remote(ref, ref, self.sems.at[0, i], self.sems.at[1, i], (me, 1 - core)).wait_recv()

        @pl.when(z + 1 + t <= 3)
        def _():
            me, core, z, y, x = self.where
            ref = self.part(z + 1 + t, y, x)
            i = 2 * t
            remote(ref, ref, self.sems.at[0, i], self.sems.at[1, i], (me, 1 - core)).wait_recv()

    def plane(self, n):
        me, core, z, y, x = self.where
        x_first = self.piece[4]
        every = slice(None)
        other = (me, 1 - core)
        if n == 0:
            ref, device = self.part(every, y, x), (me ^ (1 if x_first else 2), core)
        elif n == 1 and x_first:
            ref, device = self.part(every, y, every), (me ^ 2, core)
        elif n == 1:
            ref, device = self.part(every, every, x), (me ^ 1, core)
        elif n == 2:
            ref, device = self.part(every, y, x), other
        elif n == 3:
            ref, device = (self.part(every, y, 1 - x) if x_first else self.part(every, 1 - y, x)), other
        else:
            ref, device = (self.part(every, 1 - y, every) if x_first else self.part(every, every, 1 - x)), other
        return remote(ref, ref, self.sems.at[0, 6 + n], self.sems.at[1, 6 + n], device)

    def run(self, stage):
        if stage < 3:
            if stage:
                self.z_waits(stage - 1)
            self.z_sends(stage, lambda copy: copy.start())
        elif stage == 3:
            self.z_waits(2)
            self.plane(0).start()
            self.plane(2).start()
        elif stage == 4:
            self.plane(0).wait_recv()
            self.plane(1).start()
            self.plane(3).start()
        elif stage == 5:
            self.plane(1).wait_recv()
            self.plane(4).start()
        else:
            for n in (2, 3, 4):
                self.plane(n).wait_recv()

    def sent(self):
        for t in range(3):
            self.z_sends(t, lambda copy: copy.wait_send())
        for n in range(5):
            self.plane(n).wait_send()


class Scatter:
    def __init__(self, where, local, sums, from_core, from_near, from_far, from_z, fetch, piece, sems):
        self.where, self.local, self.sums, self.piece, self.sems = where, local, sums, piece, sems
        self.from_core, self.from_near, self.from_far, self.from_z = from_core, from_near, from_far, from_z
        self.half, self.fetch = sums.shape[4], fetch

    def cut(self, ref, *lead, core=None):
        r0, rows, c0, cols, _ = self.piece
        at = c0 if core is None else pl.multiple_of(core * self.half + c0, 128)
        return ref.at[(*lead, pl.ds(r0, rows), pl.ds(at, cols))]

    def between_cores(self):
        me, core = self.where[0], self.where[1]
        every = slice(None)
        src = self.cut(self.local, every, every, every, core=1 - core)
        dst = self.cut(self.from_core, every, every, every)
        return remote(src, dst, self.sems.at[0, 0], self.sems.at[1, 0], (me, 1 - core))

    def own_half(self):
        every = slice(None)
        src = self.cut(self.local, every, every, every, core=self.where[1])
        return pltpu.make_async_copy(src, self.cut(self.sums, every, every, every), self.fetch)

    def near(self):
        me, core, z, y, x = self.where
        every = slice(None)
        if self.piece[4]:
            src, device = self.cut(self.sums, every, 1 - y, every), (me ^ 2, core)
        else:
            src, device = self.cut(self.sums, every, every, 1 - x), (me ^ 1, core)
        dst = self.cut(self.from_near, every, every)
        return remote(src, dst, self.sems.at[0, 1], self.sems.at[1, 1], device)

    def far(self):
        me, core, z, y, x = self.where
        every = slice(None)
        if self.piece[4]:
            src, device = self.cut(self.sums, every, y, 1 - x), (me ^ 1, core)
        else:
            src, device = self.cut(self.sums, every, 1 - y, x), (me ^ 2, core)
        dst = self.cut(self.from_far, every)
        return remote(src, dst, self.sems.at[0, 2], self.sems.at[1, 2], device)

    def along_z(self, sender, upward):
        me, core, z, y, x = self.where
        lead = pl.ds(sender + 1, 3 - sender) if upward else pl.ds(0, sender)
        src = self.cut(self.sums, lead, y, x)
        dst = self.cut(self.from_z, 1 if upward else 0, lead)
        i = 3 + (1 if upward else 0)
        step = 4 if upward else -4
        return remote(src, dst, self.sems.at[0, i], self.sems.at[1, i], (me + step, core))

    def add(self, target, other):
        total = target[...].astype(jnp.float32) + other[...].astype(jnp.float32)
        target[...] = total.astype(jnp.bfloat16)

    def z_got(self, sender, upward):
        me, core, z, y, x = self.where
        self.along_z(sender, upward).wait_recv()
        for d in range(sender + 1, 4) if upward else range(sender):
            self.add(self.cut(self.sums, d, y, x), self.cut(self.from_z, 1 if upward else 0, d))

    def run(self, stage):
        me, core, z, y, x = self.where
        if stage == 0:
            self.between_cores().start()
            self.own_half().start()
        elif stage == 1:
            self.own_half().wait()
            self.between_cores().wait_recv()

            def one(i, carry):
                a, b, c = lax.div(i, 4), lax.div(lax.rem(i, 4), 2), lax.rem(i, 2)
                self.add(self.cut(self.sums, a, b, c), self.cut(self.from_core, a, b, c))
                return carry

            lax.fori_loop(0, 16, one, 0)
            self.near().start()
        elif stage == 2:
            self.near().wait_recv()

            def one(i, carry):
                a, b = lax.div(i, 2), lax.rem(i, 2)
                target = self.cut(self.sums, a, y, b) if self.piece[4] else self.cut(self.sums, a, b, x)
                self.add(target, self.cut(self.from_near, a, b))
                return carry

            lax.fori_loop(0, 8, one, 0)
            self.far().start()
        elif stage == 3:
            self.far().wait_recv()

            def one(i, carry):
                self.add(self.cut(self.sums, i, y, x), self.cut(self.from_far, i))
                return carry

            lax.fori_loop(0, 4, one, 0)

            @pl.when(z == 3)
            def _():
                self.along_z(3, False).start()

            @pl.when(z == 0)
            def _():
                self.along_z(0, True).start()

        elif stage == 4:

            @pl.when(z == 2)
            def _():
                self.z_got(3, False)
                self.along_z(2, False).start()

            @pl.when(z == 1)
            def _():
                self.z_got(0, True)
                self.along_z(1, True).start()

        elif stage == 5:

            @pl.when(z == 1)
            def _():
                self.z_got(2, False)
                self.along_z(1, False).start()

            @pl.when(z == 2)
            def _():
                self.z_got(1, True)
                self.along_z(2, True).start()

        elif stage == 6:

            @pl.when(z == 0)
            def _():
                self.z_got(1, False)

            @pl.when(z == 3)
            def _():
                self.z_got(2, True)

    def sent(self):
        z = self.where[2]
        self.between_cores().wait_send()
        self.near().wait_send()
        self.far().wait_send()
        for sender in range(4):

            @pl.when(z == sender)
            def _(sender=sender):
                if sender > 0:
                    self.along_z(sender, False).wait_send()
                if sender < 3:
                    self.along_z(sender, True).wait_send()


def stepper(tasks):
    def step(k):
        for pair, plan in tasks:
            if k in plan:
                for task in pair:
                    task.run(plan.index(k))

    return step, max(plan[-1] for _, plan in tasks) + 1


def normed_rows(rows):
    centre = rows - jnp.mean(rows, axis=-1, keepdims=True)
    spread = lax.rsqrt(jnp.mean(centre * centre, axis=-1, keepdims=True) + EPS_NORM)
    return centre * spread, spread


def dense_part(
    homed, cotangent, context, vec, w_out, w_up, w_down,
    result, grad_one_ref, grad_context, g_out, g_up, g_down, vec_grads,
    act, slope, hidden_low, fetch,
):
    width = homed.shape[1]
    chunks = w_up.shape[4] // width
    f32 = jnp.float32
    low = jnp.bfloat16

    def columns(ref, c):
        return ref[:, :, :, :, c * width : (c + 1) * width].reshape(width, width)

    def keep(n, line):
        vec_grads[n : n + 1] = jnp.sum(line, axis=0, keepdims=True)

    attn_out = jnp.dot(context[...], columns(w_out, 0), preferred_element_type=f32) + vec[2:3]
    normed_one, spread_one = normed_rows(homed[...].astype(f32) + attn_out)
    hidden = normed_one * vec[3:4] + vec[4:5]
    hidden_low[...] = hidden.astype(low)
    branch = None
    for c in range(chunks):
        pre = jnp.dot(hidden_low[...], columns(w_up, c), preferred_element_type=f32) + vec[8 + c : 9 + c]
        below = 0.5 * (1.0 + lax.erf(pre * 0.7071067811865476))
        act[c] = (pre * below).astype(low)
        slope[c] = below + pre * (jnp.exp(-0.5 * pre * pre) * 0.3989422804014327)
        part = jnp.dot(act[c], w_down[c].reshape(width, width), preferred_element_type=f32)
        branch = part if branch is None else branch + part
    normed_two, spread_two = normed_rows(hidden + branch + vec[5:6])
    result[...] = (normed_two * vec[6:7] + vec[7:8]).astype(low)

    def back(e, normed, spread, gain):
        scaled = e * gain
        return spread * (
            scaled
            - jnp.mean(scaled, axis=-1, keepdims=True)
            - normed * jnp.mean(scaled * normed, axis=-1, keepdims=True)
        )

    fetch()
    e = cotangent[...].astype(f32)
    keep(6, e * normed_two)
    keep(7, e)
    grad_two = back(e, normed_two, spread_two, vec[6:7])
    grad_branch = grad_two.astype(low)
    keep(5, grad_branch.astype(f32))
    grad_hidden = grad_two
    for c in range(chunks):
        g_down[c] = (
            lax.dot_general(act[c], grad_branch, TN, preferred_element_type=f32)
            .astype(low)
            .reshape(g_down.shape[1:])
        )
        grad_act = lax.dot_general(
            grad_branch, w_down[c].reshape(width, width), NT, preferred_element_type=f32
        )
        grad_pre = (grad_act * slope[c]).astype(low)
        keep(8 + c, grad_pre.astype(f32))
        g_up[:, :, :, :, c * width : (c + 1) * width] = (
            lax.dot_general(hidden_low[...], grad_pre, TN, preferred_element_type=f32)
            .astype(low)
            .reshape(*g_up.shape[:4], width)
        )
        grad_hidden = grad_hidden + lax.dot_general(
            grad_pre, columns(w_up, c), NT, preferred_element_type=f32
        )
    keep(3, grad_hidden * normed_one)
    keep(4, grad_hidden)
    grad_one = back(grad_hidden, normed_one, spread_one, vec[3:4])
    grad_one_ref[...] = grad_one
    grad_attn = grad_one.astype(low)
    keep(2, grad_attn.astype(f32))
    g_out[...] = (
        lax.dot_general(context[...], grad_attn, TN, preferred_element_type=f32)
        .astype(low)
        .reshape(g_out.shape)
    )
    grad_context[...] = lax.dot_general(
        grad_attn, columns(w_out, 0), NT, preferred_element_type=f32
    ).astype(low)
    vec_grads[0:2] = jnp.zeros((2, width), f32)
    vec_grads[12:] = jnp.zeros((vec_grads.shape[0] - 12, width), f32)


PAIRS = 6
READY = 8
SEND_ROWS = 4


def gather_plan(n, early):
    z, wide = n // 2, 3 + n
    if early:
        return (z, z + 1, z + 2, wide, wide + 1, wide + 2, wide + 3)
    return (z, z + 1, z + 2, wide, wide + 2, wide + 4, wide + 6)


def split_shard(shard, halves, beside=None):
    rows, half = shard.shape[0], halves.shape[2]
    halves[...] = jnp.zeros_like(halves)
    halves[0, :rows] = shard[:, :half]
    if beside is None:
        halves[1, :rows] = shard[:, half:]
    else:
        rest = shard.shape[1] - half
        halves[1, :rows, :rest] = shard[:, half:]
        halves[1, :rows, rest : rest + 128] = beside


def inbound_kernel(
    rows_ref, grad_ref, slot_line, home_line, box_x, box_y, tables, r_qkv, r_out, r_up, r_down, r_vec,
    homed, qkv, w_qkv, codes, flipped, result, grad_one, grad_context, g_out, g_up, g_down, vec_grads,
    cotangent, context, vec_rows, w_out, w_up, w_down, act, slope, hidden_low, square,
    s_qkv, s_out, s_up, s_down,
    packed, arrived_a, arrived_b, loose, p_qkv, p_out, p_up, p_down, b_qkv, b_out, b_up, b_down,
    send_a, recv_a, send_b, recv_b, local_sems, pair_sems, block_sems, piece_sems,
):
    where = place()
    me, core, z, y, x = where
    shards = (s_qkv, s_out, s_up, s_down)
    others = (p_qkv, p_out, p_up, p_down)
    blocks = (b_qkv, b_out, b_up, b_down)
    wholes = (w_qkv, w_out, w_up, w_down)
    square[...] = jnp.zeros_like(square)
    square[: r_vec.shape[0], : r_vec.shape[1]] = r_vec[...].astype(jnp.float32)
    split_shard(r_qkv, s_qkv, square[...].T[: r_qkv.shape[0]].astype(jnp.bfloat16))
    split_shard(r_out, s_out)
    split_shard(r_up, s_up)
    split_shard(r_down, s_down)
    enter(me, core)
    pairs = [
        remote(shards[i].at[1 - core], others[i], pair_sems.at[0, i], pair_sems.at[1, i], (me, 1 - core))
        for i in range(4)
    ]
    for pair in pairs:
        pair.start()
    codes[...] = code_rows_of(box_x, box_y, False)
    flipped[...] = code_rows_of(box_x, box_y, True)
    moved = Exchange(where, packed, arrived_a, loose, send_a, recv_a, local_sems.at[0])
    moved_grad = Exchange(where, packed, arrived_b, loose, send_b, recv_b, local_sems.at[1])
    placed = []
    tasks = []
    for i in range(4):
        pairs[i].wait_recv()
        half = blocks[i].shape[1]
        rows = blocks[i].shape[0] // 2
        mine = shards[i][core][:rows].astype(jnp.float32)
        other = others[i][:rows].astype(jnp.float32)
        first = jnp.where(core == 0, mine, other)
        second = jnp.where(core == 0, other, mine)
        blocks[i][...] = jnp.concatenate([first, second], axis=0).astype(jnp.bfloat16)
        at = pl.multiple_of(core * half, 128)
        copy = pltpu.make_async_copy(
            blocks[i], wholes[i].at[z, y, x, :, pl.ds(at, half)], block_sems.at[i]
        )
        copy.start()
        placed.append(copy)
    for i in range(4):
        placed[i].wait()
        for pair in pieces_of(blocks[i].shape[0], blocks[i].shape[1]):
            n = len(tasks)
            pair = [Gather(where, wholes[i], piece, piece_sems.at[2 * n + j]) for j, piece in enumerate(pair)]
            tasks.append((pair, gather_plan(n, i == 0)))
    step, steps = stepper(tasks)

    for k in range(READY):
        step(k)
        if k == SEND_ROWS:
            moved.pack(rows_ref, slot_line)
    moved.wait()
    moved.unpack(home_line, homed, jnp.bfloat16)
    moved_grad.pack(grad_ref, slot_line)
    width = homed.shape[1]
    columns = w_qkv[:, :, :, :, 3 * width : 3 * width + 128].reshape(width, 128)
    vec_rows[...] = columns.astype(jnp.float32).T[: vec_rows.shape[0]]
    for n in range(3):
        part = w_qkv[:, :, :, :, n * width : (n + 1) * width].reshape(width, width)
        projected = jnp.dot(homed[...], part, preferred_element_type=jnp.float32)
        if n != 1:
            projected = projected + vec_rows[n // 2 : n // 2 + 1]
        qkv[:, n * width : (n + 1) * width] = projected.astype(jnp.bfloat16)

    def one(pair, carry):
        attend_pair(pair, qkv, tables, codes, context)
        for j in range(PAIRS):

            @pl.when(pair == j)
            def _(j=j):
                step(READY + j)

        return carry

    lax.fori_loop(0, PAIRS, one, 0)
    for k in range(READY + PAIRS, steps):
        step(k)

    def fetch():
        moved_grad.wait()
        moved_grad.unpack(home_line, cotangent, jnp.bfloat16)

    dense_part(
        homed, cotangent, context, vec_rows, w_out, w_up, w_down,
        result, grad_one, grad_context, g_out, g_up, g_down, vec_grads,
        act, slope, hidden_low, fetch,
    )
    for pair in pairs:
        pair.wait_send()
    for pair, _ in tasks:
        for task in pair:
            task.sent()


def vmem(count):
    return [pl.BlockSpec(memory_space=pltpu.VMEM)] * count


def inbound(rows, grads, slot_line, home_line, box_x, box_y, tables, shards, vectors):
    tokens, width = rows.shape
    slots = 2 * (2 * tokens // PEERS)
    low, f32 = jnp.bfloat16, jnp.float32
    buffer = pltpu.VMEM((PEERS, slots, width // 2), low)
    wholes, halves, pair_shapes, block_shapes = [], [], [], []
    for n, shard in enumerate(shards):
        count, columns = shard.shape
        half = (columns + (VEC_COLS if n == 0 else 0)) // 2
        padded = count + -count % 16
        wholes.append((4, 2, 2, 2 * count, 2 * half))
        halves.append(pltpu.VMEM((2, padded, half), low))
        pair_shapes.append(pltpu.VMEM((padded, half), low))
        block_shapes.append(pltpu.VMEM((2 * count, half), low))
    chunks = wholes[2][4] // width
    dma = pltpu.SemaphoreType.DMA

    def array(shape, kind=low):
        return jax.ShapeDtypeStruct(shape, kind)

    return pl.pallas_call(
        inbound_kernel,
        out_shape=[
            array((tokens, width)),
            array((tokens, 3 * width)),
            array(wholes[0]),
            array((tokens, 128)),
            array((tokens, 128)),
            array((tokens, width)),
            array((tokens, width), f32),
            array((tokens, width)),
            *[array(shape) for shape in wholes[1:]],
            array((128, width), f32),
        ],
        in_specs=vmem(12),
        out_specs=vmem(12),
        scratch_shapes=[
            pltpu.VMEM((tokens, width), low),
            pltpu.VMEM((tokens, width), low),
            pltpu.VMEM((16, width), f32),
            *[pltpu.VMEM(shape, low) for shape in wholes[1:]],
            pltpu.VMEM((chunks, tokens, width), low),
            pltpu.VMEM((chunks, tokens, width), f32),
            pltpu.VMEM((tokens, width), low),
            pltpu.VMEM((128, 128), f32),
        ]
        + halves
        + [buffer] * 3
        + [pltpu.VMEM((PEERS * (slots // 2), width), low)]
        + pair_shapes
        + block_shapes
        + [dma((PEERS,)), dma((PEERS,)), dma((PEERS,)), dma((PEERS,)), dma((2,)), dma((2, 4)), dma((4,)), dma((14, 2, 11))],
        compiler_params=pltpu.CompilerParams(
            collective_id=1, has_side_effects=True, vmem_limit_bytes=62 << 20
        ),
        name="inbound",
    )(rows, grads, slot_line, home_line, box_x, box_y, tables, *shards, vectors)


LAST = 7


def scatter_plan(n, late):
    if late:
        return tuple(range(LAST, LAST + 7))
    return (n // 2, 3 + n, 5 + n, 7 + n, 8 + n, 9 + n, 10 + n)


def outbound_kernel(
    result_ref, grad_one, qkv, grad_context, homed, vec_grads, home_line, slot_line, tables, codes, flipped,
    w_qkv, g_out, g_up, g_down,
    result_out, arrived_b, table_out, o_qkv, o_out, o_up, o_down,
    packed, arrived_a, loose, table_got, grad_qkv, g_qkv,
    t_qkv, t_out, t_up, t_down, c_qkv, c_out, c_up, c_down, n_qkv, n_out, n_up, n_down,
    f_qkv, f_out, f_up, f_down, z_qkv, z_out, z_up, z_down, e_qkv, e_out, e_up, e_down,
    send_a, recv_a, send_b, recv_b, local_sems, table_sems, piece_sems, fetch_sems, last_sems,
):
    where = place()
    me, core, z, y, x = where
    enter(me, core)
    local = (g_qkv, g_out, g_up, g_down)
    sums = (t_qkv, t_out, t_up, t_down)
    from_core = (c_qkv, c_out, c_up, c_down)
    from_near = (n_qkv, n_out, n_up, n_down)
    from_far = (f_qkv, f_out, f_up, f_down)
    from_z = (z_qkv, z_out, z_up, z_down)
    ends = (e_qkv, e_out, e_up, e_down)
    outs = (o_qkv, o_out, o_up, o_down)
    low = jnp.bfloat16
    tasks = []
    for i in (3, 2, 1, 0):
        refs = (local[i], sums[i], from_core[i], from_near[i], from_far[i], from_z[i])
        for pair in pieces_of(sums[i].shape[3], sums[i].shape[4]):
            n = len(tasks)
            pair = [
                Scatter(where, *refs, fetch_sems.at[2 * n + j], piece, piece_sems.at[2 * n + j])
                for j, piece in enumerate(pair)
            ]
            tasks.append((pair, scatter_plan(n, i == 0)))
    step, steps = stepper(tasks)
    moved = Exchange(where, packed, arrived_a, loose, send_a, recv_a, local_sems.at[0])
    moved_grad = Exchange(where, packed, arrived_b, loose, send_b, recv_b, local_sems.at[1])
    devices = [(me, 1 - core), (me ^ 1, core), (me ^ 2, core), (me ^ 4, core), (me ^ 8, core)]
    shares = [
        remote(table_got.at[0, n], table_got.at[1, n], table_sems.at[0, n], table_sems.at[1, n], device)
        for n, device in enumerate(devices)
    ]

    table_out[...] = jnp.zeros_like(table_out)
    step(0)
    moved.pack(result_ref, home_line)

    def one(pair, carry):
        attend_pair_back(pair, qkv, grad_context, tables, codes, flipped, grad_qkv, table_out)
        for j in range(PAIRS):

            @pl.when(pair == j)
            def _(j=j):
                step(1 + j)

        return carry

    lax.fori_loop(0, PAIRS, one, 0)
    width = homed.shape[1]
    sums_of = []
    in_home = grad_one[...]
    for n in range(3):
        part = grad_qkv[:, n * width : (n + 1) * width]
        g_qkv[:, :, :, :, n * width : (n + 1) * width] = (
            lax.dot_general(homed[...], part, TN, preferred_element_type=jnp.float32)
            .astype(low)
            .reshape(*g_qkv.shape[:4], width)
        )
        sums_of.append(jnp.sum(part.astype(jnp.float32), axis=0, keepdims=True))
        weights = w_qkv[:, :, :, :, n * width : (n + 1) * width].reshape(width, width)
        in_home = in_home + lax.dot_general(part, weights, NT, preferred_element_type=jnp.float32)
    row = lax.broadcasted_iota(jnp.int32, (128, width), 0)
    lines = jnp.where(row == 0, sums_of[0], jnp.where(row == 1, sums_of[2], vec_grads[...]))
    beside = lines.T.astype(low).reshape(*g_qkv.shape[:4], 128)
    g_qkv[:, :, :, :, 3 * width : 3 * width + 128] = beside
    g_qkv[:, :, :, :, 3 * width + 128 :] = jnp.zeros_like(beside)
    step(LAST)
    moved.wait()
    moved_grad.pack(in_home.astype(low), home_line)
    moved.unpack(slot_line, result_out, low)
    for k in range(LAST + 1, steps):
        step(k)
        n = k - LAST - 1
        if 0 < n <= 5:
            shares[n - 1].wait_recv()
            table_out[...] += table_got[1, n - 1]
        if n < 5:
            table_got[0, n] = table_out[...]
            shares[n].start()
    finals = []
    for i in (3, 2, 1, 0):
        block = sums[i][z, y, x].astype(jnp.float32)
        rows = block.shape[0] // 2
        ends[i][0] = block[:rows]
        ends[i][1] = block[rows:]
        outs[i][core] = ends[i][core]
        copy = remote(ends[i].at[1 - core], outs[i].at[core], last_sems.at[0, i], last_sems.at[1, i], (me, 1 - core))
        copy.start()
        finals.append(copy)
    moved_grad.wait()
    for copy in finals:
        copy.wait()
    for share in shares:
        share.wait_send()
    for pair, _ in tasks:
        for task in pair:
            task.sent()


def outbound(result, grad_one, qkv, grad_context, homed, vec_grads, home_line, slot_line, tables, codes, flipped, w_qkv, locals_):
    tokens, width = result.shape
    slots = 2 * (2 * tokens // PEERS)
    low = jnp.bfloat16
    buffer = pltpu.VMEM((PEERS, slots, width // 2), low)
    halves = [(g.shape[3], g.shape[4] // 2) for g in (w_qkv, *locals_)]
    scratch = (
        [buffer] * 2
        + [pltpu.VMEM((PEERS * (slots // 2), width), low)]
        + [pltpu.VMEM((2, 5, *tables.shape), jnp.float32)]
        + [pltpu.VMEM(qkv.shape, low), pltpu.VMEM(w_qkv.shape, low)]
        + [pltpu.VMEM((4, 2, 2, r, h), low) for r, h in halves]
        + [pltpu.VMEM((4, 2, 2, r, h), low) for r, h in halves]
        + [pltpu.VMEM((4, 2, r, h), low) for r, h in halves]
        + [pltpu.VMEM((4, r, h), low) for r, h in halves]
        + [pltpu.VMEM((2, 4, r, h), low) for r, h in halves]
        + [pltpu.VMEM((2, r // 2, h), jnp.float32) for r, h in halves]
    )
    dma = pltpu.SemaphoreType.DMA
    return pl.pallas_call(
        outbound_kernel,
        out_shape=[
            jax.ShapeDtypeStruct(result.shape, low),
            jax.ShapeDtypeStruct((PEERS, slots, width // 2), low),
            jax.ShapeDtypeStruct(tables.shape, jnp.float32),
        ]
        + [jax.ShapeDtypeStruct((2, r // 2, h), jnp.float32) for r, h in halves],
        in_specs=vmem(12) + [pl.BlockSpec(memory_space=pl.ANY)] * 3,
        out_specs=vmem(7),
        scratch_shapes=scratch
        + [dma((PEERS,)), dma((PEERS,)), dma((PEERS,)), dma((PEERS,)), dma((2,)), dma((2, 5)), dma((14, 2, 5)), dma((14,)), dma((2, 4))],
        compiler_params=pltpu.CompilerParams(
            collective_id=2, has_side_effects=True, vmem_limit_bytes=62 << 20
        ),
        name="outbound",
    )(result, grad_one, qkv, grad_context, homed, vec_grads, home_line, slot_line, tables, codes, flipped, w_qkv, *locals_)


def finish_kernel(
    arrived, slot_line, moved_rows, table_sum, e_qkv, e_out, e_up, e_down, p_qkv, p_out, p_up, p_down, p_vec, p_rel,
    m_qkv, m_out, m_up, m_down, m_vec, m_rel, v_qkv, v_out, v_up, v_down, v_vec, v_rel,
    layer_out, in_grad, a_qkv, a_out, a_up, a_down, a_vec, a_rel, f_qkv, f_out, f_up, f_down, f_vec, f_rel,
    s_qkv, s_out, s_up, s_down, s_vec, s_rel, u_qkv, u_out, u_up, u_down, u_vec, u_rel, loose,
):
    layer_out[...] = moved_rows[...]
    in_grad[...] = unpacked(arrived, loose, slot_line)
    ends = (e_qkv, e_out, e_up, e_down)
    params = (p_qkv, p_out, p_up, p_down, p_vec, p_rel)
    moments = (m_qkv, m_out, m_up, m_down, m_vec, m_rel)
    squares = (v_qkv, v_out, v_up, v_down, v_vec, v_rel)
    grads = (a_qkv, a_out, a_up, a_down, a_vec, a_rel)
    firsts = (f_qkv, f_out, f_up, f_down, f_vec, f_rel)
    seconds = (s_qkv, s_out, s_up, s_down, s_vec, s_rel)
    updates = (u_qkv, u_out, u_up, u_down, u_vec, u_rel)

    def adam(i, grad, columns):
        rate = DECAY_RATE if i < 4 else 0.0
        param = params[i][:, columns].astype(jnp.float32)
        new = adam_step(param, grad, moments[i][:, columns], squares[i][:, columns], rate)
        for ref, value in zip((grads[i], firsts[i], seconds[i], updates[i]), (grad, *new)):
            ref[:, columns] = value

    for i in range(4):
        half = ends[i].shape[2]
        width = params[i].shape[1]
        adam(i, ends[i][0], slice(0, half))
        adam(i, ends[i][1][:, : width - half], slice(half, width))
    kinds, features = params[4].shape
    rest = params[0].shape[1] - ends[0].shape[2]
    turned = ends[0][1][:, rest : rest + 128].T
    adam(4, turned[:kinds], slice(0, features))
    heads, entries = params[5].shape
    adam(5, table_sum[:heads, :entries], slice(0, entries))


def finish(arrived, slot_line, moved_rows, table_sum, ends, params, moments, squares):
    f32 = jnp.float32
    tokens, width = moved_rows.shape
    like = [jax.ShapeDtypeStruct(param.shape, f32) for param in params]
    return pl.pallas_call(
        finish_kernel,
        out_shape=[
            jax.ShapeDtypeStruct((tokens, width), jnp.bfloat16),
            jax.ShapeDtypeStruct((tokens, width), f32),
        ]
        + like * 4,
        in_specs=vmem(4 + 4 + 18),
        out_specs=vmem(2 + 24),
        scratch_shapes=[pltpu.VMEM((PEERS * (arrived.shape[1] // 2), width), jnp.bfloat16)],
        compiler_params=pltpu.CompilerParams(vmem_limit_bytes=60 << 20),
        name="finish",
    )(arrived, slot_line, moved_rows, table_sum, *ends, *params, *moments, *squares)


def per_device(
    layer_in,
    out_grad,
    w_qkv,
    w_out,
    w_up,
    w_down,
    vectors,
    relative,
    first_qkv,
    second_qkv,
    first_out,
    second_out,
    first_up,
    second_up,
    first_down,
    second_down,
    first_vectors,
    second_vectors,
    first_relative,
    second_relative,
    token_slot,
    home_index,
    box_x,
    box_y,
):
    heads, entries = relative.shape
    tables = jnp.pad(relative, ((0, -heads % 8), (0, -entries % 128)))
    homed, qkv, whole_qkv, codes, flipped, result, grad_one, grad_context, *local_grads, vec_grads = inbound(
        layer_in[0],
        out_grad[0],
        token_slot,
        home_index,
        box_x,
        box_y,
        tables,
        [w_qkv, w_out, w_up, w_down],
        vectors,
    )
    moved_rows, arrived, table_sum, *ends = outbound(
        result,
        grad_one,
        qkv,
        grad_context,
        homed,
        vec_grads,
        home_index,
        token_slot,
        tables,
        codes,
        flipped,
        whole_qkv,
        local_grads,
    )
    layer_out, in_grad, *new = finish(
        arrived,
        token_slot,
        moved_rows,
        table_sum,
        ends,
        [w_qkv, w_out, w_up, w_down, vectors, relative],
        [first_qkv, first_out, first_up, first_down, first_vectors, first_relative],
        [second_qkv, second_out, second_up, second_down, second_vectors, second_relative],
    )
    by_weight = [new[6 * kind + i] for i in range(6) for kind in range(4)]
    return (layer_out[None], in_grad[None], *by_weight)


def spread_device(
    layer_in,
    out_grad,
    w_qkv,
    w_out,
    w_up,
    w_down,
    vectors,
    relative,
    first_qkv,
    second_qkv,
    first_out,
    second_out,
    first_up,
    second_up,
    first_down,
    second_down,
    first_vectors,
    second_vectors,
    first_relative,
    second_relative,
    token_slot,
    home_index,
    box_x,
    box_y,
):
    tokens = layer_in[0]
    rows_dev = tokens.shape[0]
    model_dim = tokens.shape[1]
    groups = lax.axis_size("regions")
    slot_cap = 2 * rows_dev // groups
    page_num = rows_dev // PAGE
    slot_of = token_slot[0]
    home_rows = home_index[0]
    full_qkv, full_out, full_up, full_down, full_vec = (
        lax.all_gather(w_qkv, ("regions", "shard"), axis=0, tiled=True),
        lax.all_gather(w_out, ("regions", "shard"), axis=0, tiled=True),
        lax.all_gather(w_up, ("regions", "shard"), axis=0, tiled=True),
        lax.all_gather(w_down, ("regions", "shard"), axis=0, tiled=True),
        lax.all_gather(vectors, ("regions", "shard"), axis=1, tiled=True),
    )
    vec_rows = full_vec.astype(jnp.float32)
    qkv_bias = jnp.concatenate([vec_rows[0], jnp.zeros_like(vec_rows[0]), vec_rows[1]])
    code_rows = position_codes(box_x[0].reshape(page_num, PAGE), box_y[0].reshape(page_num, PAGE))
    bias_mats = bias_table(relative)
    homed = exchange(tokens, slot_of, home_rows, groups, slot_cap).astype(jnp.bfloat16)
    cotangent = exchange(out_grad[0], slot_of, home_rows, groups, slot_cap)
    projected = (jnp.dot(homed, full_qkv, preferred_element_type=jnp.float32) + qkv_bias).astype(
        jnp.bfloat16
    )
    paged = projected.reshape(page_num, PAGE, 3 * model_dim)
    context_pages, log_totals = lax.map(
        lambda member: page_forward(member[0], member[1], bias_mats), (paged, code_rows)
    )
    context = context_pages.reshape(rows_dev, model_dim)
    attn_out = jnp.dot(context, full_out, preferred_element_type=jnp.float32) + vec_rows[2]
    hidden, normed_one, spread_one = norm_forward(
        homed.astype(jnp.float32) + attn_out, vec_rows[3], vec_rows[4]
    )
    hidden_low = hidden.astype(jnp.bfloat16)
    pre_act = jnp.dot(hidden_low, full_up, preferred_element_type=jnp.float32) + vec_rows[
        8:12
    ].reshape(-1)
    activated, gelu_back = jax.vjp(lambda value: jax.nn.gelu(value, approximate=False), pre_act)
    act_low = activated.astype(jnp.bfloat16)
    branch = jnp.dot(act_low, full_down, preferred_element_type=jnp.float32) + vec_rows[5]
    result, normed_two, spread_two = norm_forward(hidden + branch, vec_rows[6], vec_rows[7])
    grad_two, grad_gain_two, grad_shift_two = norm_back(
        cotangent, normed_two, spread_two, vec_rows[6]
    )
    grad_branch = grad_two.astype(jnp.bfloat16)
    grad_down = jnp.einsum("tf,td->fd", act_low, grad_branch, preferred_element_type=jnp.float32)
    grad_act = jnp.einsum("td,fd->tf", grad_branch, full_down, preferred_element_type=jnp.float32)
    grad_pre = gelu_back(grad_act)[0].astype(jnp.bfloat16)
    grad_up = jnp.einsum("td,tf->df", hidden_low, grad_pre, preferred_element_type=jnp.float32)
    grad_hidden = grad_two + jnp.einsum(
        "tf,df->td", grad_pre, full_up, preferred_element_type=jnp.float32
    )
    grad_one, grad_gain_one, grad_shift_one = norm_back(
        grad_hidden, normed_one, spread_one, vec_rows[3]
    )
    grad_attn = grad_one.astype(jnp.bfloat16)
    grad_out = jnp.einsum("td,te->de", context, grad_attn, preferred_element_type=jnp.float32)
    grad_context = jnp.einsum(
        "te,de->td", grad_attn, full_out, preferred_element_type=jnp.float32
    ).astype(jnp.bfloat16)
    grad_home = grad_context.reshape(page_num, PAGE, model_dim)
    grad_pages, mats_pages = lax.map(
        lambda member: page_backward(member[0], member[1], member[2], member[3], bias_mats),
        (paged, code_rows, log_totals, grad_home),
    )
    grad_dense = grad_pages.reshape(rows_dev, 3 * model_dim)
    bias_sums = jnp.sum(grad_dense.astype(jnp.float32), axis=0)
    grad_qkv = jnp.einsum("td,tf->df", homed, grad_dense, preferred_element_type=jnp.float32)
    in_home = grad_one + jnp.einsum(
        "tf,df->td", grad_dense, full_qkv, preferred_element_type=jnp.float32
    )
    layer_out = exchange(result.astype(jnp.bfloat16), home_rows, slot_of, groups, slot_cap)
    in_grad = exchange(in_home.astype(jnp.bfloat16), home_rows, slot_of, groups, slot_cap)
    grad_vec = jnp.concatenate(
        [
            jnp.stack(
                [
                    bias_sums[:model_dim],
                    bias_sums[2 * model_dim :],
                    jnp.sum(grad_attn.astype(jnp.float32), axis=0),
                    grad_gain_one,
                    grad_shift_one,
                    jnp.sum(grad_branch.astype(jnp.float32), axis=0),
                    grad_gain_two,
                    grad_shift_two,
                ]
            ),
            jnp.sum(grad_pre.astype(jnp.float32), axis=0).reshape(4, model_dim),
        ],
        axis=0,
    )
    grad_qkv, grad_out, grad_up, grad_down, grad_vectors = (
        lax.psum_scatter(grad_qkv, ("regions", "shard"), scatter_dimension=0, tiled=True),
        lax.psum_scatter(grad_out, ("regions", "shard"), scatter_dimension=0, tiled=True),
        lax.psum_scatter(grad_up, ("regions", "shard"), scatter_dimension=0, tiled=True),
        lax.psum_scatter(grad_down, ("regions", "shard"), scatter_dimension=0, tiled=True),
        lax.psum_scatter(grad_vec, ("regions", "shard"), scatter_dimension=1, tiled=True),
    )
    mats_total = jnp.sum(mats_pages, axis=0)
    table_back = jax.vjp(bias_table, relative)[1]
    grad_relative = lax.psum(table_back(mats_total)[0], ("regions", "shard"))
    firsts_qkv, seconds_qkv, update_qkv = adam_step(
        w_qkv.astype(jnp.float32), grad_qkv, first_qkv, second_qkv, DECAY_RATE
    )
    firsts_out, seconds_out, update_out = adam_step(
        w_out.astype(jnp.float32), grad_out, first_out, second_out, DECAY_RATE
    )
    firsts_up, seconds_up, update_up = adam_step(
        w_up.astype(jnp.float32), grad_up, first_up, second_up, DECAY_RATE
    )
    firsts_down, seconds_down, update_down = adam_step(
        w_down.astype(jnp.float32), grad_down, first_down, second_down, DECAY_RATE
    )
    firsts_vectors, seconds_vectors, update_vectors = adam_step(
        vectors.astype(jnp.float32), grad_vectors, first_vectors, second_vectors, 0.0
    )
    firsts_relative, seconds_relative, update_relative = adam_step(
        relative, grad_relative, first_relative, second_relative, 0.0
    )
    return (
        layer_out.astype(jnp.bfloat16)[None],
        in_grad[None],
        grad_qkv,
        firsts_qkv,
        seconds_qkv,
        update_qkv,
        grad_out,
        firsts_out,
        seconds_out,
        update_out,
        grad_up,
        firsts_up,
        seconds_up,
        update_up,
        grad_down,
        firsts_down,
        seconds_down,
        update_down,
        grad_vectors,
        firsts_vectors,
        seconds_vectors,
        update_vectors,
        grad_relative,
        firsts_relative,
        seconds_relative,
        update_relative,
    )


def solution(mesh):
    kernels = mesh.shape["regions"] == PEERS and mesh.shape["shard"] == 2
    return jax.shard_map(
        per_device if kernels else spread_device,
        mesh=mesh,
        in_specs=(
            P("shard", "regions", None),
            P("shard", "regions", None),
            P(("regions", "shard"), None),
            P(("regions", "shard"), None),
            P(("regions", "shard"), None),
            P(("regions", "shard"), None),
            P(None, ("regions", "shard")),
            P(),
            P(("regions", "shard"), None),
            P(("regions", "shard"), None),
            P(("regions", "shard"), None),
            P(("regions", "shard"), None),
            P(("regions", "shard"), None),
            P(("regions", "shard"), None),
            P(("regions", "shard"), None),
            P(("regions", "shard"), None),
            P(None, ("regions", "shard")),
            P(None, ("regions", "shard")),
            P(),
            P(),
            P("shard", "regions"),
            P("shard", "regions"),
            P("shard", "regions"),
            P("shard", "regions"),
        ),
        out_specs=(
            P("shard", "regions", None),
            P("shard", "regions", None),
            P(("regions", "shard"), None),
            P(("regions", "shard"), None),
            P(("regions", "shard"), None),
            P(("regions", "shard"), None),
            P(("regions", "shard"), None),
            P(("regions", "shard"), None),
            P(("regions", "shard"), None),
            P(("regions", "shard"), None),
            P(("regions", "shard"), None),
            P(("regions", "shard"), None),
            P(("regions", "shard"), None),
            P(("regions", "shard"), None),
            P(("regions", "shard"), None),
            P(("regions", "shard"), None),
            P(("regions", "shard"), None),
            P(("regions", "shard"), None),
            P(None, ("regions", "shard")),
            P(None, ("regions", "shard")),
            P(None, ("regions", "shard")),
            P(None, ("regions", "shard")),
            P(),
            P(),
            P(),
            P(),
        ),
        check_vma=False,
    )
```

```python
import functools

import jax
import jax.numpy as jnp
import numpy as np
from jax import lax
from jax.experimental import pallas as pl
from jax.experimental.pallas import tpu as pltpu
from jax.sharding import PartitionSpec as P

REGIONS, SHARD = "regions", "shard"
BOTH = (REGIONS, SHARD)
HEADS = 12
HEAD = 64
PAGE = 576


PRECISE = lax.Precision.HIGHEST
EPS_NORM = 1e-05
BETA_ONE = 0.9
BETA_TWO = 0.999
ADAM_EPS = 1e-08
LAYER_FACTOR = 0.5625
DECAY_RATE = 0.05
STEP_COUNT = 10.0


def skewed(line, size):
    count = line.shape[0]
    wide = jnp.pad(line, ((0, 0), (0, 1)))
    flat = jnp.broadcast_to(wide[:, None, :], (count, size, 2 * size)).reshape(count, -1)
    rows = flat[:, : size * (2 * size - 1)].reshape(count, size, 2 * size - 1)
    return rows[:, :, size - 1 :]


def bias_table(relative):
    seq = skewed(relative[:, :127], 64)
    horizontal = skewed(relative[:, 127:190], 32)
    vertical = skewed(relative[:, 190:253], 32)
    return (
        jnp.pad(seq, ((0, 0), (0, 64), (0, 64)))
        + jnp.pad(horizontal, ((0, 0), (64, 32), (64, 32)))
        + jnp.pad(vertical, ((0, 0), (96, 0), (96, 0)))
    )


def position_codes(box_x, box_y):
    places = jnp.arange(PAGE, dtype=jnp.int32)
    seq_bucket = places * 64 // PAGE
    columns = jnp.arange(128, dtype=jnp.int32)
    matched = (
        (columns[None, None, :] == seq_bucket[None, :, None])
        | (columns == 64 + box_x[..., None])
        | (columns == 96 + box_y[..., None])
    )
    return matched.astype(jnp.float32)


def layout_bias(code_rows, bias_mats):
    lifted = jnp.einsum("pa,hab->hpb", code_rows, bias_mats, precision=PRECISE)
    return jnp.einsum("hpb,qb->hpq", lifted, code_rows, precision=PRECISE)


def page_scores(page_qkv, code_rows, bias_mats):
    parted = page_qkv.reshape(PAGE, 3, HEADS, HEAD)
    queries = parted[:, 0]
    key_rows = parted[:, 1]
    values = parted[:, 2]
    scores = jnp.einsum(
        "phd,qhd->hpq", queries, key_rows, preferred_element_type=jnp.float32
    ) * 0.125 + layout_bias(code_rows, bias_mats)
    return (queries, key_rows, values, scores)


def page_forward(page_qkv, code_rows, bias_mats):
    queries, key_rows, values, scores = page_scores(page_qkv, code_rows, bias_mats)
    row_max = jnp.max(scores, axis=2, keepdims=True)
    raised = jnp.exp(scores - row_max)
    totals = jnp.sum(raised, axis=2, keepdims=True)
    attn_w = (raised / totals).astype(jnp.bfloat16)
    context = jnp.einsum("hpq,qhd->phd", attn_w, values, preferred_element_type=jnp.float32)
    log_total = (row_max + jnp.log(totals))[..., 0]
    return (context.reshape(PAGE, HEADS * HEAD).astype(jnp.bfloat16), log_total)


def page_backward(page_qkv, code_rows, log_total, grad_ctx, bias_mats):
    queries, key_rows, values, scores = page_scores(page_qkv, code_rows, bias_mats)
    chances = jnp.exp(scores - log_total[..., None])
    attn_w = chances.astype(jnp.bfloat16)
    grad_heads = grad_ctx.reshape(PAGE, HEADS, HEAD)
    grad_values = jnp.einsum("hpq,phd->qhd", attn_w, grad_heads, preferred_element_type=jnp.float32)
    grad_chances = jnp.einsum(
        "phd,qhd->hpq", grad_heads, values, preferred_element_type=jnp.float32
    )
    inner = jnp.sum(chances * grad_chances, axis=2, keepdims=True)
    grad_scores = (chances * (grad_chances - inner)).astype(jnp.bfloat16)
    grad_queries = (
        jnp.einsum("hpq,qhd->phd", grad_scores, key_rows, preferred_element_type=jnp.float32)
        * 0.125
    )
    grad_keys = (
        jnp.einsum("hpq,phd->qhd", grad_scores, queries, preferred_element_type=jnp.float32) * 0.125
    )
    partial_codes = jnp.einsum(
        "hpq,qb->hpb",
        grad_scores,
        code_rows.astype(jnp.bfloat16),
        preferred_element_type=jnp.float32,
    )
    grad_mats = jnp.einsum("pa,hpb->hab", code_rows, partial_codes, precision=PRECISE)
    grad_page = jnp.stack([grad_queries, grad_keys, grad_values], axis=1).reshape(
        PAGE, 3 * HEADS * HEAD
    )
    return (grad_page.astype(jnp.bfloat16), grad_mats)


def exchange(rows, targets, picks, groups, slot_cap):
    slots = groups * slot_cap
    places = jnp.arange(slots, dtype=jnp.int32)
    packing = (places[:, None] == targets[None, :]).astype(jnp.bfloat16)
    packed = jnp.dot(packing, rows, preferred_element_type=jnp.float32).astype(jnp.bfloat16)
    arrived = lax.all_to_all(
        packed.reshape(groups, slot_cap, rows.shape[1]),
        REGIONS,
        split_axis=0,
        concat_axis=0,
        tiled=True,
    ).reshape(slots, rows.shape[1])
    picking = (picks[:, None] == places[None, :]).astype(jnp.bfloat16)
    return jnp.dot(picking, arrived, preferred_element_type=jnp.float32)


def norm_forward(rows, gain, shift):
    centre = rows - jnp.mean(rows, axis=-1, keepdims=True)
    spread = lax.rsqrt(jnp.mean(centre * centre, axis=-1, keepdims=True) + EPS_NORM)
    normed = centre * spread
    return (normed * gain + shift, normed, spread)


def norm_back(incoming, normed, spread, gain):
    scaled = incoming * gain
    grad_rows = spread * (
        scaled
        - jnp.mean(scaled, axis=-1, keepdims=True)
        - normed * jnp.mean(scaled * normed, axis=-1, keepdims=True)
    )
    return (grad_rows, jnp.sum(incoming * normed, axis=0), jnp.sum(incoming, axis=0))


def adam_step(param, grad, moment, square, decay):
    moment_new = BETA_ONE * moment + (1.0 - BETA_ONE) * grad
    square_new = BETA_TWO * square + (1.0 - BETA_TWO) * grad * grad
    moment_hat = moment_new / (1.0 - BETA_ONE**STEP_COUNT)
    square_hat = square_new / (1.0 - BETA_TWO**STEP_COUNT)
    update = LAYER_FACTOR * (moment_hat / (jnp.sqrt(square_hat) + ADAM_EPS) + decay * param)
    return (moment_new, square_new, update)


ROWS = 576


def softly(scores, axis):
    peak = jnp.max(scores, axis=axis, keepdims=True)
    raised = jnp.exp(scores - peak)
    return raised * (1.0 / jnp.sum(raised, axis=axis, keepdims=True))


def head_lift(tables, codes, h):
    line = tables[pl.ds(h, 1), :]
    lane = lax.broadcasted_iota(jnp.int32, (64, 128), 1)

    def spread(entry, size, low, high):
        if low == 0:
            start = pltpu.roll(line[:, :128], 128 - entry, 1)
        else:
            start = pltpu.roll(line, 256 - entry, 1)[:, :128]
        turned = pltpu.roll(jnp.broadcast_to(start, (size, 128)), 0, 1, stride=1, stride_axis=0)
        return jnp.where((lane[:size] >= low) & (lane[:size] < high), turned, 0.0)

    table = jnp.concatenate(
        [spread(63, 64, 0, 64), spread(94, 32, 64, 96), spread(125, 32, 96, 128)], axis=0
    )
    high = table.astype(jnp.bfloat16)
    low = (table - high.astype(jnp.float32)).astype(jnp.bfloat16)
    both = jnp.concatenate([high, low], axis=1)
    return jnp.dot(codes, both, preferred_element_type=jnp.float32).astype(jnp.bfloat16)


def lane_mask(rows, h):
    lane = lax.broadcasted_iota(jnp.int32, (rows, 128), 1)
    return (lane < 64) if h == 0 else (lane >= 64)


def pair_columns(qkv, pair):
    width = qkv.shape[1] // 3
    at = [pl.multiple_of(n * width + pair * 128, 128) for n in range(3)]
    return [qkv[:, pl.ds(a, 128)] for a in at]


NT = (((1,), (1,)), ((), ()))
TN = (((0,), (0,)), ((), ()))


def attend_pair(pair, qkv, tables, codes_ref, context):
    count = qkv.shape[0]
    codes = codes_ref[...]
    queries, keys, values = pair_columns(qkv, pair)
    right = jnp.concatenate([keys, codes, codes], axis=1)
    scaled = queries * jnp.bfloat16(0.125)
    results = []
    for h in range(2):
        mine = jnp.where(lane_mask(count, h), scaled, jnp.zeros_like(scaled))
        left = jnp.concatenate([mine, head_lift(tables, codes, 2 * pair + h)], axis=1)
        parts = []
        for r in range(0, count, ROWS):
            scores = lax.dot_general(left[r : r + ROWS], right, NT, preferred_element_type=jnp.float32)
            weights = softly(scores, 1).astype(jnp.bfloat16)
            parts.append(jnp.dot(weights, values, preferred_element_type=jnp.float32))
        results.append(parts)
    for n, r in enumerate(range(0, count, ROWS)):
        both = jnp.where(lane_mask(ROWS, 0), results[0][n], results[1][n])
        context[pl.ds(r, ROWS), pl.ds(pl.multiple_of(pair * 128, 128), 128)] = both.astype(jnp.bfloat16)


def attend_pair_back(pair, qkv, grad_ref, tables, codes_ref, flipped_ref, grad_qkv, grad_tables):
    count = qkv.shape[0]
    width = qkv.shape[1] // 3
    codes = codes_ref[...]
    queries, keys, values = pair_columns(qkv, pair)
    grads = grad_ref[:, pl.ds(pl.multiple_of(pair * 128, 128), 128)]
    left = jnp.concatenate([keys, codes, codes], axis=1)
    near = jnp.concatenate([keys, codes], axis=1)
    scaled = queries * jnp.bfloat16(0.125)
    out_q, out_k, out_v = [], [], []
    for h in range(2):
        mask = lane_mask(count, h)
        mine = jnp.where(mask, scaled, jnp.zeros_like(scaled))
        mine_grad = jnp.where(mask, grads, jnp.zeros_like(grads))
        right = jnp.concatenate([mine, head_lift(tables, codes, 2 * pair + h)], axis=1)
        total = None
        k_parts, v_parts = [], []
        if True:
            scores = lax.dot_general(left, right, NT, preferred_element_type=jnp.float32)
            chances = softly(scores, 0)
            grad_chances = lax.dot_general(values, mine_grad, NT, preferred_element_type=jnp.float32)
            inner = jnp.sum(chances * grad_chances, axis=0, keepdims=True)
            grad_scores = (chances * (grad_chances - inner)).astype(jnp.bfloat16)
            v_rows = jnp.dot(chances.astype(jnp.bfloat16), grads, preferred_element_type=jnp.float32)
            k_rows = jnp.dot(grad_scores, queries, preferred_element_type=jnp.float32)
            total = lax.dot_general(grad_scores, near, TN, preferred_element_type=jnp.float32)
        out_q.append(total[:, :128])
        out_k.append(k_rows)
        out_v.append(v_rows)
        partial = total[:, 128:]
        high = partial.astype(jnp.bfloat16)
        low = (partial - high.astype(jnp.float32)).astype(jnp.bfloat16)
        mats = lax.dot_general(
            flipped_ref[...], jnp.concatenate([high, low], axis=1), TN, preferred_element_type=jnp.float32
        )
        mats = mats[:, :128] + mats[:, 128:]
        lane = lax.broadcasted_iota(jnp.int32, (64, 128), 1)

        def gathered(row, size, low_lane, high_lane):
            part = jnp.where((lane[:size] >= low_lane) & (lane[:size] < high_lane), mats[row : row + size], 0.0)
            turned = pltpu.roll(part, 0, 1, stride=1, stride_axis=0)
            return jnp.sum(turned, axis=0, keepdims=True)

        blank = jnp.zeros((1, 128), jnp.float32)
        seq, across, down = [
            jnp.concatenate([part, blank], axis=1)
            for part in (gathered(0, 64, 0, 64), gathered(64, 32, 64, 96), pltpu.roll(gathered(96, 32, 96, 128), 32, 1))
        ]
        grad_tables[pl.ds(2 * pair + h, 1), :] = seq + pltpu.roll(across, 63, 1) + pltpu.roll(down, 190, 1)
    mask = lane_mask(count, 0)
    for n, (parts, factor) in enumerate(((out_q, 0.125), (out_k, 0.125), (out_v, 1.0))):
        both = jnp.where(mask, parts[0], parts[1]) * factor
        grad_qkv[:, pl.ds(pl.multiple_of(n * width + pair * 128, 128), 128)] = both.astype(jnp.bfloat16)


def code_rows_of(box_x, box_y, flip):
    count = box_x.shape[1]
    column = lax.broadcasted_iota(jnp.int32, (128, count), 0)
    row = lax.broadcasted_iota(jnp.int32, (128, count), 1)
    start = (63 - column if flip else column) * (count // 64)
    hit_seq = (column < 64) & (row >= start) & (row < start + count // 64)
    across, down = box_x[...], box_y[...]
    if flip:
        across, down = 31 - across, 31 - down
    hit = hit_seq | (column == 64 + across) | (column == 96 + down)
    return jnp.where(hit, 1.0, 0.0).T.astype(jnp.bfloat16)


def as_columns(line):
    wide = jnp.broadcast_to(line[...].astype(jnp.float32), (128, line.shape[1]))
    return wide.T.astype(jnp.int32)


MESH = pl.DeviceIdType.MESH
PEERS = 16
VEC_COLS = 256


def place():
    me = lax.axis_index(REGIONS)
    core = lax.axis_index(SHARD)
    z = lax.div(me, 4)
    y = lax.div(lax.rem(me, 4), 2)
    x = lax.rem(me, 2)
    return me, core, z, y, x


def enter(me, core):
    barrier = pltpu.get_barrier_semaphore()
    for k in range(1, PEERS):
        pl.semaphore_signal(barrier, inc=1, device_id=(me ^ k, core), device_id_type=MESH)
    pl.semaphore_signal(barrier, inc=1, device_id=(me, 1 - core), device_id_type=MESH)
    pl.semaphore_wait(barrier, PEERS)


def remote(src, dst, send, recv, device):
    return pltpu.make_async_remote_copy(
        src_ref=src, dst_ref=dst, send_sem=send, recv_sem=recv, device_id=device, device_id_type=MESH
    )


class Exchange:
    def __init__(self, where, packed, arrived, loose, send, recv, local):
        self.me, self.core = where[0], where[1]
        self.packed, self.arrived, self.loose = packed, arrived, loose
        self.send, self.recv, self.local = send, recv, local
        self.slots, self.half = packed.shape[1], packed.shape[2]

    def pack(self, rows, slot_of):
        count = self.slots // 2
        for j in range(4):
            group = lax.div(self.me, 4) ^ j
            at = lax.broadcasted_iota(jnp.int32, (4 * count, rows.shape[0]), 0) + group * (4 * count)
            picking = jnp.where(at == slot_of[...], 1.0, 0.0).astype(jnp.bfloat16)
            block = jnp.dot(picking, rows[...], preferred_element_type=jnp.float32)
            for n in range(4):
                own = block[n * count : (n + 1) * count]
                both = jnp.concatenate([own[:, : self.half], own[:, self.half :]], axis=0)
                self.packed[4 * group + n] = both.astype(jnp.bfloat16)
            for k in range(4):
                if j + k:
                    self.copy(4 * j + k).start()
                else:
                    self.own().start()

    def copy(self, k):
        d = self.me ^ k
        return remote(
            self.packed.at[d], self.arrived.at[self.me], self.send.at[k], self.recv.at[k], (d, self.core)
        )

    def own(self):
        return pltpu.make_async_copy(self.packed.at[self.me], self.arrived.at[self.me], self.local)

    def wait(self):
        self.own().wait()

        def one(k, carry):
            self.copy(k).wait()
            return carry

        lax.fori_loop(1, PEERS, one, 0)

    def unpack(self, slot_of, out, kind):
        out[...] = unpacked(self.arrived, self.loose, slot_of).astype(kind)


def unpacked(arrived, loose, slot_of):
    count = arrived.shape[1] // 2
    rows = []
    for n in range(PEERS):
        block = arrived[n].astype(jnp.float32)
        rows.append(jnp.concatenate([block[:count], block[count:]], axis=1))
        if n % 2:
            pair = jnp.concatenate(rows, axis=0)
            loose[pl.ds((n - 1) * count, 2 * count)] = pair.astype(jnp.bfloat16)
            rows = []
    wanted = as_columns(slot_of)
    lane = lax.broadcasted_iota(jnp.int32, wanted.shape, 1)
    picking = jnp.concatenate(
        [
            jnp.where(lane + first == wanted, 1.0, 0.0).astype(jnp.bfloat16)
            for first in range(0, PEERS * count, 128)
        ],
        axis=1,
    )
    return jnp.dot(picking, loose[...], preferred_element_type=jnp.float32)


def pieces_of(rows, half):
    tiles = half // 128
    if rows % 64 == 0:
        cuts = [(n * rows // 4, rows // 4, 0, half) for n in range(4)]
    elif tiles < 4:
        wide = (tiles + 1) // 2 * 128
        cuts = [(0, rows, 0, wide), (0, rows, wide, half - wide)]
    else:
        ends = [0, (tiles + 3) // 4, tiles // 2, tiles - (tiles + 3) // 4, tiles]
        cuts = [(0, rows, 128 * ends[n], 128 * (ends[n + 1] - ends[n])) for n in range(4)]
    return [[(*cuts[n], True), (*cuts[n + 1], False)] for n in range(0, len(cuts), 2)]


class Gather:
    def __init__(self, where, whole, piece, sems):
        self.where, self.whole, self.piece, self.sems = where, whole, piece, sems

    def part(self, z, y, x):
        core = self.where[1]
        r0, rows, c0, cols, _ = self.piece
        half = self.whole.shape[4] // 2
        at = pl.multiple_of(core * half + c0, 128)
        return self.whole.at[z, y, x, pl.ds(r0, rows), pl.ds(at, cols)]

    def along_z(self, t, upward):
        me, core, z, y, x = self.where
        step = 1 if upward else -1
        origin = z - step * t
        ref = self.part(origin, y, x)
        i = 2 * t + (1 if upward else 0)
        return remote(ref, ref, self.sems.at[0, i], self.sems.at[1, i], (me + 4 * step, core))

    def z_sends(self, t, do):
        z = self.where[2]

        @pl.when((z >= t) & (z <= 2))
        def _():
            do(self.along_z(t, True))

        @pl.when((z + t <= 3) & (z >= 1))
        def _():
            do(self.along_z(t, False))

    def z_waits(self, t):
        z = self.where[2]

        @pl.when(z - 1 - t >= 0)
        def _():
            me, core, z, y, x = self.where
            ref = self.part(z - 1 - t, y, x)
            i = 2 * t + 1
            remote(ref, ref, self.sems.at[0, i], self.sems.at[1, i], (me, 1 - core)).wait_recv()

        @pl.when(z + 1 + t <= 3)
        def _():
            me, core, z, y, x = self.where
            ref = self.part(z + 1 + t, y, x)
            i = 2 * t
            remote(ref, ref, self.sems.at[0, i], self.sems.at[1, i], (me, 1 - core)).wait_recv()

    def plane(self, n):
        me, core, z, y, x = self.where
        x_first = self.piece[4]
        every = slice(None)
        other = (me, 1 - core)
        if n == 0:
            ref, device = self.part(every, y, x), (me ^ (1 if x_first else 2), core)
        elif n == 1 and x_first:
            ref, device = self.part(every, y, every), (me ^ 2, core)
        elif n == 1:
            ref, device = self.part(every, every, x), (me ^ 1, core)
        elif n == 2:
            ref, device = self.part(every, y, x), other
        elif n == 3:
            ref, device = (self.part(every, y, 1 - x) if x_first else self.part(every, 1 - y, x)), other
        else:
            ref, device = (self.part(every, 1 - y, every) if x_first else self.part(every, every, 1 - x)), other
        return remote(ref, ref, self.sems.at[0, 6 + n], self.sems.at[1, 6 + n], device)

    def run(self, stage):
        if stage < 3:
            if stage:
                self.z_waits(stage - 1)
            self.z_sends(stage, lambda copy: copy.start())
        elif stage == 3:
            self.z_waits(2)
            self.plane(0).start()
            self.plane(2).start()
        elif stage == 4:
            self.plane(0).wait_recv()
            self.plane(1).start()
            self.plane(3).start()
        elif stage == 5:
            self.plane(1).wait_recv()
            self.plane(4).start()
        else:
            for n in (2, 3, 4):
                self.plane(n).wait_recv()

    def sent(self):
        for t in range(3):
            self.z_sends(t, lambda copy: copy.wait_send())
        for n in range(5):
            self.plane(n).wait_send()


class Scatter:
    def __init__(self, where, local, sums, from_core, from_near, from_far, from_z, fetch, piece, sems):
        self.where, self.local, self.sums, self.piece, self.sems = where, local, sums, piece, sems
        self.from_core, self.from_near, self.from_far, self.from_z = from_core, from_near, from_far, from_z
        self.half, self.fetch = sums.shape[4], fetch

    def cut(self, ref, *lead, core=None):
        r0, rows, c0, cols, _ = self.piece
        at = c0 if core is None else pl.multiple_of(core * self.half + c0, 128)
        return ref.at[(*lead, pl.ds(r0, rows), pl.ds(at, cols))]

    def between_cores(self):
        me, core = self.where[0], self.where[1]
        every = slice(None)
        src = self.cut(self.local, every, every, every, core=1 - core)
        dst = self.cut(self.from_core, every, every, every)
        return remote(src, dst, self.sems.at[0, 0], self.sems.at[1, 0], (me, 1 - core))

    def own_half(self):
        every = slice(None)
        src = self.cut(self.local, every, every, every, core=self.where[1])
        return pltpu.make_async_copy(src, self.cut(self.sums, every, every, every), self.fetch)

    def near(self):
        me, core, z, y, x = self.where
        every = slice(None)
        if self.piece[4]:
            src, device = self.cut(self.sums, every, 1 - y, every), (me ^ 2, core)
        else:
            src, device = self.cut(self.sums, every, every, 1 - x), (me ^ 1, core)
        dst = self.cut(self.from_near, every, every)
        return remote(src, dst, self.sems.at[0, 1], self.sems.at[1, 1], device)

    def far(self):
        me, core, z, y, x = self.where
        every = slice(None)
        if self.piece[4]:
            src, device = self.cut(self.sums, every, y, 1 - x), (me ^ 1, core)
        else:
            src, device = self.cut(self.sums, every, 1 - y, x), (me ^ 2, core)
        dst = self.cut(self.from_far, every)
        return remote(src, dst, self.sems.at[0, 2], self.sems.at[1, 2], device)

    def along_z(self, sender, upward):
        me, core, z, y, x = self.where
        lead = pl.ds(sender + 1, 3 - sender) if upward else pl.ds(0, sender)
        src = self.cut(self.sums, lead, y, x)
        dst = self.cut(self.from_z, 1 if upward else 0, lead)
        i = 3 + (1 if upward else 0)
        step = 4 if upward else -4
        return remote(src, dst, self.sems.at[0, i], self.sems.at[1, i], (me + step, core))

    def add(self, target, other):
        total = target[...].astype(jnp.float32) + other[...].astype(jnp.float32)
        target[...] = total.astype(jnp.bfloat16)

    def z_got(self, sender, upward):
        me, core, z, y, x = self.where
        self.along_z(sender, upward).wait_recv()
        for d in range(sender + 1, 4) if upward else range(sender):
            self.add(self.cut(self.sums, d, y, x), self.cut(self.from_z, 1 if upward else 0, d))

    def run(self, stage):
        me, core, z, y, x = self.where
        if stage == 0:
            self.between_cores().start()
            self.own_half().start()
        elif stage == 1:
            self.own_half().wait()
            self.between_cores().wait_recv()

            def one(i, carry):
                a, b, c = lax.div(i, 4), lax.div(lax.rem(i, 4), 2), lax.rem(i, 2)
                self.add(self.cut(self.sums, a, b, c), self.cut(self.from_core, a, b, c))
                return carry

            lax.fori_loop(0, 16, one, 0)
            self.near().start()
        elif stage == 2:
            self.near().wait_recv()

            def one(i, carry):
                a, b = lax.div(i, 2), lax.rem(i, 2)
                target = self.cut(self.sums, a, y, b) if self.piece[4] else self.cut(self.sums, a, b, x)
                self.add(target, self.cut(self.from_near, a, b))
                return carry

            lax.fori_loop(0, 8, one, 0)
            self.far().start()
        elif stage == 3:
            self.far().wait_recv()

            def one(i, carry):
                self.add(self.cut(self.sums, i, y, x), self.cut(self.from_far, i))
                return carry

            lax.fori_loop(0, 4, one, 0)

            @pl.when(z == 3)
            def _():
                self.along_z(3, False).start()

            @pl.when(z == 0)
            def _():
                self.along_z(0, True).start()

        elif stage == 4:

            @pl.when(z == 2)
            def _():
                self.z_got(3, False)
                self.along_z(2, False).start()

            @pl.when(z == 1)
            def _():
                self.z_got(0, True)
                self.along_z(1, True).start()

        elif stage == 5:

            @pl.when(z == 1)
            def _():
                self.z_got(2, False)
                self.along_z(1, False).start()

            @pl.when(z == 2)
            def _():
                self.z_got(1, True)
                self.along_z(2, True).start()

        elif stage == 6:

            @pl.when(z == 0)
            def _():
                self.z_got(1, False)

            @pl.when(z == 3)
            def _():
                self.z_got(2, True)

    def sent(self):
        z = self.where[2]
        self.between_cores().wait_send()
        self.near().wait_send()
        self.far().wait_send()
        for sender in range(4):

            @pl.when(z == sender)
            def _(sender=sender):
                if sender > 0:
                    self.along_z(sender, False).wait_send()
                if sender < 3:
                    self.along_z(sender, True).wait_send()


def stepper(tasks):
    def step(k):
        for pair, plan in tasks:
            if k in plan:
                for task in pair:
                    task.run(plan.index(k))

    return step, max(plan[-1] for _, plan in tasks) + 1


HOMED, QKV, WHOLE, CODES, FLIPPED, RESULT, ONE, CONTEXT, OUT, VECTORS, DOWN, UP = range(12)


def normed_rows(rows):
    centre = rows - jnp.mean(rows, axis=-1, keepdims=True)
    spread = lax.rsqrt(jnp.mean(centre * centre, axis=-1, keepdims=True) + EPS_NORM)
    return centre * spread, spread


def dense_part(
    homed, cotangent, context, vec, w_out, w_up, w_down,
    result, grad_one_ref, grad_context, g_out, g_up, g_down, vec_grads,
    act, slope, hidden_low, fetch, save,
):
    width = homed.shape[1]
    chunks = w_up.shape[4] // width
    f32 = jnp.float32
    low = jnp.bfloat16

    def columns(ref, c):
        return ref[:, :, :, :, c * width : (c + 1) * width].reshape(width, width)

    def keep(n, line):
        vec_grads[n : n + 1] = jnp.sum(line, axis=0, keepdims=True)

    attn_out = jnp.dot(context[...], columns(w_out, 0), preferred_element_type=f32) + vec[2:3]
    normed_one, spread_one = normed_rows(homed[...].astype(f32) + attn_out)
    hidden = normed_one * vec[3:4] + vec[4:5]
    hidden_low[...] = hidden.astype(low)
    branch = None
    for c in range(chunks):
        pre = jnp.dot(hidden_low[...], columns(w_up, c), preferred_element_type=f32) + vec[8 + c : 9 + c]
        below = 0.5 * (1.0 + lax.erf(pre * 0.7071067811865476))
        act[c] = (pre * below).astype(low)
        slope[c] = below + pre * (jnp.exp(-0.5 * pre * pre) * 0.3989422804014327)
        part = jnp.dot(act[c], w_down[c].reshape(width, width), preferred_element_type=f32)
        branch = part if branch is None else branch + part
    normed_two, spread_two = normed_rows(hidden + branch + vec[5:6])
    result[...] = (normed_two * vec[6:7] + vec[7:8]).astype(low)
    save(RESULT)

    def back(e, normed, spread, gain):
        scaled = e * gain
        return spread * (
            scaled
            - jnp.mean(scaled, axis=-1, keepdims=True)
            - normed * jnp.mean(scaled * normed, axis=-1, keepdims=True)
        )

    fetch()
    e = cotangent[...].astype(f32)
    keep(6, e * normed_two)
    keep(7, e)
    grad_two = back(e, normed_two, spread_two, vec[6:7])
    grad_branch = grad_two.astype(low)
    keep(5, grad_branch.astype(f32))
    grad_hidden = grad_two
    for c in range(chunks):
        if c > 1:
            save(DOWN, c - 2, done=True)
            save(UP, c - 2, done=True)
        g_down[c % 2] = (
            lax.dot_general(act[c], grad_branch, TN, preferred_element_type=f32)
            .astype(low)
            .reshape(g_down.shape[1:])
        )
        save(DOWN, c)
        grad_act = lax.dot_general(
            grad_branch, w_down[c].reshape(width, width), NT, preferred_element_type=f32
        )
        grad_pre = (grad_act * slope[c]).astype(low)
        keep(8 + c, grad_pre.astype(f32))
        g_up[c % 2] = (
            lax.dot_general(hidden_low[...], grad_pre, TN, preferred_element_type=f32)
            .astype(low)
            .reshape(g_up.shape[1:])
        )
        save(UP, c)
        grad_hidden = grad_hidden + lax.dot_general(
            grad_pre, columns(w_up, c), NT, preferred_element_type=f32
        )
    keep(3, grad_hidden * normed_one)
    keep(4, grad_hidden)
    grad_one = back(grad_hidden, normed_one, spread_one, vec[3:4])
    grad_one_ref[...] = grad_one
    save(ONE)
    grad_attn = grad_one.astype(low)
    keep(2, grad_attn.astype(f32))
    g_out[...] = (
        lax.dot_general(context[...], grad_attn, TN, preferred_element_type=f32)
        .astype(low)
        .reshape(g_out.shape)
    )
    save(OUT)
    grad_context[...] = lax.dot_general(
        grad_attn, columns(w_out, 0), NT, preferred_element_type=f32
    ).astype(low)
    vec_grads[0:2] = jnp.zeros((2, width), f32)
    vec_grads[12:] = jnp.zeros((vec_grads.shape[0] - 12, width), f32)
    save(CONTEXT)
    save(VECTORS)


PAIRS = 6
READY = 8
SEND_ROWS = 4


def gather_plan(n, early):
    z, wide = n // 2, 3 + n
    if early:
        return (z, z + 1, z + 2, wide, wide + 1, wide + 2, wide + 3)
    return (z, z + 1, z + 2, wide, wide + 2, wide + 4, wide + 6)


def split_shard(shard, halves, beside=None):
    rows, half = shard.shape[0], halves.shape[2]
    halves[...] = jnp.zeros_like(halves)
    halves[0, :rows] = shard[:, :half]
    if beside is None:
        halves[1, :rows] = shard[:, half:]
    else:
        rest = shard.shape[1] - half
        halves[1, :rows, :rest] = shard[:, half:]
        halves[1, :rows, rest : rest + 128] = beside


def inbound_kernel(
    rows_ref, grad_ref, slot_line, home_line, box_x, box_y, r_tables, r_qkv, r_out, r_up, r_down, r_vec,
    h_homed, h_qkv, h_whole, h_codes, h_flipped, h_result, h_one, h_context, h_out, h_up, h_down, h_vec,
    homed, qkv, w_qkv, codes, flipped, result, grad_one, g_out, vec_grads, g_up, g_down,
    context, vec_rows, w_out, w_up, w_down, act, slope, hidden_low, square, tables,
    s_qkv, s_out, s_up, s_down,
    packed, arrived_a, arrived_b, loose, p_qkv, p_out, p_up, p_down, b_qkv, b_out, b_up, b_down,
    send_a, recv_a, send_b, recv_b, local_sems, pair_sems, block_sems, piece_sems, save_sems,
):
    where = place()
    me, core, z, y, x = where
    width = homed.shape[1]
    cotangent = loose.at[pl.ds(0, homed.shape[0])]
    kept = (
        (homed, h_homed), (qkv, h_qkv), (w_qkv, h_whole), (codes, h_codes), (flipped, h_flipped),
        (result, h_result), (grad_one, h_one), (context, h_context), (g_out, h_out), (vec_grads, h_vec),
        (g_down, h_down), (g_up, h_up),
    )
    saves = {}

    def save(which, c=None, done=False):
        if done:
            saves.pop((which, c)).wait()
            return
        src, dst = kept[which]
        if which == DOWN:
            src, dst = src.at[c % 2], dst.at[c]
        elif which == UP:
            src, dst = src.at[c % 2], dst.at[:, :, :, :, pl.ds(c * width, width)]
        n = which if c is None else DOWN + c + (4 if which == UP else 0)
        saves[which, c] = pltpu.make_async_copy(src, dst, save_sems.at[n])
        saves[which, c].start()

    shards = (s_qkv, s_out, s_up, s_down)
    others = (p_qkv, p_out, p_up, p_down)
    blocks = (b_qkv, b_out, b_up, b_down)
    wholes = (w_qkv, w_out, w_up, w_down)
    tables[...] = jnp.zeros_like(tables)
    tables[: r_tables.shape[0], : r_tables.shape[1]] = r_tables[...]
    square[...] = jnp.zeros_like(square)
    square[: r_vec.shape[0], : r_vec.shape[1]] = r_vec[...].astype(jnp.float32)
    split_shard(r_qkv, s_qkv, square[...].T[: r_qkv.shape[0]].astype(jnp.bfloat16))
    split_shard(r_out, s_out)
    split_shard(r_up, s_up)
    split_shard(r_down, s_down)
    enter(me, core)
    pairs = [
        remote(shards[i].at[1 - core], others[i], pair_sems.at[0, i], pair_sems.at[1, i], (me, 1 - core))
        for i in range(4)
    ]
    for pair in pairs:
        pair.start()
    moved = Exchange(where, packed, arrived_a, loose, send_a, recv_a, local_sems.at[0])
    moved_grad = Exchange(where, packed, arrived_b, loose, send_b, recv_b, local_sems.at[1])
    tasks = []
    for i in range(4):
        for pair in pieces_of(blocks[i].shape[0], blocks[i].shape[1]):
            n = len(tasks)
            pair = [Gather(where, wholes[i], piece, piece_sems.at[2 * n + j]) for j, piece in enumerate(pair)]
            tasks.append((pair, gather_plan(n, i == 0)))
    step, steps = stepper(tasks)

    def assemble(i):
        pairs[i].wait_recv()
        half = blocks[i].shape[1]
        rows = blocks[i].shape[0] // 2
        mine = shards[i][core][:rows].astype(jnp.float32)
        other = others[i][:rows].astype(jnp.float32)
        first = jnp.where(core == 0, mine, other)
        second = jnp.where(core == 0, other, mine)
        blocks[i][...] = jnp.concatenate([first, second], axis=0).astype(jnp.bfloat16)
        at = pl.multiple_of(core * half, 128)
        copy = pltpu.make_async_copy(
            blocks[i], wholes[i].at[z, y, x, :, pl.ds(at, half)], block_sems.at[i]
        )
        copy.start()
        return copy

    assemble(0).wait()
    step(0)
    placed = [assemble(i) for i in range(1, 4)]
    codes[...] = code_rows_of(box_x, box_y, False)
    flipped[...] = code_rows_of(box_x, box_y, True)
    save(CODES)
    save(FLIPPED)
    for copy in placed:
        copy.wait()

    for k in range(1, READY):
        step(k)
        if k == SEND_ROWS:
            moved.pack(rows_ref, slot_line)
    moved.wait()
    moved.unpack(home_line, homed, jnp.bfloat16)
    moved_grad.pack(grad_ref, slot_line)
    columns = w_qkv[:, :, :, :, 3 * width : 3 * width + 128].reshape(width, 128)
    vec_rows[...] = columns.astype(jnp.float32).T[: vec_rows.shape[0]]
    for n in range(3):
        part = w_qkv[:, :, :, :, n * width : (n + 1) * width].reshape(width, width)
        projected = jnp.dot(homed[...], part, preferred_element_type=jnp.float32)
        if n != 1:
            projected = projected + vec_rows[n // 2 : n // 2 + 1]
        qkv[:, n * width : (n + 1) * width] = projected.astype(jnp.bfloat16)
    for which in (HOMED, WHOLE, QKV):
        save(which)

    def one(pair, carry):
        attend_pair(pair, qkv, tables, codes, context)
        for j in range(PAIRS):

            @pl.when(pair == j)
            def _(j=j):
                step(READY + j)

        return carry

    lax.fori_loop(0, PAIRS, one, 0)
    for k in range(READY + PAIRS, steps):
        step(k)

    def fetch():
        moved_grad.wait()
        moved_grad.unpack(home_line, cotangent, jnp.bfloat16)

    dense_part(
        homed, cotangent, context, vec_rows, w_out, w_up, w_down,
        result, grad_one, context, g_out, g_up, g_down, vec_grads,
        act, slope, hidden_low, fetch, save,
    )
    for copy in saves.values():
        copy.wait()
    for pair in pairs:
        pair.wait_send()
    for pair, _ in tasks:
        for task in pair:
            task.sent()


def vmem(count):
    return [pl.BlockSpec(memory_space=pltpu.VMEM)] * count


def inbound(rows, grads, slot_line, home_line, box_x, box_y, tables, shards, vectors):
    tokens, width = rows.shape
    slots = 2 * (2 * tokens // PEERS)
    low, f32 = jnp.bfloat16, jnp.float32
    buffer = pltpu.VMEM((PEERS, slots, width // 2), low)
    wholes, halves, pair_shapes, block_shapes = [], [], [], []
    for n, shard in enumerate(shards):
        count, columns = shard.shape
        half = (columns + (VEC_COLS if n == 0 else 0)) // 2
        padded = count + -count % 16
        wholes.append((4, 2, 2, 2 * count, 2 * half))
        halves.append(pltpu.VMEM((2, padded, half), low))
        pair_shapes.append(pltpu.VMEM((padded, half), low))
        block_shapes.append(pltpu.VMEM((2 * count, half), low))
    chunks = wholes[2][4] // width
    dma = pltpu.SemaphoreType.DMA

    def array(shape, kind=low):
        return jax.ShapeDtypeStruct(shape, kind)

    results = [
        array((tokens, width)),
        array((tokens, 3 * width)),
        array(wholes[0]),
        array((tokens, 128)),
        array((tokens, 128)),
        array((tokens, width)),
        array((tokens, width), f32),
        array((tokens, width)),
        *[array(shape) for shape in wholes[1:]],
        array((128, width), f32),
    ]
    return pl.pallas_call(
        inbound_kernel,
        out_shape=results,
        in_specs=vmem(12),
        out_specs=[pl.BlockSpec(memory_space=pl.ANY)] * 12,
        scratch_shapes=[pltpu.VMEM(results[n].shape, results[n].dtype) for n in range(12) if n not in (7, 9, 10)]
        + [
            pltpu.VMEM((2, *wholes[2][:4], width), low),
            pltpu.VMEM((2, *wholes[3][1:]), low),
            pltpu.VMEM((tokens, width), low),
            pltpu.VMEM((16, width), f32),
            *[pltpu.VMEM(shape, low) for shape in wholes[1:]],
            pltpu.VMEM((chunks, tokens, width), low),
            pltpu.VMEM((chunks, tokens, width), f32),
            pltpu.VMEM((tokens, width), low),
            pltpu.VMEM((128, 128), f32),
            pltpu.VMEM((16, 256), f32),
        ]
        + halves
        + [buffer] * 3
        + [pltpu.VMEM((PEERS * (slots // 2), width), low)]
        + pair_shapes
        + block_shapes
        + [dma((PEERS,)), dma((PEERS,)), dma((PEERS,)), dma((PEERS,)), dma((2,)), dma((2, 4)), dma((4,)), dma((14, 2, 11)), dma((10 + 2 * chunks,))],
        compiler_params=pltpu.CompilerParams(
            collective_id=1, has_side_effects=True, vmem_limit_bytes=60 << 20
        ),
        name="inbound",
    )(rows, grads, slot_line, home_line, box_x, box_y, tables, *shards, vectors)


LAST = 7


def scatter_plan(n, late):
    if late:
        return tuple(range(LAST, LAST + 7))
    return (n // 2, 3 + n, 5 + n, 7 + n, 8 + n, 9 + n, 10 + n)


def outbound_kernel(
    h_result, h_one, h_qkv, h_context, h_homed, h_vec, home_line, slot_line, r_tables, codes, flipped,
    h_whole, g_out, g_up, g_down,
    result_out, arrived_b, table_out, o_qkv, o_out, o_up, o_down,
    packed, arrived_a, loose, table_got, grad_qkv, g_qkv,
    t_qkv, t_out, t_up, t_down, c_qkv, c_out, c_up, c_down, n_qkv, n_out, n_up, n_down,
    f_qkv, f_out, f_up, f_down, z_qkv, z_out, z_up, z_down, e_qkv, e_out, e_up, e_down,
    result_ref, grad_one, qkv, grad_context, homed, vec_grads, w_qkv, tables,
    send_a, recv_a, send_b, recv_b, local_sems, table_sems, piece_sems, fetch_sems, last_sems, load_sems,
):
    where = place()
    me, core, z, y, x = where
    sources = (h_result, h_qkv, h_context, h_homed, h_whole, h_one, h_vec)
    targets = (result_ref, qkv, grad_context, homed, w_qkv, grad_one, vec_grads)
    loads = [
        pltpu.make_async_copy(src, dst, load_sems.at[n])
        for n, (src, dst) in enumerate(zip(sources, targets))
    ]
    for load in loads:
        load.start()
    tables[...] = jnp.zeros_like(tables)
    tables[: r_tables.shape[0], : r_tables.shape[1]] = r_tables[...]
    enter(me, core)
    local = (g_qkv, g_out, g_up, g_down)
    sums = (t_qkv, t_out, t_up, t_down)
    from_core = (c_qkv, c_out, c_up, c_down)
    from_near = (n_qkv, n_out, n_up, n_down)
    from_far = (f_qkv, f_out, f_up, f_down)
    from_z = (z_qkv, z_out, z_up, z_down)
    ends = (e_qkv, e_out, e_up, e_down)
    outs = (o_qkv, o_out, o_up, o_down)
    low = jnp.bfloat16
    tasks = []
    for i in (3, 2, 1, 0):
        refs = (local[i], sums[i], from_core[i], from_near[i], from_far[i], from_z[i])
        for pair in pieces_of(sums[i].shape[3], sums[i].shape[4]):
            n = len(tasks)
            pair = [
                Scatter(where, *refs, fetch_sems.at[2 * n + j], piece, piece_sems.at[2 * n + j])
                for j, piece in enumerate(pair)
            ]
            tasks.append((pair, scatter_plan(n, i == 0)))
    step, steps = stepper(tasks)
    moved = Exchange(where, packed, arrived_a, loose, send_a, recv_a, local_sems.at[0])
    moved_grad = Exchange(where, packed, arrived_b, loose, send_b, recv_b, local_sems.at[1])
    devices = [(me, 1 - core), (me ^ 1, core), (me ^ 2, core), (me ^ 4, core), (me ^ 8, core)]
    shares = [
        remote(table_got.at[0, n], table_got.at[1, n], table_sems.at[0, n], table_sems.at[1, n], device)
        for n, device in enumerate(devices)
    ]

    table_out[...] = jnp.zeros_like(table_out)
    step(0)
    loads[0].wait()
    moved.pack(result_ref, home_line)
    for load in loads[1:]:
        load.wait()

    def one(pair, carry):
        attend_pair_back(pair, qkv, grad_context, tables, codes, flipped, grad_qkv, table_out)
        for j in range(PAIRS):

            @pl.when(pair == j)
            def _(j=j):
                step(1 + j)

        return carry

    lax.fori_loop(0, PAIRS, one, 0)
    width = homed.shape[1]
    sums_of = []
    in_home = grad_one[...]
    for n in range(3):
        part = grad_qkv[:, n * width : (n + 1) * width]
        g_qkv[:, :, :, :, n * width : (n + 1) * width] = (
            lax.dot_general(homed[...], part, TN, preferred_element_type=jnp.float32)
            .astype(low)
            .reshape(*g_qkv.shape[:4], width)
        )
        sums_of.append(jnp.sum(part.astype(jnp.float32), axis=0, keepdims=True))
        weights = w_qkv[:, :, :, :, n * width : (n + 1) * width].reshape(width, width)
        in_home = in_home + lax.dot_general(part, weights, NT, preferred_element_type=jnp.float32)
    row = lax.broadcasted_iota(jnp.int32, (128, width), 0)
    lines = jnp.where(row == 0, sums_of[0], jnp.where(row == 1, sums_of[2], vec_grads[...]))
    beside = lines.T.astype(low).reshape(*g_qkv.shape[:4], 128)
    g_qkv[:, :, :, :, 3 * width : 3 * width + 128] = beside
    g_qkv[:, :, :, :, 3 * width + 128 :] = jnp.zeros_like(beside)
    step(LAST)
    moved.wait()
    moved_grad.pack(in_home.astype(low), home_line)
    moved.unpack(slot_line, result_out, low)
    for k in range(LAST + 1, steps):
        step(k)
        n = k - LAST - 1
        if 0 < n <= 5:
            shares[n - 1].wait_recv()
            table_out[...] += table_got[1, n - 1]
        if n < 5:
            table_got[0, n] = table_out[...]
            shares[n].start()
    finals = []
    for i in (3, 2, 1, 0):
        block = sums[i][z, y, x].astype(jnp.float32)
        rows = block.shape[0] // 2
        ends[i][0] = block[:rows]
        ends[i][1] = block[rows:]
        outs[i][core] = ends[i][core]
        copy = remote(ends[i].at[1 - core], outs[i].at[core], last_sems.at[0, i], last_sems.at[1, i], (me, 1 - core))
        copy.start()
        finals.append(copy)
    moved_grad.wait()
    for copy in finals:
        copy.wait()
    for share in shares:
        share.wait_send()
    for pair, _ in tasks:
        for task in pair:
            task.sent()


def outbound(result, grad_one, qkv, grad_context, homed, vec_grads, home_line, slot_line, tables, codes, flipped, w_qkv, locals_):
    tokens, width = result.shape
    slots = 2 * (2 * tokens // PEERS)
    low = jnp.bfloat16
    buffer = pltpu.VMEM((PEERS, slots, width // 2), low)
    halves = [(g.shape[3], g.shape[4] // 2) for g in (w_qkv, *locals_)]
    scratch = (
        [buffer] * 2
        + [pltpu.VMEM((PEERS * (slots // 2), width), low)]
        + [pltpu.VMEM((2, 5, 16, 256), jnp.float32)]
        + [pltpu.VMEM(qkv.shape, low), pltpu.VMEM(w_qkv.shape, low)]
        + [pltpu.VMEM((4, 2, 2, r, h), low) for r, h in halves]
        + [pltpu.VMEM((4, 2, 2, r, h), low) for r, h in halves]
        + [pltpu.VMEM((4, 2, r, h), low) for r, h in halves]
        + [pltpu.VMEM((4, r, h), low) for r, h in halves]
        + [pltpu.VMEM((2, 4, r, h), low) for r, h in halves]
        + [pltpu.VMEM((2, r // 2, h), jnp.float32) for r, h in halves]
        + [pltpu.VMEM(a.shape, a.dtype) for a in (result, grad_one, qkv, grad_context, homed, vec_grads, w_qkv)]
        + [pltpu.VMEM((16, 256), jnp.float32)]
    )
    dma = pltpu.SemaphoreType.DMA
    return pl.pallas_call(
        outbound_kernel,
        out_shape=[
            jax.ShapeDtypeStruct(result.shape, low),
            jax.ShapeDtypeStruct((PEERS, slots, width // 2), low),
            jax.ShapeDtypeStruct((16, 256), jnp.float32),
        ]
        + [jax.ShapeDtypeStruct((2, r // 2, h), jnp.float32) for r, h in halves],
        in_specs=[pl.BlockSpec(memory_space=pl.ANY)] * 6
        + vmem(5)
        + [pl.BlockSpec(memory_space=pl.ANY)] * 4,
        out_specs=vmem(7),
        scratch_shapes=scratch
        + [dma((PEERS,)), dma((PEERS,)), dma((PEERS,)), dma((PEERS,)), dma((2,)), dma((2, 5)), dma((14, 2, 5)), dma((14,)), dma((2, 4)), dma((7,))],
        compiler_params=pltpu.CompilerParams(
            collective_id=2, has_side_effects=True, vmem_limit_bytes=60 << 20
        ),
        name="outbound",
    )(result, grad_one, qkv, grad_context, homed, vec_grads, home_line, slot_line, tables, codes, flipped, w_qkv, *locals_)


def finish_kernel(
    arrived, slot_line, moved_rows, table_sum, e_qkv, e_out, e_up, e_down, p_qkv, p_out, p_up, p_down, p_vec, p_rel,
    m_qkv, m_out, m_up, m_down, m_vec, m_rel, v_qkv, v_out, v_up, v_down, v_vec, v_rel,
    layer_out, in_grad, a_qkv, a_out, a_up, a_down, a_vec, a_rel, f_qkv, f_out, f_up, f_down, f_vec, f_rel,
    s_qkv, s_out, s_up, s_down, s_vec, s_rel, u_qkv, u_out, u_up, u_down, u_vec, u_rel, loose,
):
    layer_out[...] = moved_rows[...]
    in_grad[...] = unpacked(arrived, loose, slot_line)
    ends = (e_qkv, e_out, e_up, e_down)
    params = (p_qkv, p_out, p_up, p_down, p_vec, p_rel)
    moments = (m_qkv, m_out, m_up, m_down, m_vec, m_rel)
    squares = (v_qkv, v_out, v_up, v_down, v_vec, v_rel)
    grads = (a_qkv, a_out, a_up, a_down, a_vec, a_rel)
    firsts = (f_qkv, f_out, f_up, f_down, f_vec, f_rel)
    seconds = (s_qkv, s_out, s_up, s_down, s_vec, s_rel)
    updates = (u_qkv, u_out, u_up, u_down, u_vec, u_rel)

    def adam(i, grad, columns):
        rate = DECAY_RATE if i < 4 else 0.0
        param = params[i][:, columns].astype(jnp.float32)
        new = adam_step(param, grad, moments[i][:, columns], squares[i][:, columns], rate)
        for ref, value in zip((grads[i], firsts[i], seconds[i], updates[i]), (grad, *new)):
            ref[:, columns] = value

    for i in range(4):
        half = ends[i].shape[2]
        width = params[i].shape[1]
        adam(i, ends[i][0], slice(0, half))
        adam(i, ends[i][1][:, : width - half], slice(half, width))
    kinds, features = params[4].shape
    rest = params[0].shape[1] - ends[0].shape[2]
    turned = ends[0][1][:, rest : rest + 128].T
    adam(4, turned[:kinds], slice(0, features))
    heads, entries = params[5].shape
    adam(5, table_sum[:heads, :entries], slice(0, entries))


def finish(arrived, slot_line, moved_rows, table_sum, ends, params, moments, squares):
    f32 = jnp.float32
    tokens, width = moved_rows.shape
    like = [jax.ShapeDtypeStruct(param.shape, f32) for param in params]
    return pl.pallas_call(
        finish_kernel,
        out_shape=[
            jax.ShapeDtypeStruct((tokens, width), jnp.bfloat16),
            jax.ShapeDtypeStruct((tokens, width), f32),
        ]
        + like * 4,
        in_specs=vmem(4 + 4 + 18),
        out_specs=vmem(2 + 24),
        scratch_shapes=[pltpu.VMEM((PEERS * (arrived.shape[1] // 2), width), jnp.bfloat16)],
        compiler_params=pltpu.CompilerParams(vmem_limit_bytes=60 << 20),
        name="finish",
    )(arrived, slot_line, moved_rows, table_sum, *ends, *params, *moments, *squares)


def per_device(
    layer_in,
    out_grad,
    w_qkv,
    w_out,
    w_up,
    w_down,
    vectors,
    relative,
    first_qkv,
    second_qkv,
    first_out,
    second_out,
    first_up,
    second_up,
    first_down,
    second_down,
    first_vectors,
    second_vectors,
    first_relative,
    second_relative,
    token_slot,
    home_index,
    box_x,
    box_y,
):
    homed, qkv, whole_qkv, codes, flipped, result, grad_one, grad_context, *local_grads, vec_grads = inbound(
        layer_in[0],
        out_grad[0],
        token_slot,
        home_index,
        box_x,
        box_y,
        relative,
        [w_qkv, w_out, w_up, w_down],
        vectors,
    )
    moved_rows, arrived, table_sum, *ends = outbound(
        result,
        grad_one,
        qkv,
        grad_context,
        homed,
        vec_grads,
        home_index,
        token_slot,
        relative,
        codes,
        flipped,
        whole_qkv,
        local_grads,
    )
    layer_out, in_grad, *new = finish(
        arrived,
        token_slot,
        moved_rows,
        table_sum,
        ends,
        [w_qkv, w_out, w_up, w_down, vectors, relative],
        [first_qkv, first_out, first_up, first_down, first_vectors, first_relative],
        [second_qkv, second_out, second_up, second_down, second_vectors, second_relative],
    )
    by_weight = [new[6 * kind + i] for i in range(6) for kind in range(4)]
    return (layer_out[None], in_grad[None], *by_weight)


def spread_device(
    layer_in,
    out_grad,
    w_qkv,
    w_out,
    w_up,
    w_down,
    vectors,
    relative,
    first_qkv,
    second_qkv,
    first_out,
    second_out,
    first_up,
    second_up,
    first_down,
    second_down,
    first_vectors,
    second_vectors,
    first_relative,
    second_relative,
    token_slot,
    home_index,
    box_x,
    box_y,
):
    tokens = layer_in[0]
    rows_dev = tokens.shape[0]
    model_dim = tokens.shape[1]
    groups = lax.axis_size(REGIONS)
    slot_cap = 2 * rows_dev // groups
    page_num = rows_dev // PAGE
    slot_of = token_slot[0]
    home_rows = home_index[0]
    full_qkv, full_out, full_up, full_down, full_vec = (
        lax.all_gather(w_qkv, BOTH, axis=0, tiled=True),
        lax.all_gather(w_out, BOTH, axis=0, tiled=True),
        lax.all_gather(w_up, BOTH, axis=0, tiled=True),
        lax.all_gather(w_down, BOTH, axis=0, tiled=True),
        lax.all_gather(vectors, BOTH, axis=1, tiled=True),
    )
    vec_rows = full_vec.astype(jnp.float32)
    qkv_bias = jnp.concatenate([vec_rows[0], jnp.zeros_like(vec_rows[0]), vec_rows[1]])
    code_rows = position_codes(box_x[0].reshape(page_num, PAGE), box_y[0].reshape(page_num, PAGE))
    bias_mats = bias_table(relative)
    homed = exchange(tokens, slot_of, home_rows, groups, slot_cap).astype(jnp.bfloat16)
    cotangent = exchange(out_grad[0], slot_of, home_rows, groups, slot_cap)
    projected = (jnp.dot(homed, full_qkv, preferred_element_type=jnp.float32) + qkv_bias).astype(
        jnp.bfloat16
    )
    paged = projected.reshape(page_num, PAGE, 3 * model_dim)
    context_pages, log_totals = lax.map(
        lambda member: page_forward(member[0], member[1], bias_mats), (paged, code_rows)
    )
    context = context_pages.reshape(rows_dev, model_dim)
    attn_out = jnp.dot(context, full_out, preferred_element_type=jnp.float32) + vec_rows[2]
    hidden, normed_one, spread_one = norm_forward(
        homed.astype(jnp.float32) + attn_out, vec_rows[3], vec_rows[4]
    )
    hidden_low = hidden.astype(jnp.bfloat16)
    pre_act = jnp.dot(hidden_low, full_up, preferred_element_type=jnp.float32) + vec_rows[
        8:12
    ].reshape(-1)
    activated, gelu_back = jax.vjp(lambda value: jax.nn.gelu(value, approximate=False), pre_act)
    act_low = activated.astype(jnp.bfloat16)
    branch = jnp.dot(act_low, full_down, preferred_element_type=jnp.float32) + vec_rows[5]
    result, normed_two, spread_two = norm_forward(hidden + branch, vec_rows[6], vec_rows[7])
    grad_two, grad_gain_two, grad_shift_two = norm_back(
        cotangent, normed_two, spread_two, vec_rows[6]
    )
    grad_branch = grad_two.astype(jnp.bfloat16)
    grad_down = jnp.einsum("tf,td->fd", act_low, grad_branch, preferred_element_type=jnp.float32)
    grad_act = jnp.einsum("td,fd->tf", grad_branch, full_down, preferred_element_type=jnp.float32)
    grad_pre = gelu_back(grad_act)[0].astype(jnp.bfloat16)
    grad_up = jnp.einsum("td,tf->df", hidden_low, grad_pre, preferred_element_type=jnp.float32)
    grad_hidden = grad_two + jnp.einsum(
        "tf,df->td", grad_pre, full_up, preferred_element_type=jnp.float32
    )
    grad_one, grad_gain_one, grad_shift_one = norm_back(
        grad_hidden, normed_one, spread_one, vec_rows[3]
    )
    grad_attn = grad_one.astype(jnp.bfloat16)
    grad_out = jnp.einsum("td,te->de", context, grad_attn, preferred_element_type=jnp.float32)
    grad_context = jnp.einsum(
        "te,de->td", grad_attn, full_out, preferred_element_type=jnp.float32
    ).astype(jnp.bfloat16)
    grad_home = grad_context.reshape(page_num, PAGE, model_dim)
    grad_pages, mats_pages = lax.map(
        lambda member: page_backward(member[0], member[1], member[2], member[3], bias_mats),
        (paged, code_rows, log_totals, grad_home),
    )
    grad_dense = grad_pages.reshape(rows_dev, 3 * model_dim)
    bias_sums = jnp.sum(grad_dense.astype(jnp.float32), axis=0)
    grad_qkv = jnp.einsum("td,tf->df", homed, grad_dense, preferred_element_type=jnp.float32)
    in_home = grad_one + jnp.einsum(
        "tf,df->td", grad_dense, full_qkv, preferred_element_type=jnp.float32
    )
    layer_out = exchange(result.astype(jnp.bfloat16), home_rows, slot_of, groups, slot_cap)
    in_grad = exchange(in_home.astype(jnp.bfloat16), home_rows, slot_of, groups, slot_cap)
    grad_vec = jnp.concatenate(
        [
            jnp.stack(
                [
                    bias_sums[:model_dim],
                    bias_sums[2 * model_dim :],
                    jnp.sum(grad_attn.astype(jnp.float32), axis=0),
                    grad_gain_one,
                    grad_shift_one,
                    jnp.sum(grad_branch.astype(jnp.float32), axis=0),
                    grad_gain_two,
                    grad_shift_two,
                ]
            ),
            jnp.sum(grad_pre.astype(jnp.float32), axis=0).reshape(4, model_dim),
        ],
        axis=0,
    )
    grad_qkv, grad_out, grad_up, grad_down, grad_vectors = (
        lax.psum_scatter(grad_qkv, BOTH, scatter_dimension=0, tiled=True),
        lax.psum_scatter(grad_out, BOTH, scatter_dimension=0, tiled=True),
        lax.psum_scatter(grad_up, BOTH, scatter_dimension=0, tiled=True),
        lax.psum_scatter(grad_down, BOTH, scatter_dimension=0, tiled=True),
        lax.psum_scatter(grad_vec, BOTH, scatter_dimension=1, tiled=True),
    )
    mats_total = jnp.sum(mats_pages, axis=0)
    table_back = jax.vjp(bias_table, relative)[1]
    grad_relative = lax.psum(table_back(mats_total)[0], BOTH)
    firsts_qkv, seconds_qkv, update_qkv = adam_step(
        w_qkv.astype(jnp.float32), grad_qkv, first_qkv, second_qkv, DECAY_RATE
    )
    firsts_out, seconds_out, update_out = adam_step(
        w_out.astype(jnp.float32), grad_out, first_out, second_out, DECAY_RATE
    )
    firsts_up, seconds_up, update_up = adam_step(
        w_up.astype(jnp.float32), grad_up, first_up, second_up, DECAY_RATE
    )
    firsts_down, seconds_down, update_down = adam_step(
        w_down.astype(jnp.float32), grad_down, first_down, second_down, DECAY_RATE
    )
    firsts_vectors, seconds_vectors, update_vectors = adam_step(
        vectors.astype(jnp.float32), grad_vectors, first_vectors, second_vectors, 0.0
    )
    firsts_relative, seconds_relative, update_relative = adam_step(
        relative, grad_relative, first_relative, second_relative, 0.0
    )
    return (
        layer_out.astype(jnp.bfloat16)[None],
        in_grad[None],
        grad_qkv,
        firsts_qkv,
        seconds_qkv,
        update_qkv,
        grad_out,
        firsts_out,
        seconds_out,
        update_out,
        grad_up,
        firsts_up,
        seconds_up,
        update_up,
        grad_down,
        firsts_down,
        seconds_down,
        update_down,
        grad_vectors,
        firsts_vectors,
        seconds_vectors,
        update_vectors,
        grad_relative,
        firsts_relative,
        seconds_relative,
        update_relative,
    )


def solution(mesh):
    kernels = mesh.shape[REGIONS] == PEERS and mesh.shape[SHARD] == 2
    return jax.shard_map(
        per_device if kernels else spread_device,
        mesh=mesh,
        in_specs=(
            P(SHARD, REGIONS, None),
            P(SHARD, REGIONS, None),
            P(BOTH, None),
            P(BOTH, None),
            P(BOTH, None),
            P(BOTH, None),
            P(None, BOTH),
            P(),
            P(BOTH, None),
            P(BOTH, None),
            P(BOTH, None),
            P(BOTH, None),
            P(BOTH, None),
            P(BOTH, None),
            P(BOTH, None),
            P(BOTH, None),
            P(None, BOTH),
            P(None, BOTH),
            P(),
            P(),
            P(SHARD, REGIONS),
            P(SHARD, REGIONS),
            P(SHARD, REGIONS),
            P(SHARD, REGIONS),
        ),
        out_specs=(
            P(SHARD, REGIONS, None),
            P(SHARD, REGIONS, None),
            P(BOTH, None),
            P(BOTH, None),
            P(BOTH, None),
            P(BOTH, None),
            P(BOTH, None),
            P(BOTH, None),
            P(BOTH, None),
            P(BOTH, None),
            P(BOTH, None),
            P(BOTH, None),
            P(BOTH, None),
            P(BOTH, None),
            P(BOTH, None),
            P(BOTH, None),
            P(BOTH, None),
            P(BOTH, None),
            P(None, BOTH),
            P(None, BOTH),
            P(None, BOTH),
            P(None, BOTH),
            P(),
            P(),
            P(),
            P(),
        ),
        check_vma=False,
    )
```

```python
import functools

import jax
import jax.numpy as jnp
import numpy as np
from jax import lax
from jax.experimental import pallas as pl
from jax.experimental.pallas import tpu as pltpu
from jax.sharding import PartitionSpec as P

REGIONS, SHARD = "regions", "shard"
BOTH = (REGIONS, SHARD)
HEADS = 12
HEAD = 64
PAGE = 576


PRECISE = lax.Precision.HIGHEST
EPS_NORM = 1e-05
BETA_ONE = 0.9
BETA_TWO = 0.999
ADAM_EPS = 1e-08
LAYER_FACTOR = 0.5625
DECAY_RATE = 0.05
STEP_COUNT = 10.0


def skewed(line, size):
    count = line.shape[0]
    wide = jnp.pad(line, ((0, 0), (0, 1)))
    flat = jnp.broadcast_to(wide[:, None, :], (count, size, 2 * size)).reshape(count, -1)
    rows = flat[:, : size * (2 * size - 1)].reshape(count, size, 2 * size - 1)
    return rows[:, :, size - 1 :]


def bias_table(relative):
    seq = skewed(relative[:, :127], 64)
    horizontal = skewed(relative[:, 127:190], 32)
    vertical = skewed(relative[:, 190:253], 32)
    return (
        jnp.pad(seq, ((0, 0), (0, 64), (0, 64)))
        + jnp.pad(horizontal, ((0, 0), (64, 32), (64, 32)))
        + jnp.pad(vertical, ((0, 0), (96, 0), (96, 0)))
    )


def position_codes(box_x, box_y):
    places = jnp.arange(PAGE, dtype=jnp.int32)
    seq_bucket = places * 64 // PAGE
    columns = jnp.arange(128, dtype=jnp.int32)
    matched = (
        (columns[None, None, :] == seq_bucket[None, :, None])
        | (columns == 64 + box_x[..., None])
        | (columns == 96 + box_y[..., None])
    )
    return matched.astype(jnp.float32)


def layout_bias(code_rows, bias_mats):
    lifted = jnp.einsum("pa,hab->hpb", code_rows, bias_mats, precision=PRECISE)
    return jnp.einsum("hpb,qb->hpq", lifted, code_rows, precision=PRECISE)


def page_scores(page_qkv, code_rows, bias_mats):
    parted = page_qkv.reshape(PAGE, 3, HEADS, HEAD)
    queries = parted[:, 0]
    key_rows = parted[:, 1]
    values = parted[:, 2]
    scores = jnp.einsum(
        "phd,qhd->hpq", queries, key_rows, preferred_element_type=jnp.float32
    ) * 0.125 + layout_bias(code_rows, bias_mats)
    return (queries, key_rows, values, scores)


def page_forward(page_qkv, code_rows, bias_mats):
    queries, key_rows, values, scores = page_scores(page_qkv, code_rows, bias_mats)
    row_max = jnp.max(scores, axis=2, keepdims=True)
    raised = jnp.exp(scores - row_max)
    totals = jnp.sum(raised, axis=2, keepdims=True)
    attn_w = (raised / totals).astype(jnp.bfloat16)
    context = jnp.einsum("hpq,qhd->phd", attn_w, values, preferred_element_type=jnp.float32)
    log_total = (row_max + jnp.log(totals))[..., 0]
    return (context.reshape(PAGE, HEADS * HEAD).astype(jnp.bfloat16), log_total)


def page_backward(page_qkv, code_rows, log_total, grad_ctx, bias_mats):
    queries, key_rows, values, scores = page_scores(page_qkv, code_rows, bias_mats)
    chances = jnp.exp(scores - log_total[..., None])
    attn_w = chances.astype(jnp.bfloat16)
    grad_heads = grad_ctx.reshape(PAGE, HEADS, HEAD)
    grad_values = jnp.einsum("hpq,phd->qhd", attn_w, grad_heads, preferred_element_type=jnp.float32)
    grad_chances = jnp.einsum(
        "phd,qhd->hpq", grad_heads, values, preferred_element_type=jnp.float32
    )
    inner = jnp.sum(chances * grad_chances, axis=2, keepdims=True)
    grad_scores = (chances * (grad_chances - inner)).astype(jnp.bfloat16)
    grad_queries = (
        jnp.einsum("hpq,qhd->phd", grad_scores, key_rows, preferred_element_type=jnp.float32)
        * 0.125
    )
    grad_keys = (
        jnp.einsum("hpq,phd->qhd", grad_scores, queries, preferred_element_type=jnp.float32) * 0.125
    )
    partial_codes = jnp.einsum(
        "hpq,qb->hpb",
        grad_scores,
        code_rows.astype(jnp.bfloat16),
        preferred_element_type=jnp.float32,
    )
    grad_mats = jnp.einsum("pa,hpb->hab", code_rows, partial_codes, precision=PRECISE)
    grad_page = jnp.stack([grad_queries, grad_keys, grad_values], axis=1).reshape(
        PAGE, 3 * HEADS * HEAD
    )
    return (grad_page.astype(jnp.bfloat16), grad_mats)


def exchange(rows, targets, picks, groups, slot_cap):
    slots = groups * slot_cap
    places = jnp.arange(slots, dtype=jnp.int32)
    packing = (places[:, None] == targets[None, :]).astype(jnp.bfloat16)
    packed = jnp.dot(packing, rows, preferred_element_type=jnp.float32).astype(jnp.bfloat16)
    arrived = lax.all_to_all(
        packed.reshape(groups, slot_cap, rows.shape[1]),
        REGIONS,
        split_axis=0,
        concat_axis=0,
        tiled=True,
    ).reshape(slots, rows.shape[1])
    picking = (picks[:, None] == places[None, :]).astype(jnp.bfloat16)
    return jnp.dot(picking, arrived, preferred_element_type=jnp.float32)


def norm_forward(rows, gain, shift):
    centre = rows - jnp.mean(rows, axis=-1, keepdims=True)
    spread = lax.rsqrt(jnp.mean(centre * centre, axis=-1, keepdims=True) + EPS_NORM)
    normed = centre * spread
    return (normed * gain + shift, normed, spread)


def norm_back(incoming, normed, spread, gain):
    scaled = incoming * gain
    grad_rows = spread * (
        scaled
        - jnp.mean(scaled, axis=-1, keepdims=True)
        - normed * jnp.mean(scaled * normed, axis=-1, keepdims=True)
    )
    return (grad_rows, jnp.sum(incoming * normed, axis=0), jnp.sum(incoming, axis=0))


def adam_step(param, grad, moment, square, decay):
    moment_new = BETA_ONE * moment + (1.0 - BETA_ONE) * grad
    square_new = BETA_TWO * square + (1.0 - BETA_TWO) * grad * grad
    moment_hat = moment_new / (1.0 - BETA_ONE**STEP_COUNT)
    square_hat = square_new / (1.0 - BETA_TWO**STEP_COUNT)
    update = LAYER_FACTOR * (moment_hat / (jnp.sqrt(square_hat) + ADAM_EPS) + decay * param)
    return (moment_new, square_new, update)


ROWS = 576


def softly(scores, axis):
    peak = jnp.max(scores, axis=axis, keepdims=True)
    raised = jnp.exp(scores - peak)
    return raised * (1.0 / jnp.sum(raised, axis=axis, keepdims=True))


def head_lift(tables, codes, h):
    line = tables[pl.ds(h, 1), :]
    lane = lax.broadcasted_iota(jnp.int32, (64, 128), 1)

    def spread(entry, size, low, high):
        if low == 0:
            start = pltpu.roll(line[:, :128], 128 - entry, 1)
        else:
            start = pltpu.roll(line, 256 - entry, 1)[:, :128]
        turned = pltpu.roll(jnp.broadcast_to(start, (size, 128)), 0, 1, stride=1, stride_axis=0)
        return jnp.where((lane[:size] >= low) & (lane[:size] < high), turned, 0.0)

    table = jnp.concatenate(
        [spread(63, 64, 0, 64), spread(94, 32, 64, 96), spread(125, 32, 96, 128)], axis=0
    )
    high = table.astype(jnp.bfloat16)
    low = (table - high.astype(jnp.float32)).astype(jnp.bfloat16)
    both = jnp.concatenate([high, low], axis=1)
    return jnp.dot(codes, both, preferred_element_type=jnp.float32).astype(jnp.bfloat16)


def lane_mask(rows, h):
    lane = lax.broadcasted_iota(jnp.int32, (rows, 128), 1)
    return (lane < 64) if h == 0 else (lane >= 64)


def pair_columns(qkv, pair):
    width = qkv.shape[1] // 3
    at = [pl.multiple_of(n * width + pair * 128, 128) for n in range(3)]
    return [qkv[:, pl.ds(a, 128)] for a in at]


NT = (((1,), (1,)), ((), ()))
TN = (((0,), (0,)), ((), ()))


def attend_pair(pair, qkv, tables, codes_ref, context):
    count = qkv.shape[0]
    codes = codes_ref[...]
    queries, keys, values = pair_columns(qkv, pair)
    right = jnp.concatenate([keys, codes, codes], axis=1)
    scaled = queries * jnp.bfloat16(0.125)
    results = []
    for h in range(2):
        mine = jnp.where(lane_mask(count, h), scaled, jnp.zeros_like(scaled))
        left = jnp.concatenate([mine, head_lift(tables, codes, 2 * pair + h)], axis=1)
        parts = []
        for r in range(0, count, ROWS):
            scores = lax.dot_general(left[r : r + ROWS], right, NT, preferred_element_type=jnp.float32)
            weights = softly(scores, 1).astype(jnp.bfloat16)
            parts.append(jnp.dot(weights, values, preferred_element_type=jnp.float32))
        results.append(parts)
    for n, r in enumerate(range(0, count, ROWS)):
        both = jnp.where(lane_mask(ROWS, 0), results[0][n], results[1][n])
        context[pl.ds(r, ROWS), pl.ds(pl.multiple_of(pair * 128, 128), 128)] = both.astype(jnp.bfloat16)


def attend_pair_back(pair, qkv, grad_ref, tables, codes_ref, flipped_ref, grad_qkv, grad_tables):
    count = qkv.shape[0]
    width = qkv.shape[1] // 3
    codes = codes_ref[...]
    queries, keys, values = pair_columns(qkv, pair)
    grads = grad_ref[:, pl.ds(pl.multiple_of(pair * 128, 128), 128)]
    left = jnp.concatenate([keys, codes, codes], axis=1)
    near = jnp.concatenate([keys, codes], axis=1)
    scaled = queries * jnp.bfloat16(0.125)
    out_q, out_k, out_v = [], [], []
    for h in range(2):
        mask = lane_mask(count, h)
        mine = jnp.where(mask, scaled, jnp.zeros_like(scaled))
        mine_grad = jnp.where(mask, grads, jnp.zeros_like(grads))
        right = jnp.concatenate([mine, head_lift(tables, codes, 2 * pair + h)], axis=1)
        total = None
        k_parts, v_parts = [], []
        if True:
            scores = lax.dot_general(left, right, NT, preferred_element_type=jnp.float32)
            chances = softly(scores, 0)
            grad_chances = lax.dot_general(values, mine_grad, NT, preferred_element_type=jnp.float32)
            inner = jnp.sum(chances * grad_chances, axis=0, keepdims=True)
            grad_scores = (chances * (grad_chances - inner)).astype(jnp.bfloat16)
            v_rows = jnp.dot(chances.astype(jnp.bfloat16), grads, preferred_element_type=jnp.float32)
            k_rows = jnp.dot(grad_scores, queries, preferred_element_type=jnp.float32)
            total = lax.dot_general(grad_scores, near, TN, preferred_element_type=jnp.float32)
        out_q.append(total[:, :128])
        out_k.append(k_rows)
        out_v.append(v_rows)
        partial = total[:, 128:]
        high = partial.astype(jnp.bfloat16)
        low = (partial - high.astype(jnp.float32)).astype(jnp.bfloat16)
        mats = lax.dot_general(
            flipped_ref[...], jnp.concatenate([high, low], axis=1), TN, preferred_element_type=jnp.float32
        )
        mats = mats[:, :128] + mats[:, 128:]
        lane = lax.broadcasted_iota(jnp.int32, (64, 128), 1)

        def gathered(row, size, low_lane, high_lane):
            part = jnp.where((lane[:size] >= low_lane) & (lane[:size] < high_lane), mats[row : row + size], 0.0)
            turned = pltpu.roll(part, 0, 1, stride=1, stride_axis=0)
            return jnp.sum(turned, axis=0, keepdims=True)

        blank = jnp.zeros((1, 128), jnp.float32)
        seq, across, down = [
            jnp.concatenate([part, blank], axis=1)
            for part in (gathered(0, 64, 0, 64), gathered(64, 32, 64, 96), pltpu.roll(gathered(96, 32, 96, 128), 32, 1))
        ]
        grad_tables[pl.ds(2 * pair + h, 1), :] = seq + pltpu.roll(across, 63, 1) + pltpu.roll(down, 190, 1)
    mask = lane_mask(count, 0)
    for n, (parts, factor) in enumerate(((out_q, 0.125), (out_k, 0.125), (out_v, 1.0))):
        both = jnp.where(mask, parts[0], parts[1]) * factor
        grad_qkv[:, pl.ds(pl.multiple_of(n * width + pair * 128, 128), 128)] = both.astype(jnp.bfloat16)


def code_rows_of(box_x, box_y, flip):
    count = box_x.shape[1]
    column = lax.broadcasted_iota(jnp.int32, (128, count), 0)
    row = lax.broadcasted_iota(jnp.int32, (128, count), 1)
    start = (63 - column if flip else column) * (count // 64)
    hit_seq = (column < 64) & (row >= start) & (row < start + count // 64)
    across, down = box_x[...], box_y[...]
    if flip:
        across, down = 31 - across, 31 - down
    hit = hit_seq | (column == 64 + across) | (column == 96 + down)
    return jnp.where(hit, 1.0, 0.0).T.astype(jnp.bfloat16)


def as_columns(line):
    wide = jnp.broadcast_to(line[...].astype(jnp.float32), (128, line.shape[1]))
    return wide.T.astype(jnp.int32)


MESH = pl.DeviceIdType.MESH
PEERS = 16
VEC_COLS = 256


def place():
    me = lax.axis_index(REGIONS)
    core = lax.axis_index(SHARD)
    z = lax.div(me, 4)
    y = lax.div(lax.rem(me, 4), 2)
    x = lax.rem(me, 2)
    return me, core, z, y, x


def enter(me, core):
    barrier = pltpu.get_barrier_semaphore()
    for k in range(1, PEERS):
        pl.semaphore_signal(barrier, inc=1, device_id=(me ^ k, core), device_id_type=MESH)
    pl.semaphore_signal(barrier, inc=1, device_id=(me, 1 - core), device_id_type=MESH)
    pl.semaphore_wait(barrier, PEERS)


def remote(src, dst, send, recv, device):
    return pltpu.make_async_remote_copy(
        src_ref=src, dst_ref=dst, send_sem=send, recv_sem=recv, device_id=device, device_id_type=MESH
    )


class Exchange:
    def __init__(self, where, packed, arrived, loose, send, recv, local):
        self.me, self.core = where[0], where[1]
        self.packed, self.arrived, self.loose = packed, arrived, loose
        self.send, self.recv, self.local = send, recv, local
        self.slots, self.half = packed.shape[1], packed.shape[2]

    def pack(self, rows, slot_of):
        count = self.slots // 2
        for j in range(4):
            group = lax.div(self.me, 4) ^ j
            at = lax.broadcasted_iota(jnp.int32, (4 * count, rows.shape[0]), 0) + group * (4 * count)
            picking = jnp.where(at == slot_of[...], 1.0, 0.0).astype(jnp.bfloat16)
            block = jnp.dot(picking, rows[...], preferred_element_type=jnp.float32)
            for n in range(4):
                own = block[n * count : (n + 1) * count]
                both = jnp.concatenate([own[:, : self.half], own[:, self.half :]], axis=0)
                self.packed[4 * group + n] = both.astype(jnp.bfloat16)
            for k in range(4):
                if j + k:
                    self.copy(4 * j + k).start()
                else:
                    self.own().start()

    def copy(self, k):
        d = self.me ^ k
        return remote(
            self.packed.at[d], self.arrived.at[self.me], self.send.at[k], self.recv.at[k], (d, self.core)
        )

    def own(self):
        return pltpu.make_async_copy(self.packed.at[self.me], self.arrived.at[self.me], self.local)

    def wait(self):
        self.own().wait()

        def one(k, carry):
            self.copy(k).wait()
            return carry

        lax.fori_loop(1, PEERS, one, 0)

    def unpack(self, slot_of, out, kind):
        out[...] = unpacked(self.arrived, self.loose, slot_of).astype(kind)


def unpacked(arrived, loose, slot_of):
    count = arrived.shape[1] // 2
    rows = []
    for n in range(PEERS):
        block = arrived[n].astype(jnp.float32)
        rows.append(jnp.concatenate([block[:count], block[count:]], axis=1))
        if n % 2:
            pair = jnp.concatenate(rows, axis=0)
            loose[pl.ds((n - 1) * count, 2 * count)] = pair.astype(jnp.bfloat16)
            rows = []
    wanted = as_columns(slot_of)
    lane = lax.broadcasted_iota(jnp.int32, wanted.shape, 1)
    picking = jnp.concatenate(
        [
            jnp.where(lane + first == wanted, 1.0, 0.0).astype(jnp.bfloat16)
            for first in range(0, PEERS * count, 128)
        ],
        axis=1,
    )
    return jnp.dot(picking, loose[...], preferred_element_type=jnp.float32)


def pieces_of(rows, half):
    tiles = half // 128
    if rows % 64 == 0:
        cuts = [(n * rows // 4, rows // 4, 0, half) for n in range(4)]
    elif tiles < 4:
        wide = (tiles + 1) // 2 * 128
        cuts = [(0, rows, 0, wide), (0, rows, wide, half - wide)]
    else:
        ends = [0, (tiles + 3) // 4, tiles // 2, tiles - (tiles + 3) // 4, tiles]
        cuts = [(0, rows, 128 * ends[n], 128 * (ends[n + 1] - ends[n])) for n in range(4)]
    return [[(*cuts[n], True), (*cuts[n + 1], False)] for n in range(0, len(cuts), 2)]


class Gather:
    def __init__(self, where, whole, piece, sems):
        self.where, self.whole, self.piece, self.sems = where, whole, piece, sems

    def part(self, z, y, x):
        core = self.where[1]
        r0, rows, c0, cols, _ = self.piece
        half = self.whole.shape[4] // 2
        at = pl.multiple_of(core * half + c0, 128)
        return self.whole.at[z, y, x, pl.ds(r0, rows), pl.ds(at, cols)]

    def along_z(self, t, upward):
        me, core, z, y, x = self.where
        step = 1 if upward else -1
        origin = z - step * t
        ref = self.part(origin, y, x)
        i = 2 * t + (1 if upward else 0)
        return remote(ref, ref, self.sems.at[0, i], self.sems.at[1, i], (me + 4 * step, core))

    def z_sends(self, t, do):
        z = self.where[2]

        @pl.when((z >= t) & (z <= 2))
        def _():
            do(self.along_z(t, True))

        @pl.when((z + t <= 3) & (z >= 1))
        def _():
            do(self.along_z(t, False))

    def z_waits(self, t):
        z = self.where[2]

        @pl.when(z - 1 - t >= 0)
        def _():
            me, core, z, y, x = self.where
            ref = self.part(z - 1 - t, y, x)
            i = 2 * t + 1
            remote(ref, ref, self.sems.at[0, i], self.sems.at[1, i], (me, 1 - core)).wait_recv()

        @pl.when(z + 1 + t <= 3)
        def _():
            me, core, z, y, x = self.where
            ref = self.part(z + 1 + t, y, x)
            i = 2 * t
            remote(ref, ref, self.sems.at[0, i], self.sems.at[1, i], (me, 1 - core)).wait_recv()

    def plane(self, n):
        me, core, z, y, x = self.where
        x_first = self.piece[4]
        every = slice(None)
        other = (me, 1 - core)
        if n == 0:
            ref, device = self.part(every, y, x), (me ^ (1 if x_first else 2), core)
        elif n == 1 and x_first:
            ref, device = self.part(every, y, every), (me ^ 2, core)
        elif n == 1:
            ref, device = self.part(every, every, x), (me ^ 1, core)
        elif n == 2:
            ref, device = self.part(every, y, x), other
        elif n == 3:
            ref, device = (self.part(every, y, 1 - x) if x_first else self.part(every, 1 - y, x)), other
        else:
            ref, device = (self.part(every, 1 - y, every) if x_first else self.part(every, every, 1 - x)), other
        return remote(ref, ref, self.sems.at[0, 6 + n], self.sems.at[1, 6 + n], device)

    def run(self, stage):
        if stage < 3:
            if stage:
                self.z_waits(stage - 1)
            self.z_sends(stage, lambda copy: copy.start())
        elif stage == 3:
            self.z_waits(2)
            self.plane(0).start()
            self.plane(2).start()
        elif stage == 4:
            self.plane(0).wait_recv()
            self.plane(1).start()
            self.plane(3).start()
        elif stage == 5:
            self.plane(1).wait_recv()
            self.plane(4).start()
        else:
            for n in (2, 3, 4):
                self.plane(n).wait_recv()

    def sent(self):
        for t in range(3):
            self.z_sends(t, lambda copy: copy.wait_send())
        for n in range(5):
            self.plane(n).wait_send()


class Scatter:
    def __init__(self, where, local, sums, from_core, from_near, from_far, from_z, fetch, piece, sems):
        self.where, self.local, self.sums, self.piece, self.sems = where, local, sums, piece, sems
        self.from_core, self.from_near, self.from_far, self.from_z = from_core, from_near, from_far, from_z
        self.half, self.fetch = sums.shape[4], fetch

    def cut(self, ref, *lead, core=None):
        r0, rows, c0, cols, _ = self.piece
        at = c0 if core is None else pl.multiple_of(core * self.half + c0, 128)
        return ref.at[(*lead, pl.ds(r0, rows), pl.ds(at, cols))]

    def between_cores(self):
        me, core = self.where[0], self.where[1]
        every = slice(None)
        src = self.cut(self.local, every, every, every, core=1 - core)
        dst = self.cut(self.from_core, every, every, every)
        return remote(src, dst, self.sems.at[0, 0], self.sems.at[1, 0], (me, 1 - core))

    def own_half(self):
        every = slice(None)
        src = self.cut(self.local, every, every, every, core=self.where[1])
        return pltpu.make_async_copy(src, self.cut(self.sums, every, every, every), self.fetch)

    def near(self):
        me, core, z, y, x = self.where
        every = slice(None)
        if self.piece[4]:
            src, device = self.cut(self.sums, every, 1 - y, every), (me ^ 2, core)
        else:
            src, device = self.cut(self.sums, every, every, 1 - x), (me ^ 1, core)
        dst = self.cut(self.from_near, every, every)
        return remote(src, dst, self.sems.at[0, 1], self.sems.at[1, 1], device)

    def far(self):
        me, core, z, y, x = self.where
        every = slice(None)
        if self.piece[4]:
            src, device = self.cut(self.sums, every, y, 1 - x), (me ^ 1, core)
        else:
            src, device = self.cut(self.sums, every, 1 - y, x), (me ^ 2, core)
        dst = self.cut(self.from_far, every)
        return remote(src, dst, self.sems.at[0, 2], self.sems.at[1, 2], device)

    def along_z(self, sender, upward):
        me, core, z, y, x = self.where
        lead = pl.ds(sender + 1, 3 - sender) if upward else pl.ds(0, sender)
        src = self.cut(self.sums, lead, y, x)
        dst = self.cut(self.from_z, 1 if upward else 0, lead)
        i = 3 + (1 if upward else 0)
        step = 4 if upward else -4
        return remote(src, dst, self.sems.at[0, i], self.sems.at[1, i], (me + step, core))

    def add(self, target, other):
        total = target[...].astype(jnp.float32) + other[...].astype(jnp.float32)
        target[...] = total.astype(jnp.bfloat16)

    def z_got(self, sender, upward):
        me, core, z, y, x = self.where
        self.along_z(sender, upward).wait_recv()
        for d in range(sender + 1, 4) if upward else range(sender):
            self.add(self.cut(self.sums, d, y, x), self.cut(self.from_z, 1 if upward else 0, d))

    def run(self, stage):
        me, core, z, y, x = self.where
        if stage == 0:
            self.between_cores().start()
            self.own_half().start()
        elif stage == 1:
            self.own_half().wait()
            self.between_cores().wait_recv()

            def one(i, carry):
                a, b, c = lax.div(i, 4), lax.div(lax.rem(i, 4), 2), lax.rem(i, 2)
                self.add(self.cut(self.sums, a, b, c), self.cut(self.from_core, a, b, c))
                return carry

            lax.fori_loop(0, 16, one, 0)
            self.near().start()
        elif stage == 2:
            self.near().wait_recv()

            def one(i, carry):
                a, b = lax.div(i, 2), lax.rem(i, 2)
                target = self.cut(self.sums, a, y, b) if self.piece[4] else self.cut(self.sums, a, b, x)
                self.add(target, self.cut(self.from_near, a, b))
                return carry

            lax.fori_loop(0, 8, one, 0)
            self.far().start()
        elif stage == 3:
            self.far().wait_recv()

            def one(i, carry):
                self.add(self.cut(self.sums, i, y, x), self.cut(self.from_far, i))
                return carry

            lax.fori_loop(0, 4, one, 0)

            @pl.when(z == 3)
            def _():
                self.along_z(3, False).start()

            @pl.when(z == 0)
            def _():
                self.along_z(0, True).start()

        elif stage == 4:

            @pl.when(z == 2)
            def _():
                self.z_got(3, False)
                self.along_z(2, False).start()

            @pl.when(z == 1)
            def _():
                self.z_got(0, True)
                self.along_z(1, True).start()

        elif stage == 5:

            @pl.when(z == 1)
            def _():
                self.z_got(2, False)
                self.along_z(1, False).start()

            @pl.when(z == 2)
            def _():
                self.z_got(1, True)
                self.along_z(2, True).start()

        elif stage == 6:

            @pl.when(z == 0)
            def _():
                self.z_got(1, False)

            @pl.when(z == 3)
            def _():
                self.z_got(2, True)

    def sent(self):
        z = self.where[2]
        self.between_cores().wait_send()
        self.near().wait_send()
        self.far().wait_send()
        for sender in range(4):

            @pl.when(z == sender)
            def _(sender=sender):
                if sender > 0:
                    self.along_z(sender, False).wait_send()
                if sender < 3:
                    self.along_z(sender, True).wait_send()


def stepper(tasks):
    def step(k):
        for pair, plan in tasks:
            if k in plan:
                for task in pair:
                    task.run(plan.index(k))

    return step, max(plan[-1] for _, plan in tasks) + 1


HOMED, QKV, WHOLE, CODES, FLIPPED, RESULT, ONE, CONTEXT, OUT, VECTORS, DOWN, UP = range(12)


def normed_rows(rows):
    centre = rows - jnp.mean(rows, axis=-1, keepdims=True)
    spread = lax.rsqrt(jnp.mean(centre * centre, axis=-1, keepdims=True) + EPS_NORM)
    return centre * spread, spread


def dense_part(
    homed, cotangent, context, vec, w_out, w_up, w_down,
    result, grad_one_ref, grad_context, g_out, g_up, g_down, vec_grads,
    act, slope, hidden_low, arrive, fetch, save,
):
    width = homed.shape[1]
    chunks = w_up.shape[4] // width
    f32 = jnp.float32
    low = jnp.bfloat16

    def columns(ref, c):
        return ref[:, :, :, :, c * width : (c + 1) * width].reshape(width, width)

    def keep(n, line):
        vec_grads[n : n + 1] = jnp.sum(line, axis=0, keepdims=True)

    attn_out = jnp.dot(context[...], columns(w_out, 0), preferred_element_type=f32) + vec[2:3]
    normed_one, spread_one = normed_rows(homed[...].astype(f32) + attn_out)
    hidden = normed_one * vec[3:4] + vec[4:5]
    hidden_low[...] = hidden.astype(low)
    branch = None
    for c in range(chunks):
        pre = jnp.dot(hidden_low[...], columns(w_up, c), preferred_element_type=f32) + vec[8 + c : 9 + c]
        below = 0.5 * (1.0 + lax.erf(pre * 0.7071067811865476))
        act[c] = (pre * below).astype(low)
        slope[c] = below + pre * (jnp.exp(-0.5 * pre * pre) * 0.3989422804014327)
    arrive()
    for c in range(chunks):
        part = jnp.dot(act[c], w_down[c].reshape(width, width), preferred_element_type=f32)
        branch = part if branch is None else branch + part
    normed_two, spread_two = normed_rows(hidden + branch + vec[5:6])
    result[...] = (normed_two * vec[6:7] + vec[7:8]).astype(low)
    save(RESULT)

    def back(e, normed, spread, gain):
        scaled = e * gain
        return spread * (
            scaled
            - jnp.mean(scaled, axis=-1, keepdims=True)
            - normed * jnp.mean(scaled * normed, axis=-1, keepdims=True)
        )

    fetch()
    e = cotangent[...].astype(f32)
    keep(6, e * normed_two)
    keep(7, e)
    grad_two = back(e, normed_two, spread_two, vec[6:7])
    grad_branch = grad_two.astype(low)
    keep(5, grad_branch.astype(f32))
    grad_hidden = grad_two
    for c in range(chunks):
        if c > 1:
            save(DOWN, c - 2, done=True)
            save(UP, c - 2, done=True)
        g_down[c % 2] = (
            lax.dot_general(act[c], grad_branch, TN, preferred_element_type=f32)
            .astype(low)
            .reshape(g_down.shape[1:])
        )
        save(DOWN, c)
        grad_act = lax.dot_general(
            grad_branch, w_down[c].reshape(width, width), NT, preferred_element_type=f32
        )
        grad_pre = (grad_act * slope[c]).astype(low)
        keep(8 + c, grad_pre.astype(f32))
        g_up[c % 2] = (
            lax.dot_general(hidden_low[...], grad_pre, TN, preferred_element_type=f32)
            .astype(low)
            .reshape(g_up.shape[1:])
        )
        save(UP, c)
        grad_hidden = grad_hidden + lax.dot_general(
            grad_pre, columns(w_up, c), NT, preferred_element_type=f32
        )
    keep(3, grad_hidden * normed_one)
    keep(4, grad_hidden)
    grad_one = back(grad_hidden, normed_one, spread_one, vec[3:4])
    grad_one_ref[...] = grad_one
    save(ONE)
    grad_attn = grad_one.astype(low)
    keep(2, grad_attn.astype(f32))
    g_out[...] = (
        lax.dot_general(context[...], grad_attn, TN, preferred_element_type=f32)
        .astype(low)
        .reshape(g_out.shape)
    )
    save(OUT)
    grad_context[...] = lax.dot_general(
        grad_attn, columns(w_out, 0), NT, preferred_element_type=f32
    ).astype(low)
    vec_grads[0:2] = jnp.zeros((2, width), f32)
    vec_grads[12:] = jnp.zeros((vec_grads.shape[0] - 12, width), f32)
    save(CONTEXT)
    save(VECTORS)


PAIRS = 6
READY = 8
SEND_ROWS = 4


def gather_plan(n, early):
    z, wide = n // 2, 3 + n
    if early:
        return (z, z + 1, z + 2, wide, wide + 1, wide + 2, wide + 3)
    return (z, z + 1, z + 2, wide, wide + 2, wide + 4, wide + 6)


def split_shard(shard, halves, beside=None):
    rows, half = shard.shape[0], halves.shape[2]
    halves[...] = jnp.zeros_like(halves)
    halves[0, :rows] = shard[:, :half]
    if beside is None:
        halves[1, :rows] = shard[:, half:]
    else:
        rest = shard.shape[1] - half
        halves[1, :rows, :rest] = shard[:, half:]
        halves[1, :rows, rest : rest + 128] = beside


def inbound_kernel(
    rows_ref, grad_ref, slot_line, home_line, box_x, box_y, r_tables, r_qkv, r_out, r_up, r_down, r_vec,
    h_homed, h_qkv, h_whole, h_codes, h_flipped, h_result, h_one, h_context, h_out, h_up, h_down, h_vec,
    homed, qkv, w_qkv, codes, flipped, result, grad_one, g_out, vec_grads, g_up, g_down,
    context, vec_rows, w_out, w_up, w_down, act, slope, hidden_low, square, tables,
    s_qkv, s_out, s_up, s_down,
    packed, arrived_a, arrived_b, loose, p_qkv, p_out, p_up, p_down, b_qkv, b_out, b_up, b_down,
    send_a, recv_a, send_b, recv_b, local_sems, pair_sems, block_sems, piece_sems, save_sems,
):
    where = place()
    me, core, z, y, x = where
    width = homed.shape[1]
    cotangent = loose.at[pl.ds(0, homed.shape[0])]
    kept = (
        (homed, h_homed), (qkv, h_qkv), (w_qkv, h_whole), (codes, h_codes), (flipped, h_flipped),
        (result, h_result), (grad_one, h_one), (context, h_context), (g_out, h_out), (vec_grads, h_vec),
        (g_down, h_down), (g_up, h_up),
    )
    saves = {}

    def save(which, c=None, done=False):
        if done:
            saves.pop((which, c)).wait()
            return
        src, dst = kept[which]
        if which == DOWN:
            src, dst = src.at[c % 2], dst.at[c]
        elif which == UP:
            src, dst = src.at[c % 2], dst.at[:, :, :, :, pl.ds(c * width, width)]
        n = which if c is None else DOWN + c + (4 if which == UP else 0)
        saves[which, c] = pltpu.make_async_copy(src, dst, save_sems.at[n])
        saves[which, c].start()

    shards = (s_qkv, s_out, s_up, s_down)
    others = (p_qkv, p_out, p_up, p_down)
    blocks = (b_qkv, b_out, b_up, b_down)
    wholes = (w_qkv, w_out, w_up, w_down)
    tables[...] = jnp.zeros_like(tables)
    tables[: r_tables.shape[0], : r_tables.shape[1]] = r_tables[...]
    square[...] = jnp.zeros_like(square)
    square[: r_vec.shape[0], : r_vec.shape[1]] = r_vec[...].astype(jnp.float32)
    split_shard(r_qkv, s_qkv, square[...].T[: r_qkv.shape[0]].astype(jnp.bfloat16))
    split_shard(r_out, s_out)
    split_shard(r_up, s_up)
    split_shard(r_down, s_down)
    enter(me, core)
    pairs = [
        remote(shards[i].at[1 - core], others[i], pair_sems.at[0, i], pair_sems.at[1, i], (me, 1 - core))
        for i in range(4)
    ]
    for pair in pairs:
        pair.start()
    moved = Exchange(where, packed, arrived_a, loose, send_a, recv_a, local_sems.at[0])
    moved_grad = Exchange(where, packed, arrived_b, loose, send_b, recv_b, local_sems.at[1])
    tasks = []
    for i in range(4):
        for pair in pieces_of(blocks[i].shape[0], blocks[i].shape[1]):
            n = len(tasks)
            pair = [Gather(where, wholes[i], piece, piece_sems.at[2 * n + j]) for j, piece in enumerate(pair)]
            tasks.append((pair, gather_plan(n, i == 0)))
    step, steps = stepper(tasks)

    def assemble(i):
        pairs[i].wait_recv()
        half = blocks[i].shape[1]
        rows = blocks[i].shape[0] // 2
        mine = shards[i][core][:rows].astype(jnp.float32)
        other = others[i][:rows].astype(jnp.float32)
        first = jnp.where(core == 0, mine, other)
        second = jnp.where(core == 0, other, mine)
        blocks[i][...] = jnp.concatenate([first, second], axis=0).astype(jnp.bfloat16)
        at = pl.multiple_of(core * half, 128)
        copy = pltpu.make_async_copy(
            blocks[i], wholes[i].at[z, y, x, :, pl.ds(at, half)], block_sems.at[i]
        )
        copy.start()
        return copy

    assemble(0).wait()
    step(0)
    placed = [assemble(i) for i in range(1, 4)]
    codes[...] = code_rows_of(box_x, box_y, False)
    flipped[...] = code_rows_of(box_x, box_y, True)
    save(CODES)
    save(FLIPPED)
    for copy in placed:
        copy.wait()

    for k in range(1, READY):
        step(k)
        if k == SEND_ROWS:
            moved.pack(rows_ref, slot_line)
    moved.wait()
    moved_grad.pack(grad_ref, slot_line)
    moved.unpack(home_line, homed, jnp.bfloat16)
    columns = w_qkv[:, :, :, :, 3 * width : 3 * width + 128].reshape(width, 128)
    vec_rows[...] = columns.astype(jnp.float32).T[: vec_rows.shape[0]]
    for n in range(3):
        part = w_qkv[:, :, :, :, n * width : (n + 1) * width].reshape(width, width)
        projected = jnp.dot(homed[...], part, preferred_element_type=jnp.float32)
        if n != 1:
            projected = projected + vec_rows[n // 2 : n // 2 + 1]
        qkv[:, n * width : (n + 1) * width] = projected.astype(jnp.bfloat16)
    for which in (HOMED, WHOLE, QKV):
        save(which)

    def one(pair, carry):
        attend_pair(pair, qkv, tables, codes, context)
        for j in range(PAIRS):

            @pl.when(pair == j)
            def _(j=j):
                step(READY + j)

        return carry

    lax.fori_loop(0, PAIRS, one, 0)
    def arrive():
        for k in range(READY + PAIRS, steps):
            step(k)

    def fetch():
        moved_grad.wait()
        moved_grad.unpack(home_line, cotangent, jnp.bfloat16)

    dense_part(
        homed, cotangent, context, vec_rows, w_out, w_up, w_down,
        result, grad_one, context, g_out, g_up, g_down, vec_grads,
        act, slope, hidden_low, arrive, fetch, save,
    )
    for copy in saves.values():
        copy.wait()
    for pair in pairs:
        pair.wait_send()
    for pair, _ in tasks:
        for task in pair:
            task.sent()


def vmem(count):
    return [pl.BlockSpec(memory_space=pltpu.VMEM)] * count


def inbound(rows, grads, slot_line, home_line, box_x, box_y, tables, shards, vectors):
    tokens, width = rows.shape
    slots = 2 * (2 * tokens // PEERS)
    low, f32 = jnp.bfloat16, jnp.float32
    buffer = pltpu.VMEM((PEERS, slots, width // 2), low)
    wholes, halves, pair_shapes, block_shapes = [], [], [], []
    for n, shard in enumerate(shards):
        count, columns = shard.shape
        half = (columns + (VEC_COLS if n == 0 else 0)) // 2
        padded = count + -count % 16
        wholes.append((4, 2, 2, 2 * count, 2 * half))
        halves.append(pltpu.VMEM((2, padded, half), low))
        pair_shapes.append(pltpu.VMEM((padded, half), low))
        block_shapes.append(pltpu.VMEM((2 * count, half), low))
    chunks = wholes[2][4] // width
    dma = pltpu.SemaphoreType.DMA

    def array(shape, kind=low):
        return jax.ShapeDtypeStruct(shape, kind)

    results = [
        array((tokens, width)),
        array((tokens, 3 * width)),
        array(wholes[0]),
        array((tokens, 128)),
        array((tokens, 128)),
        array((tokens, width)),
        array((tokens, width), f32),
        array((tokens, width)),
        *[array(shape) for shape in wholes[1:]],
        array((128, width), f32),
    ]
    return pl.pallas_call(
        inbound_kernel,
        out_shape=results,
        in_specs=vmem(12),
        out_specs=[pl.BlockSpec(memory_space=pl.ANY)] * 12,
        scratch_shapes=[pltpu.VMEM(results[n].shape, results[n].dtype) for n in range(12) if n not in (7, 9, 10)]
        + [
            pltpu.VMEM((2, *wholes[2][:4], width), low),
            pltpu.VMEM((2, *wholes[3][1:]), low),
            pltpu.VMEM((tokens, width), low),
            pltpu.VMEM((16, width), f32),
            *[pltpu.VMEM(shape, low) for shape in wholes[1:]],
            pltpu.VMEM((chunks, tokens, width), low),
            pltpu.VMEM((chunks, tokens, width), f32),
            pltpu.VMEM((tokens, width), low),
            pltpu.VMEM((128, 128), f32),
            pltpu.VMEM((16, 256), f32),
        ]
        + halves
        + [buffer] * 3
        + [pltpu.VMEM((PEERS * (slots // 2), width), low)]
        + pair_shapes
        + block_shapes
        + [dma((PEERS,)), dma((PEERS,)), dma((PEERS,)), dma((PEERS,)), dma((2,)), dma((2, 4)), dma((4,)), dma((14, 2, 11)), dma((10 + 2 * chunks,))],
        compiler_params=pltpu.CompilerParams(
            collective_id=1, has_side_effects=True, vmem_limit_bytes=60 << 20
        ),
        name="inbound",
    )(rows, grads, slot_line, home_line, box_x, box_y, tables, *shards, vectors)


LAST = 7


def scatter_plan(n, late):
    if late:
        return tuple(range(LAST, LAST + 7))
    return (n // 2, 3 + n, 5 + n, 7 + n, 8 + n, 9 + n, 10 + n)


def outbound_kernel(
    h_result, h_one, h_qkv, h_context, h_homed, h_vec, home_line, slot_line, r_tables, codes, flipped,
    h_whole, g_out, g_up, g_down,
    result_out, arrived_b, table_out, o_qkv, o_out, o_up, o_down,
    packed, arrived_a, loose, table_got, grad_qkv, g_qkv,
    t_qkv, t_out, t_up, t_down, c_qkv, c_out, c_up, c_down, n_qkv, n_out, n_up, n_down,
    f_qkv, f_out, f_up, f_down, z_qkv, z_out, z_up, z_down, e_qkv, e_out, e_up, e_down,
    result_ref, grad_one, qkv, grad_context, homed, vec_grads, w_qkv, tables,
    send_a, recv_a, send_b, recv_b, local_sems, table_sems, piece_sems, fetch_sems, last_sems, load_sems,
):
    where = place()
    me, core, z, y, x = where
    sources = (h_result, h_qkv, h_context, h_homed, h_whole, h_one, h_vec)
    targets = (result_ref, qkv, grad_context, homed, w_qkv, grad_one, vec_grads)
    loads = [
        pltpu.make_async_copy(src, dst, load_sems.at[n])
        for n, (src, dst) in enumerate(zip(sources, targets))
    ]
    for load in loads:
        load.start()
    tables[...] = jnp.zeros_like(tables)
    tables[: r_tables.shape[0], : r_tables.shape[1]] = r_tables[...]
    enter(me, core)
    local = (g_qkv, g_out, g_up, g_down)
    sums = (t_qkv, t_out, t_up, t_down)
    from_core = (c_qkv, c_out, c_up, c_down)
    from_near = (n_qkv, n_out, n_up, n_down)
    from_far = (f_qkv, f_out, f_up, f_down)
    from_z = (z_qkv, z_out, z_up, z_down)
    ends = (e_qkv, e_out, e_up, e_down)
    outs = (o_qkv, o_out, o_up, o_down)
    low = jnp.bfloat16
    tasks = []
    for i in (3, 2, 1, 0):
        refs = (local[i], sums[i], from_core[i], from_near[i], from_far[i], from_z[i])
        for pair in pieces_of(sums[i].shape[3], sums[i].shape[4]):
            n = len(tasks)
            pair = [
                Scatter(where, *refs, fetch_sems.at[2 * n + j], piece, piece_sems.at[2 * n + j])
                for j, piece in enumerate(pair)
            ]
            tasks.append((pair, scatter_plan(n, i == 0)))
    step, steps = stepper(tasks)
    moved = Exchange(where, packed, arrived_a, loose, send_a, recv_a, local_sems.at[0])
    moved_grad = Exchange(where, packed, arrived_b, loose, send_b, recv_b, local_sems.at[1])
    devices = [(me, 1 - core), (me ^ 1, core), (me ^ 2, core), (me ^ 4, core), (me ^ 8, core)]
    shares = [
        remote(table_got.at[0, n], table_got.at[1, n], table_sems.at[0, n], table_sems.at[1, n], device)
        for n, device in enumerate(devices)
    ]

    table_out[...] = jnp.zeros_like(table_out)
    step(0)
    loads[0].wait()
    moved.pack(result_ref, home_line)
    for load in loads[1:]:
        load.wait()

    def one(pair, carry):
        attend_pair_back(pair, qkv, grad_context, tables, codes, flipped, grad_qkv, table_out)
        for j in range(PAIRS):

            @pl.when(pair == j)
            def _(j=j):
                step(1 + j)

        return carry

    lax.fori_loop(0, PAIRS, one, 0)
    width = homed.shape[1]
    sums_of = []
    in_home = grad_one[...]
    for n in range(3):
        part = grad_qkv[:, n * width : (n + 1) * width]
        g_qkv[:, :, :, :, n * width : (n + 1) * width] = (
            lax.dot_general(homed[...], part, TN, preferred_element_type=jnp.float32)
            .astype(low)
            .reshape(*g_qkv.shape[:4], width)
        )
        sums_of.append(jnp.sum(part.astype(jnp.float32), axis=0, keepdims=True))
        weights = w_qkv[:, :, :, :, n * width : (n + 1) * width].reshape(width, width)
        in_home = in_home + lax.dot_general(part, weights, NT, preferred_element_type=jnp.float32)
    row = lax.broadcasted_iota(jnp.int32, (128, width), 0)
    lines = jnp.where(row == 0, sums_of[0], jnp.where(row == 1, sums_of[2], vec_grads[...]))
    beside = lines.T.astype(low).reshape(*g_qkv.shape[:4], 128)
    g_qkv[:, :, :, :, 3 * width : 3 * width + 128] = beside
    g_qkv[:, :, :, :, 3 * width + 128 :] = jnp.zeros_like(beside)
    step(LAST)
    moved.wait()
    moved_grad.pack(in_home.astype(low), home_line)
    moved.unpack(slot_line, result_out, low)
    for k in range(LAST + 1, steps):
        step(k)
        n = k - LAST - 1
        if 0 < n <= 5:
            shares[n - 1].wait_recv()
            table_out[...] += table_got[1, n - 1]
        if n < 5:
            table_got[0, n] = table_out[...]
            shares[n].start()
    finals = []
    for i in (3, 2, 1, 0):
        block = sums[i][z, y, x].astype(jnp.float32)
        rows = block.shape[0] // 2
        ends[i][0] = block[:rows]
        ends[i][1] = block[rows:]
        outs[i][core] = ends[i][core]
        copy = remote(ends[i].at[1 - core], outs[i].at[core], last_sems.at[0, i], last_sems.at[1, i], (me, 1 - core))
        copy.start()
        finals.append(copy)
    moved_grad.wait()
    for copy in finals:
        copy.wait()
    for share in shares:
        share.wait_send()
    for pair, _ in tasks:
        for task in pair:
            task.sent()


def outbound(result, grad_one, qkv, grad_context, homed, vec_grads, home_line, slot_line, tables, codes, flipped, w_qkv, locals_):
    tokens, width = result.shape
    slots = 2 * (2 * tokens // PEERS)
    low = jnp.bfloat16
    buffer = pltpu.VMEM((PEERS, slots, width // 2), low)
    halves = [(g.shape[3], g.shape[4] // 2) for g in (w_qkv, *locals_)]
    scratch = (
        [buffer] * 2
        + [pltpu.VMEM((PEERS * (slots // 2), width), low)]
        + [pltpu.VMEM((2, 5, 16, 256), jnp.float32)]
        + [pltpu.VMEM(qkv.shape, low), pltpu.VMEM(w_qkv.shape, low)]
        + [pltpu.VMEM((4, 2, 2, r, h), low) for r, h in halves]
        + [pltpu.VMEM((4, 2, 2, r, h), low) for r, h in halves]
        + [pltpu.VMEM((4, 2, r, h), low) for r, h in halves]
        + [pltpu.VMEM((4, r, h), low) for r, h in halves]
        + [pltpu.VMEM((2, 4, r, h), low) for r, h in halves]
        + [pltpu.VMEM((2, r // 2, h), jnp.float32) for r, h in halves]
        + [pltpu.VMEM(a.shape, a.dtype) for a in (result, grad_one, qkv, grad_context, homed, vec_grads, w_qkv)]
        + [pltpu.VMEM((16, 256), jnp.float32)]
    )
    dma = pltpu.SemaphoreType.DMA
    return pl.pallas_call(
        outbound_kernel,
        out_shape=[
            jax.ShapeDtypeStruct(result.shape, low),
            jax.ShapeDtypeStruct((PEERS, slots, width // 2), low),
            jax.ShapeDtypeStruct((16, 256), jnp.float32),
        ]
        + [jax.ShapeDtypeStruct((2, r // 2, h), jnp.float32) for r, h in halves],
        in_specs=[pl.BlockSpec(memory_space=pl.ANY)] * 6
        + vmem(5)
        + [pl.BlockSpec(memory_space=pl.ANY)] * 4,
        out_specs=vmem(7),
        scratch_shapes=scratch
        + [dma((PEERS,)), dma((PEERS,)), dma((PEERS,)), dma((PEERS,)), dma((2,)), dma((2, 5)), dma((14, 2, 5)), dma((14,)), dma((2, 4)), dma((7,))],
        compiler_params=pltpu.CompilerParams(
            collective_id=2, has_side_effects=True, vmem_limit_bytes=60 << 20
        ),
        name="outbound",
    )(result, grad_one, qkv, grad_context, homed, vec_grads, home_line, slot_line, tables, codes, flipped, w_qkv, *locals_)


def finish_kernel(
    arrived, slot_line, moved_rows, table_sum, e_qkv, e_out, e_up, e_down, p_qkv, p_out, p_up, p_down, p_vec, p_rel,
    m_qkv, m_out, m_up, m_down, m_vec, m_rel, v_qkv, v_out, v_up, v_down, v_vec, v_rel,
    layer_out, in_grad, a_qkv, a_out, a_up, a_down, a_vec, a_rel, f_qkv, f_out, f_up, f_down, f_vec, f_rel,
    s_qkv, s_out, s_up, s_down, s_vec, s_rel, u_qkv, u_out, u_up, u_down, u_vec, u_rel, loose,
):
    layer_out[...] = moved_rows[...]
    in_grad[...] = unpacked(arrived, loose, slot_line)
    ends = (e_qkv, e_out, e_up, e_down)
    params = (p_qkv, p_out, p_up, p_down, p_vec, p_rel)
    moments = (m_qkv, m_out, m_up, m_down, m_vec, m_rel)
    squares = (v_qkv, v_out, v_up, v_down, v_vec, v_rel)
    grads = (a_qkv, a_out, a_up, a_down, a_vec, a_rel)
    firsts = (f_qkv, f_out, f_up, f_down, f_vec, f_rel)
    seconds = (s_qkv, s_out, s_up, s_down, s_vec, s_rel)
    updates = (u_qkv, u_out, u_up, u_down, u_vec, u_rel)

    def adam(i, grad, columns):
        rate = DECAY_RATE if i < 4 else 0.0
        param = params[i][:, columns].astype(jnp.float32)
        new = adam_step(param, grad, moments[i][:, columns], squares[i][:, columns], rate)
        for ref, value in zip((grads[i], firsts[i], seconds[i], updates[i]), (grad, *new)):
            ref[:, columns] = value

    for i in range(4):
        half = ends[i].shape[2]
        width = params[i].shape[1]
        adam(i, ends[i][0], slice(0, half))
        adam(i, ends[i][1][:, : width - half], slice(half, width))
    kinds, features = params[4].shape
    rest = params[0].shape[1] - ends[0].shape[2]
    turned = ends[0][1][:, rest : rest + 128].T
    adam(4, turned[:kinds], slice(0, features))
    heads, entries = params[5].shape
    adam(5, table_sum[:heads, :entries], slice(0, entries))


def finish(arrived, slot_line, moved_rows, table_sum, ends, params, moments, squares):
    f32 = jnp.float32
    tokens, width = moved_rows.shape
    like = [jax.ShapeDtypeStruct(param.shape, f32) for param in params]
    return pl.pallas_call(
        finish_kernel,
        out_shape=[
            jax.ShapeDtypeStruct((tokens, width), jnp.bfloat16),
            jax.ShapeDtypeStruct((tokens, width), f32),
        ]
        + like * 4,
        in_specs=vmem(4 + 4 + 18),
        out_specs=vmem(2 + 24),
        scratch_shapes=[pltpu.VMEM((PEERS * (arrived.shape[1] // 2), width), jnp.bfloat16)],
        compiler_params=pltpu.CompilerParams(vmem_limit_bytes=60 << 20),
        name="finish",
    )(arrived, slot_line, moved_rows, table_sum, *ends, *params, *moments, *squares)


def per_device(
    layer_in,
    out_grad,
    w_qkv,
    w_out,
    w_up,
    w_down,
    vectors,
    relative,
    first_qkv,
    second_qkv,
    first_out,
    second_out,
    first_up,
    second_up,
    first_down,
    second_down,
    first_vectors,
    second_vectors,
    first_relative,
    second_relative,
    token_slot,
    home_index,
    box_x,
    box_y,
):
    homed, qkv, whole_qkv, codes, flipped, result, grad_one, grad_context, *local_grads, vec_grads = inbound(
        layer_in[0],
        out_grad[0],
        token_slot,
        home_index,
        box_x,
        box_y,
        relative,
        [w_qkv, w_out, w_up, w_down],
        vectors,
    )
    moved_rows, arrived, table_sum, *ends = outbound(
        result,
        grad_one,
        qkv,
        grad_context,
        homed,
        vec_grads,
        home_index,
        token_slot,
        relative,
        codes,
        flipped,
        whole_qkv,
        local_grads,
    )
    layer_out, in_grad, *new = finish(
        arrived,
        token_slot,
        moved_rows,
        table_sum,
        ends,
        [w_qkv, w_out, w_up, w_down, vectors, relative],
        [first_qkv, first_out, first_up, first_down, first_vectors, first_relative],
        [second_qkv, second_out, second_up, second_down, second_vectors, second_relative],
    )
    by_weight = [new[6 * kind + i] for i in range(6) for kind in range(4)]
    return (layer_out[None], in_grad[None], *by_weight)


def spread_device(
    layer_in,
    out_grad,
    w_qkv,
    w_out,
    w_up,
    w_down,
    vectors,
    relative,
    first_qkv,
    second_qkv,
    first_out,
    second_out,
    first_up,
    second_up,
    first_down,
    second_down,
    first_vectors,
    second_vectors,
    first_relative,
    second_relative,
    token_slot,
    home_index,
    box_x,
    box_y,
):
    tokens = layer_in[0]
    rows_dev = tokens.shape[0]
    model_dim = tokens.shape[1]
    groups = lax.axis_size(REGIONS)
    slot_cap = 2 * rows_dev // groups
    page_num = rows_dev // PAGE
    slot_of = token_slot[0]
    home_rows = home_index[0]
    full_qkv, full_out, full_up, full_down, full_vec = (
        lax.all_gather(w_qkv, BOTH, axis=0, tiled=True),
        lax.all_gather(w_out, BOTH, axis=0, tiled=True),
        lax.all_gather(w_up, BOTH, axis=0, tiled=True),
        lax.all_gather(w_down, BOTH, axis=0, tiled=True),
        lax.all_gather(vectors, BOTH, axis=1, tiled=True),
    )
    vec_rows = full_vec.astype(jnp.float32)
    qkv_bias = jnp.concatenate([vec_rows[0], jnp.zeros_like(vec_rows[0]), vec_rows[1]])
    code_rows = position_codes(box_x[0].reshape(page_num, PAGE), box_y[0].reshape(page_num, PAGE))
    bias_mats = bias_table(relative)
    homed = exchange(tokens, slot_of, home_rows, groups, slot_cap).astype(jnp.bfloat16)
    cotangent = exchange(out_grad[0], slot_of, home_rows, groups, slot_cap)
    projected = (jnp.dot(homed, full_qkv, preferred_element_type=jnp.float32) + qkv_bias).astype(
        jnp.bfloat16
    )
    paged = projected.reshape(page_num, PAGE, 3 * model_dim)
    context_pages, log_totals = lax.map(
        lambda member: page_forward(member[0], member[1], bias_mats), (paged, code_rows)
    )
    context = context_pages.reshape(rows_dev, model_dim)
    attn_out = jnp.dot(context, full_out, preferred_element_type=jnp.float32) + vec_rows[2]
    hidden, normed_one, spread_one = norm_forward(
        homed.astype(jnp.float32) + attn_out, vec_rows[3], vec_rows[4]
    )
    hidden_low = hidden.astype(jnp.bfloat16)
    pre_act = jnp.dot(hidden_low, full_up, preferred_element_type=jnp.float32) + vec_rows[
        8:12
    ].reshape(-1)
    activated, gelu_back = jax.vjp(lambda value: jax.nn.gelu(value, approximate=False), pre_act)
    act_low = activated.astype(jnp.bfloat16)
    branch = jnp.dot(act_low, full_down, preferred_element_type=jnp.float32) + vec_rows[5]
    result, normed_two, spread_two = norm_forward(hidden + branch, vec_rows[6], vec_rows[7])
    grad_two, grad_gain_two, grad_shift_two = norm_back(
        cotangent, normed_two, spread_two, vec_rows[6]
    )
    grad_branch = grad_two.astype(jnp.bfloat16)
    grad_down = jnp.einsum("tf,td->fd", act_low, grad_branch, preferred_element_type=jnp.float32)
    grad_act = jnp.einsum("td,fd->tf", grad_branch, full_down, preferred_element_type=jnp.float32)
    grad_pre = gelu_back(grad_act)[0].astype(jnp.bfloat16)
    grad_up = jnp.einsum("td,tf->df", hidden_low, grad_pre, preferred_element_type=jnp.float32)
    grad_hidden = grad_two + jnp.einsum(
        "tf,df->td", grad_pre, full_up, preferred_element_type=jnp.float32
    )
    grad_one, grad_gain_one, grad_shift_one = norm_back(
        grad_hidden, normed_one, spread_one, vec_rows[3]
    )
    grad_attn = grad_one.astype(jnp.bfloat16)
    grad_out = jnp.einsum("td,te->de", context, grad_attn, preferred_element_type=jnp.float32)
    grad_context = jnp.einsum(
        "te,de->td", grad_attn, full_out, preferred_element_type=jnp.float32
    ).astype(jnp.bfloat16)
    grad_home = grad_context.reshape(page_num, PAGE, model_dim)
    grad_pages, mats_pages = lax.map(
        lambda member: page_backward(member[0], member[1], member[2], member[3], bias_mats),
        (paged, code_rows, log_totals, grad_home),
    )
    grad_dense = grad_pages.reshape(rows_dev, 3 * model_dim)
    bias_sums = jnp.sum(grad_dense.astype(jnp.float32), axis=0)
    grad_qkv = jnp.einsum("td,tf->df", homed, grad_dense, preferred_element_type=jnp.float32)
    in_home = grad_one + jnp.einsum(
        "tf,df->td", grad_dense, full_qkv, preferred_element_type=jnp.float32
    )
    layer_out = exchange(result.astype(jnp.bfloat16), home_rows, slot_of, groups, slot_cap)
    in_grad = exchange(in_home.astype(jnp.bfloat16), home_rows, slot_of, groups, slot_cap)
    grad_vec = jnp.concatenate(
        [
            jnp.stack(
                [
                    bias_sums[:model_dim],
                    bias_sums[2 * model_dim :],
                    jnp.sum(grad_attn.astype(jnp.float32), axis=0),
                    grad_gain_one,
                    grad_shift_one,
                    jnp.sum(grad_branch.astype(jnp.float32), axis=0),
                    grad_gain_two,
                    grad_shift_two,
                ]
            ),
            jnp.sum(grad_pre.astype(jnp.float32), axis=0).reshape(4, model_dim),
        ],
        axis=0,
    )
    grad_qkv, grad_out, grad_up, grad_down, grad_vectors = (
        lax.psum_scatter(grad_qkv, BOTH, scatter_dimension=0, tiled=True),
        lax.psum_scatter(grad_out, BOTH, scatter_dimension=0, tiled=True),
        lax.psum_scatter(grad_up, BOTH, scatter_dimension=0, tiled=True),
        lax.psum_scatter(grad_down, BOTH, scatter_dimension=0, tiled=True),
        lax.psum_scatter(grad_vec, BOTH, scatter_dimension=1, tiled=True),
    )
    mats_total = jnp.sum(mats_pages, axis=0)
    table_back = jax.vjp(bias_table, relative)[1]
    grad_relative = lax.psum(table_back(mats_total)[0], BOTH)
    firsts_qkv, seconds_qkv, update_qkv = adam_step(
        w_qkv.astype(jnp.float32), grad_qkv, first_qkv, second_qkv, DECAY_RATE
    )
    firsts_out, seconds_out, update_out = adam_step(
        w_out.astype(jnp.float32), grad_out, first_out, second_out, DECAY_RATE
    )
    firsts_up, seconds_up, update_up = adam_step(
        w_up.astype(jnp.float32), grad_up, first_up, second_up, DECAY_RATE
    )
    firsts_down, seconds_down, update_down = adam_step(
        w_down.astype(jnp.float32), grad_down, first_down, second_down, DECAY_RATE
    )
    firsts_vectors, seconds_vectors, update_vectors = adam_step(
        vectors.astype(jnp.float32), grad_vectors, first_vectors, second_vectors, 0.0
    )
    firsts_relative, seconds_relative, update_relative = adam_step(
        relative, grad_relative, first_relative, second_relative, 0.0
    )
    return (
        layer_out.astype(jnp.bfloat16)[None],
        in_grad[None],
        grad_qkv,
        firsts_qkv,
        seconds_qkv,
        update_qkv,
        grad_out,
        firsts_out,
        seconds_out,
        update_out,
        grad_up,
        firsts_up,
        seconds_up,
        update_up,
        grad_down,
        firsts_down,
        seconds_down,
        update_down,
        grad_vectors,
        firsts_vectors,
        seconds_vectors,
        update_vectors,
        grad_relative,
        firsts_relative,
        seconds_relative,
        update_relative,
    )


def solution(mesh):
    kernels = mesh.shape[REGIONS] == PEERS and mesh.shape[SHARD] == 2
    return jax.shard_map(
        per_device if kernels else spread_device,
        mesh=mesh,
        in_specs=(
            P(SHARD, REGIONS, None),
            P(SHARD, REGIONS, None),
            P(BOTH, None),
            P(BOTH, None),
            P(BOTH, None),
            P(BOTH, None),
            P(None, BOTH),
            P(),
            P(BOTH, None),
            P(BOTH, None),
            P(BOTH, None),
            P(BOTH, None),
            P(BOTH, None),
            P(BOTH, None),
            P(BOTH, None),
            P(BOTH, None),
            P(None, BOTH),
            P(None, BOTH),
            P(),
            P(),
            P(SHARD, REGIONS),
            P(SHARD, REGIONS),
            P(SHARD, REGIONS),
            P(SHARD, REGIONS),
        ),
        out_specs=(
            P(SHARD, REGIONS, None),
            P(SHARD, REGIONS, None),
            P(BOTH, None),
            P(BOTH, None),
            P(BOTH, None),
            P(BOTH, None),
            P(BOTH, None),
            P(BOTH, None),
            P(BOTH, None),
            P(BOTH, None),
            P(BOTH, None),
            P(BOTH, None),
            P(BOTH, None),
            P(BOTH, None),
            P(BOTH, None),
            P(BOTH, None),
            P(BOTH, None),
            P(BOTH, None),
            P(None, BOTH),
            P(None, BOTH),
            P(None, BOTH),
            P(None, BOTH),
            P(),
            P(),
            P(),
            P(),
        ),
        check_vma=False,
    )
```
